32 devices in a mesh: tm: 8 (over z, y), head: 4 (over x, core).
Axes of the slice: x: 2, y: 2, z: 4, core: 2. Of those that a mesh axis runs over, the one named last changes fastest.
Arguments:
- query: bfloat16 [1024, 2560], P('tm', 'head'), may hold values from -8 to 8
- key: bfloat16 [1024, 2560], P('tm', 'head'), may hold values from -8 to 8
- value: bfloat16 [1024, 2560], P('tm', 'head'), may hold values from -6 to 6
- grad_out: bfloat16 [1024, 2560], P('tm', 'head'), may hold values from -6 to 6
- frame_ids: int32 [8], replicated, may hold values from 0 to 2, as said below
- sink_frame: int32 [1], replicated, may hold values from 0 to 2
- window: int32 [20], P('head'), may hold values from 1 to 3, as said below
Outputs:
- attended: bfloat16 [1024, 2560], P('tm', 'head')
- query_grad: bfloat16 [1024, 2560], P('tm', 'head')
- key_grad: bfloat16 [1024, 2560], P('tm', 'head')
- value_grad: bfloat16 [1024, 2560], P('tm', 'head')
The draws below stay inside these ranges and needn't reach their ends.
Inputs may be any that keep to these rules, and one draw needn't show every extreme that they name: frame_ids[b] = (b + c) // 4 for one c of 1 to 3: every frame is four blocks except the first and the last, which have 4 - c and c blocks. Some head has a window of 3 and some a window of 1.
All inputs are finite; a program needn't handle non-finite values.
Results may differ from the reference program's by a relative error of at most 0.033.
Values may be sent and summed in bfloat16 or wider, within the bound.
No kernel may reach another device: no remote copies, remote signals or barrier semaphores. Data moves between devices by JAX's collectives and lax.ppermute only.
A program may use at most 128 MiB of HBM per device.

```python
import math
import jax
import jax.numpy as jnp
from jax import lax

HEADS = 20
DH = 128
NBLK = 8
TOKENS = 1024


def base_field(key, salt):
    inner = jax.random.fold_in(key, salt)
    return jnp.clip(jax.random.normal(inner, (TOKENS, HEADS * DH), jnp.float32), -6.0, 6.0)


def draw_query(key, part):
    field = base_field(key, 11)
    return field.astype(jnp.bfloat16)


def draw_key(key, part):
    field = base_field(key, 12)
    return field.astype(jnp.bfloat16)


def draw_frame_ids(key, part):
    start = jax.random.randint(jax.random.fold_in(key, 21), (), 1, 4)
    return ((jnp.arange(NBLK, dtype=jnp.int32) + start) // 4).astype(jnp.int32)


def draw_window(key, part):
    spans = jax.random.randint(jax.random.fold_in(key, 31), (HEADS,), 1, 4)
    order = jax.random.permutation(jax.random.fold_in(key, 32), HEADS)
    spans = spans.at[order[0]].set(3)
    spans = spans.at[order[1]].set(1)
    return spans.astype(jnp.int32)


def steps_of(own_key, extent, pieces, smallest, top_value):
    level, own = 1.0, jax.random.fold_in(own_key, 6)
    for axis_at, shards_of in pieces:
        heights = jnp.exp(jax.random.uniform(jax.random.fold_in(own, axis_at), (shards_of,), jnp.float32, smallest / len(pieces), top_value / len(pieces)))
        level = level * jnp.repeat(heights, extent[axis_at] // shards_of).reshape([-1 if axis == axis_at else 1 for axis in range(len(extent))])
    return level


def gaussian(own_key, dims, scale, most, cuts=(), held_as=jnp.bfloat16):
    result = scale * jax.random.normal(own_key, dims, jnp.float32)
    if cuts:
        result = result * steps_of(own_key, dims, cuts, -0.22, 0.18)
    return jnp.clip(result, -most, most).astype(held_as)


def setup_inputs(seed: int = 0) -> dict:
    keys = jax.random.split(jax.random.key(seed), 8)
    return {
        "query": draw_query(jax.random.fold_in(keys[7], 71), 0),
        "key": draw_key(jax.random.fold_in(keys[7], 71), 0),
        "value": gaussian(keys[2], (TOKENS, HEADS * DH), 1.0, 6.0, ((0, 8), (1, 4))),
        "grad_out": gaussian(keys[3], (TOKENS, HEADS * DH), 1.0, 6.0, ((0, 8), (1, 4))),
        "frame_ids": draw_frame_ids(jax.random.fold_in(keys[7], 71), 0),
        "sink_frame": jax.random.randint(keys[5], (1,), 0, NBLK // 4 + 1).astype(jnp.int32),
        "window": draw_window(jax.random.fold_in(keys[7], 71), 0),
    }


masked_score = -1e+30

def to_bf16_values(array):
    return lax.optimization_barrier(array.astype(jnp.bfloat16)).astype(jnp.float32)

def reference(query, key, value, grad_out, frame_ids, sink_frame, window):
    tokens, row_width = query.shape
    head_count = window.shape[0]
    head_dim = row_width // head_count
    blocks = frame_ids.shape[0]
    block_rows = tokens // blocks
    scaling = 1.0 / math.sqrt(head_dim)
    sink_index = sink_frame[0]
    query_heads = query.astype(jnp.float32).reshape(tokens, head_count, head_dim)
    key_heads = key.astype(jnp.float32).reshape(tokens, head_count, head_dim)
    value_heads = value.astype(jnp.float32).reshape(tokens, head_count, head_dim)
    grad_heads = grad_out.astype(jnp.float32).reshape(tokens, head_count, head_dim)
    key_frames = jnp.repeat(frame_ids, block_rows)

    def one_block(carry, block_id):
        key_acc, value_acc = carry
        query_frame = frame_ids[block_id]
        in_window = (key_frames[None, :] <= query_frame) & (key_frames[None, :] > query_frame - window[:, None])
        at_sink = (key_frames[None, :] == sink_index) & (sink_index <= query_frame)
        visible = (in_window | at_sink)[:, None, :]
        start = block_id * block_rows
        q_rows = lax.dynamic_slice_in_dim(query_heads, start, block_rows, 0)
        g_rows = lax.dynamic_slice_in_dim(grad_heads, start, block_rows, 0)
        scores = jnp.einsum('qhd,khd->hqk', q_rows, key_heads) * scaling
        scores = jnp.where(visible, scores, masked_score)
        top = lax.optimization_barrier(jnp.max(scores, axis=-1, keepdims=True))
        weights = jnp.where(visible, jnp.exp(scores - top), 0.0)
        totals = lax.optimization_barrier(jnp.sum(weights, axis=-1, keepdims=True))
        mixed = jnp.einsum('hqk,khd->hqd', to_bf16_values(weights), value_heads) / totals
        attended = mixed.transpose(1, 0, 2).astype(jnp.bfloat16)
        log_total = top + jnp.log(totals)
        probs_back = jnp.where(visible, jnp.exp(scores - log_total), 0.0)
        dot_back = jnp.einsum('qhd,khd->hqk', g_rows, value_heads)
        row_dots = lax.optimization_barrier(jnp.sum(g_rows * attended.astype(jnp.float32), axis=-1)).T[:, :, None]
        score_grad = to_bf16_values(probs_back * (dot_back - row_dots))
        query_grad = (jnp.einsum('hqk,khd->qhd', score_grad, key_heads) * scaling).astype(jnp.bfloat16)
        key_acc = key_acc + jnp.einsum('hqk,qhd->khd', score_grad, q_rows) * scaling
        value_acc = value_acc + jnp.einsum('hqk,qhd->khd', to_bf16_values(probs_back), g_rows)
        return ((key_acc, value_acc), (attended, query_grad))
    start_acc = jnp.zeros((tokens, head_count, head_dim), jnp.float32)
    (key_acc, value_acc), (attended, query_grad) = lax.scan(one_block, (start_acc, start_acc), jnp.arange(blocks, dtype=jnp.int32))
    attended = attended.reshape(tokens, row_width)
    query_grad = query_grad.reshape(tokens, row_width)
    key_grad = key_acc.reshape(tokens, row_width).astype(jnp.bfloat16)
    value_grad = value_acc.reshape(tokens, row_width).astype(jnp.bfloat16)
    return (attended, query_grad, key_grad, value_grad)
```

```python
import functools
import math

import jax
import jax.numpy as jnp
import numpy as np
from jax import lax
from jax.experimental import pallas as pl
from jax.experimental.pallas import tpu as pltpu
from jax.sharding import PartitionSpec as P

hidden_score = -1e30
MIB = 1 << 20


def owner_of(group, head, blocks, heads):
    return (head * blocks // heads + group % 2) % blocks


def plan(blocks, groups, heads):
    owned = np.full((blocks, groups), -1, np.int32)
    for group in range(groups):
        for head in range(heads):
            owned[owner_of(group, head, blocks, heads), group] = head
    sent = np.full((blocks, groups, blocks), -1, np.int32)
    pairs = []
    for step in range(blocks):
        sent[:, :, step] = np.roll(owned, -step, axis=0)
        pairs.append(
            [
                (block * groups + group, (block + step) % blocks * groups + group)
                for block in range(blocks)
                for group in range(groups)
                if owned[(block + step) % blocks, group] >= 0
            ]
        )
    return owned, sent, pairs


def dot(a, b, contract):
    return lax.dot_general(a, b, (contract, ((), ())), preferred_element_type=jnp.float32)


NN = ((1,), (0,))
NT = ((1,), (1,))


def device_index():
    return lax.axis_index("tm") * lax.axis_size("head") + lax.axis_index("head")


def head_columns(head, width):
    return pl.ds(pl.multiple_of(head * width, width), width)


def pack_kernel(blocks, width, sent, query, key, value, grad_out, *outs):
    me = device_index()
    for step in range(blocks):
        head = sent[me * blocks + step]

        @pl.when(head >= 0)
        def _():
            columns = head_columns(head, width)
            outs[step][0] = query[:, columns]
            outs[step][1] = key[:, columns]
            outs[step][2] = value[:, columns]
            outs[step][3] = grad_out[:, columns].T


def unpack_kernel(blocks, width, sent, *refs):
    me = device_index()
    parts, (attended, query_grad, key_grad, value_grad) = refs[:blocks], refs[blocks:]
    for step in range(blocks):
        head = sent[me * blocks + step]

        @pl.when(head >= 0)
        def _():
            columns = head_columns(head, width)
            attended[:, columns] = parts[step][0].T
            query_grad[:, columns] = parts[step][1].T
            key_grad[:, columns] = parts[step][2]
            value_grad[:, columns] = parts[step][3]


def head_kernel(blocks, rows, owned, frame_ids, sink_frame, window, *refs):
    parts, outs = refs[:blocks], refs[blocks : 2 * blocks]
    (q_all, k_all, v_all, kt_all, vt_all, gt_all, weights, weights_low, grads_low, dk, dv, res) = refs[
        2 * blocks :
    ]
    me = device_index()
    my_block = lax.axis_index("tm")
    head = owned[me]
    width = q_all.shape[1]
    scaling = 1.0 / math.sqrt(width)
    rescale = scaling * math.log2(math.e)
    pair = 2 if blocks % 2 == 0 else 1
    chunk = pair * rows

    @pl.when(head >= 0)
    def _():
        span = window[head]
        sink = sink_frame[0]
        for step in range(blocks):
            block = lax.rem(my_block + (blocks - step), blocks)
            at = pl.ds(pl.multiple_of(block * rows, rows), rows)
            q_all[at, :] = parts[step][0]
            k_all[at, :] = parts[step][1]
            v_all[at, :] = parts[step][2]
            kt_all[:, at] = parts[step][1].T
            vt_all[:, at] = parts[step][2].T
            gt_all[:, at] = parts[step][3]
        dk[...] = jnp.zeros_like(dk)
        dv[...] = jnp.zeros_like(dv)
        lane_block = lax.broadcasted_iota(jnp.int32, (1, chunk), 1) // rows

        def one_chunk(i, carry):
            at = pl.ds(pl.multiple_of(i * chunk, chunk), chunk)
            q_rows = q_all[at, :]
            top = jnp.full((1, chunk), hidden_score, jnp.float32)
            for j in range(blocks):
                frame = frame_ids[j]
                bias = jnp.zeros((1, chunk), jnp.float32)
                for k in range(pair):
                    own = frame_ids[i * pair + k]
                    seen = ((frame <= own) & (frame > own - span)) | ((frame == sink) & (sink <= own))
                    bias = jnp.where(lane_block == k, jnp.where(seen, 0.0, hidden_score), bias)
                keys = pl.ds(j * rows, rows)
                scores = dot(k_all[keys, :], q_rows, NT) * rescale + bias
                weights[keys, :] = scores
                top = jnp.maximum(top, jnp.max(scores, axis=0, keepdims=True))
            total = jnp.zeros((1, chunk), jnp.float32)
            for j in range(blocks):
                keys = pl.ds(j * rows, rows)
                p = jnp.exp2(weights[keys, :] - top)
                total = total + jnp.sum(p, axis=0, keepdims=True)
                weights[keys, :] = p
                weights_low[keys, :] = p.astype(jnp.bfloat16)
            inverse = 1.0 / total
            mixed = (dot(vt_all[...], weights_low[...], NN) * inverse).astype(jnp.bfloat16)
            grad_t = gt_all[:, at].astype(jnp.float32)
            delta = jnp.sum(grad_t * mixed.astype(jnp.float32), axis=0, keepdims=True) * inverse
            grad_low = (grad_t * inverse).astype(jnp.bfloat16)
            for j in range(blocks):
                keys = pl.ds(j * rows, rows)
                g = weights[keys, :] * (dot(v_all[keys, :], grad_low, NN) - delta)
                g = g.astype(jnp.bfloat16)
                grads_low[keys, :] = g
                dk[keys, :] += dot(g, q_rows, NN)
                dv[keys, :] += dot(weights_low[keys, :], grad_low, NT)
            query_grad = (dot(kt_all[...], grads_low[...], NN) * scaling).astype(jnp.bfloat16)
            for k in range(pair):
                res[i * pair + k, 0] = mixed[:, k * rows : (k + 1) * rows]
                res[i * pair + k, 1] = query_grad[:, k * rows : (k + 1) * rows]
            return carry

        if blocks // pair <= 4:
            for i in range(blocks // pair):
                one_chunk(i, 0)
        else:
            lax.fori_loop(0, blocks // pair, one_chunk, 0)
        for step in range(blocks):
            block = lax.rem(my_block + (blocks - step), blocks)
            at = pl.ds(pl.multiple_of(block * rows, rows), rows)
            outs[step][0] = res[block, 0]
            outs[step][1] = res[block, 1]
            outs[step][2] = (dk[at, :] * scaling).astype(jnp.bfloat16)
            outs[step][3] = dv[at, :].astype(jnp.bfloat16)


def per_device(query, key, value, grad_out, frame_ids, sink_frame, window):
    rows, row_width = query.shape
    heads = window.shape[0]
    width = row_width // heads
    blocks = lax.axis_size("tm")
    owned, sent, pairs = plan(blocks, lax.axis_size("head"), heads)
    axes = ("tm", "head")
    smem = pl.BlockSpec(memory_space=pltpu.SMEM)
    vmem = pl.BlockSpec(memory_space=pltpu.VMEM)
    part = jax.ShapeDtypeStruct((4, rows, width), query.dtype)
    local = jax.ShapeDtypeStruct(query.shape, query.dtype)
    sent = jnp.asarray(sent.reshape(-1))
    owned = jnp.asarray(owned.reshape(-1))

    parts = pl.pallas_call(
        functools.partial(pack_kernel, blocks, width),
        out_shape=[part] * blocks,
        in_specs=[smem] + [vmem] * 4,
        out_specs=[vmem] * blocks,
        compiler_params=pltpu.CompilerParams(vmem_limit_bytes=24 * MIB),
        name="pack",
    )(sent, query, key, value, grad_out)
    parts = [parts[0]] + [lax.ppermute(parts[s], axes, pairs[s]) for s in range(1, blocks)]

    tokens = blocks * rows
    chunk = (2 if blocks % 2 == 0 else 1) * rows
    low, full = query.dtype, jnp.float32
    parts = pl.pallas_call(
        functools.partial(head_kernel, blocks, rows),
        out_shape=[part] * blocks,
        in_specs=[smem] * 4 + [vmem] * blocks,
        out_specs=[vmem] * blocks,
        scratch_shapes=[pltpu.VMEM((tokens, width), low)] * 3
        + [pltpu.VMEM((width, tokens), low)] * 3
        + [
            pltpu.VMEM((tokens, chunk), full),
            pltpu.VMEM((tokens, chunk), low),
            pltpu.VMEM((tokens, chunk), low),
            pltpu.VMEM((tokens, width), full),
            pltpu.VMEM((tokens, width), full),
            pltpu.VMEM((blocks, 2, width, rows), low),
        ],
        compiler_params=pltpu.CompilerParams(vmem_limit_bytes=40 * MIB),
        name="head_attention",
    )(owned, frame_ids, sink_frame, window, *parts)
    back = [[(b, a) for a, b in step] for step in pairs]
    parts = [parts[0]] + [lax.ppermute(parts[s], axes, back[s]) for s in range(1, blocks)]

    return pl.pallas_call(
        functools.partial(unpack_kernel, blocks, width),
        out_shape=[local] * 4,
        in_specs=[smem] + [vmem] * blocks,
        out_specs=[vmem] * 4,
        compiler_params=pltpu.CompilerParams(vmem_limit_bytes=24 * MIB),
        name="unpack",
    )(sent, *parts)


def solution(mesh):
    spec = P("tm", "head")
    return jax.shard_map(
        per_device,
        mesh=mesh,
        in_specs=(spec, spec, spec, spec, P(), P(), P("head")),
        out_specs=(spec, spec, spec, spec),
        check_vma=False,
    )
```

```python
import functools
import math

import jax
import jax.numpy as jnp
import numpy as np
from jax import lax
from jax.experimental import pallas as pl
from jax.experimental.pallas import tpu as pltpu
from jax.sharding import PartitionSpec as P

hidden_score = -1e30
MIB = 1 << 20


def owner_of(group, head, blocks, heads):
    return (head * blocks // heads + group % 2) % blocks


def owners(blocks, groups, heads):
    owned = np.full((blocks, groups), -1, np.int32)
    for group in range(groups):
        for head in range(heads):
            owned[owner_of(group, head, blocks, heads), group] = head
    return owned


def dot(a, b, contract):
    return lax.dot_general(a, b, (contract, ((), ())), preferred_element_type=jnp.float32)


NN = ((1,), (0,))
NT = ((1,), (1,))


def chosen(options, index):
    value = jnp.int32(-1)
    for n, option in enumerate(options):
        value = jnp.where(index == n, option, value)
    return value


def head_columns(head, width):
    return pl.ds(pl.multiple_of(head * width, width), width)


def pack_kernel(owned, width, query, key, value, grad_out, out, staged, sems):
    blocks = len(owned)
    group = lax.axis_index("head")
    arrays = (query, key, value, grad_out)
    copies = [pltpu.make_async_copy(a, staged.at[n], sems.at[n]) for n, a in enumerate(arrays)]
    for copy in copies:
        copy.start()
    for n, copy in enumerate(copies):
        copy.wait()
        for block in range(blocks):
            head = chosen(owned[block], group)

            @pl.when(head >= 0)
            def _():
                piece = staged[n, :, head_columns(head, width)]
                out[block, n] = piece.T if n == 3 else piece


def unpack_kernel(owned, width, *refs):
    blocks = len(owned)
    group = lax.axis_index("head")
    parts, attended, query_grad, key_grad, value_grad = refs
    for block in range(blocks):
        head = chosen(owned[block], group)

        @pl.when(head >= 0)
        def _():
            columns = head_columns(head, width)
            attended[:, columns] = parts[block, 0].T
            query_grad[:, columns] = parts[block, 1].T
            key_grad[:, columns] = parts[block, 2]
            value_grad[:, columns] = parts[block, 3]


def head_kernel(owned, rows, frame_ids, sink_frame, window, *refs):
    parts, res, q_all, k_all, v_all, kt_all, vt_all, gt_all, weights, weights_low, grads_low, dk, dv = refs
    blocks = len(owned)
    group = lax.axis_index("head")
    head = chosen([chosen(row, group) for row in owned], lax.axis_index("tm"))
    width = q_all.shape[1]
    scaling = 1.0 / math.sqrt(width)
    rescale = scaling * math.log2(math.e)
    pair = 2 if blocks % 2 == 0 else 1
    chunk = pair * rows

    @pl.when(head >= 0)
    def _():
        span = window[head]
        sink = sink_frame[0]
        for block in range(blocks):
            at = pl.ds(block * rows, rows)
            q_all[at, :] = parts[block, 0]
            k_all[at, :] = parts[block, 1]
            v_all[at, :] = parts[block, 2]
            kt_all[:, at] = parts[block, 1].T
            vt_all[:, at] = parts[block, 2].T
            gt_all[:, at] = parts[block, 3]
        dk[...] = jnp.zeros_like(dk)
        dv[...] = jnp.zeros_like(dv)
        lane_block = lax.broadcasted_iota(jnp.int32, (1, chunk), 1) // rows

        def one_chunk(i, carry):
            at = pl.ds(pl.multiple_of(i * chunk, chunk), chunk)
            q_rows = q_all[at, :]
            top = jnp.full((1, chunk), hidden_score, jnp.float32)
            for j in range(blocks):
                frame = frame_ids[j]
                bias = jnp.zeros((1, chunk), jnp.float32)
                for k in range(pair):
                    own = frame_ids[i * pair + k]
                    seen = ((frame <= own) & (frame > own - span)) | ((frame == sink) & (sink <= own))
                    bias = jnp.where(lane_block == k, jnp.where(seen, 0.0, hidden_score), bias)
                keys = pl.ds(j * rows, rows)
                scores = dot(k_all[keys, :], q_rows, NT) * rescale + bias
                weights[keys, :] = scores
                top = jnp.maximum(top, jnp.max(scores, axis=0, keepdims=True))
            total = jnp.zeros((1, chunk), jnp.float32)
            for j in range(blocks):
                keys = pl.ds(j * rows, rows)
                p = jnp.exp2(weights[keys, :] - top)
                total = total + jnp.sum(p, axis=0, keepdims=True)
                weights[keys, :] = p
                weights_low[keys, :] = p.astype(jnp.bfloat16)
            inverse = 1.0 / total
            mixed = (dot(vt_all[...], weights_low[...], NN) * inverse).astype(jnp.bfloat16)
            grad_t = gt_all[:, at].astype(jnp.float32)
            delta = jnp.sum(grad_t * mixed.astype(jnp.float32), axis=0, keepdims=True) * inverse
            grad_low = (grad_t * inverse).astype(jnp.bfloat16)
            for j in range(blocks):
                keys = pl.ds(j * rows, rows)
                g = weights[keys, :] * (dot(v_all[keys, :], grad_low, NN) - delta)
                g = g.astype(jnp.bfloat16)
                grads_low[keys, :] = g
                dk[keys, :] += dot(g, q_rows, NN)
                dv[keys, :] += dot(weights_low[keys, :], grad_low, NT)
            query_grad = (dot(kt_all[...], grads_low[...], NN) * scaling).astype(jnp.bfloat16)
            for k in range(pair):
                res[i * pair + k, 0] = mixed[:, k * rows : (k + 1) * rows]
                res[i * pair + k, 1] = query_grad[:, k * rows : (k + 1) * rows]
            return carry

        if blocks // pair <= 4:
            for i in range(blocks // pair):
                one_chunk(i, 0)
        else:
            lax.fori_loop(0, blocks // pair, one_chunk, 0)
        for block in range(blocks):
            at = pl.ds(block * rows, rows)
            res[block, 2] = (dk[at, :] * scaling).astype(jnp.bfloat16)
            res[block, 3] = dv[at, :].astype(jnp.bfloat16)


def per_device(query, key, value, grad_out, frame_ids, sink_frame, window):
    rows, row_width = query.shape
    heads = window.shape[0]
    width = row_width // heads
    blocks = lax.axis_size("tm")
    owned = owners(blocks, lax.axis_size("head"), heads).tolist()
    smem = pl.BlockSpec(memory_space=pltpu.SMEM)
    vmem = pl.BlockSpec(memory_space=pltpu.VMEM)
    in_place = pl.BlockSpec(memory_space=pltpu.HBM)
    parts_shape = jax.ShapeDtypeStruct((blocks, 4, rows, width), query.dtype)
    local = jax.ShapeDtypeStruct(query.shape, query.dtype)

    parts = pl.pallas_call(
        functools.partial(pack_kernel, owned, width),
        out_shape=parts_shape,
        in_specs=[in_place] * 4,
        out_specs=vmem,
        scratch_shapes=[pltpu.VMEM((4, rows, row_width), query.dtype), pltpu.SemaphoreType.DMA((4,))],
        compiler_params=pltpu.CompilerParams(vmem_limit_bytes=62 * MIB),
        name="pack",
    )(query, key, value, grad_out)
    parts = lax.all_to_all(parts, "tm", 0, 0, tiled=True)

    tokens = blocks * rows
    chunk = (2 if blocks % 2 == 0 else 1) * rows
    low, full = query.dtype, jnp.float32
    parts = pl.pallas_call(
        functools.partial(head_kernel, owned, rows),
        out_shape=parts_shape,
        in_specs=[smem] * 3 + [vmem],
        out_specs=vmem,
        scratch_shapes=[pltpu.VMEM((tokens, width), low)] * 3
        + [pltpu.VMEM((width, tokens), low)] * 3
        + [
            pltpu.VMEM((tokens, chunk), full),
            pltpu.VMEM((tokens, chunk), low),
            pltpu.VMEM((tokens, chunk), low),
            pltpu.VMEM((tokens, width), full),
            pltpu.VMEM((tokens, width), full),
        ],
        compiler_params=pltpu.CompilerParams(vmem_limit_bytes=40 * MIB),
        name="head_attention",
    )(frame_ids, sink_frame, window, parts)
    parts = lax.all_to_all(parts, "tm", 0, 0, tiled=True)

    return pl.pallas_call(
        functools.partial(unpack_kernel, owned, width),
        out_shape=[local] * 4,
        in_specs=[vmem],
        out_specs=[vmem] * 4,
        compiler_params=pltpu.CompilerParams(vmem_limit_bytes=24 * MIB),
        name="unpack",
    )(parts)


def solution(mesh):
    spec = P("tm", "head")
    return jax.shard_map(
        per_device,
        mesh=mesh,
        in_specs=(spec, spec, spec, spec, P(), P(), P("head")),
        out_specs=(spec, spec, spec, spec),
        check_vma=False,
    )
```

```python
import functools
import math

import jax
import jax.numpy as jnp
import numpy as np
from jax import lax
from jax.experimental import pallas as pl
from jax.experimental.pallas import tpu as pltpu
from jax.sharding import PartitionSpec as P

hidden_score = -1e30
MIB = 1 << 20


even_rounds = (
    {
        0: (3, 6, 5, 7, 1, 2, 4),
        1: (4, 7, 6, 2, 0, 3, 5),
        3: (7, 2, 0, 4, 6, 5, 1),
        5: (6, 0, 7, 1, 2, 4, 3),
        6: (2, 3, 1, 5, 4, 0, 7),
    },
    {
        2: (5, 6, 7, 1, 0, 4, 3),
        3: (0, 5, 4, 6, 7, 1, 2),
        4: (7, 1, 3, 2, 5, 6, 0),
        5: (3, 4, 2, 0, 1, 7, 6),
        7: (1, 2, 0, 4, 6, 3, 5),
    },
)


def plan(blocks, groups, heads):
    laid_out = []
    for group in range(groups):
        if blocks == 8 and heads == 5:
            laid_out.append(even_rounds[group % 2])
        else:
            owners = [(head * blocks // heads + group % 2) % blocks for head in range(heads)]
            laid_out.append({u: [(u - step) % blocks for step in range(1, blocks)] for u in owners})
    owned = np.full((groups, blocks), -1)
    sent = np.full((blocks, groups, blocks), -1)
    partner = np.full((blocks, groups, blocks), -1)
    pairs = [[] for _ in range(blocks)]
    for group, rounds in enumerate(laid_out):
        for head, (owner, sources) in enumerate(rounds.items()):
            owned[group, owner] = head
            for step, source in enumerate((owner, *sources)):
                sent[step, group, source] = head
                partner[step, group, owner] = source
                pairs[step].append((source * groups + group, owner * groups + group))
    return owned, sent, partner, [sorted(step) for step in pairs]


def looked_up(table, group, block):
    groups, blocks = table.shape
    period = next(p for p in range(1, groups + 1) if (table == table[np.arange(groups) % p]).all())
    bits = int(table.max() + 1).bit_length()
    per_word = 31 // bits
    word = jnp.int32(0)
    for row in range(period):
        for first in range(0, blocks, per_word):
            values = table[row, first : first + per_word] + 1
            packed = sum(int(value) << (bits * n) for n, value in enumerate(values))
            here = (lax.rem(group, period) == row) & (block >= first) & (block < first + per_word)
            word = jnp.where(here, packed, word)
    return ((word >> (bits * lax.rem(block, per_word))) & ((1 << bits) - 1)) - 1


def dot(a, b, contract):
    return lax.dot_general(a, b, (contract, ((), ())), preferred_element_type=jnp.float32)


NN = ((1,), (0,))
NT = ((1,), (1,))


def head_columns(head, width):
    return pl.ds(pl.multiple_of(head * width, width), width)


def pack_kernel(sent, width, query, key, value, grad_out, *refs):
    outs, (staged, sems) = refs[:-2], refs[-2:]
    group, block = lax.axis_index("head"), lax.axis_index("tm")
    arrays = (query, key, value, grad_out)
    copies = [pltpu.make_async_copy(a, staged.at[n], sems.at[n]) for n, a in enumerate(arrays)]
    for copy in copies:
        copy.start()
    for copy in copies:
        copy.wait()
    for step, out in enumerate(outs):
        head = looked_up(sent[step], group, block)

        @pl.when(head >= 0)
        def _():
            columns = head_columns(head, width)
            for n in range(3):
                out[n] = staged[n, :, columns]
            out[3] = staged[3, :, columns].T


def unpack_kernel(sent, width, *refs):
    parts, (attended, query_grad, key_grad, value_grad) = refs[:-4], refs[-4:]
    group, block = lax.axis_index("head"), lax.axis_index("tm")
    for step, part in enumerate(parts):
        head = looked_up(sent[step], group, block)

        @pl.when(head >= 0)
        def _():
            columns = head_columns(head, width)
            attended[:, columns] = part[0].T
            query_grad[:, columns] = part[1].T
            key_grad[:, columns] = part[2]
            value_grad[:, columns] = part[3]


def head_kernel(owned, partner, rows, frame_ids, sink_frame, window, *refs):
    blocks = len(partner)
    parts, outs = refs[:blocks], refs[blocks : 2 * blocks]
    (q_all, k_all, v_all, kt_all, vt_all, gt_all, weights, weights_low, grads_low, dk, dv, res) = refs[
        2 * blocks :
    ]
    group, block = lax.axis_index("head"), lax.axis_index("tm")
    head = looked_up(owned, group, block)
    width = q_all.shape[1]
    scaling = 1.0 / math.sqrt(width)
    rescale = scaling * math.log2(math.e)
    pair = 2 if blocks % 2 == 0 else 1
    chunk = pair * rows

    @pl.when(head >= 0)
    def _():
        span = window[head]
        sink = sink_frame[0]
        places = [looked_up(table, group, block) for table in partner]
        for part, place in zip(parts, places):
            at = pl.ds(pl.multiple_of(place * rows, rows), rows)
            q_all[at, :] = part[0]
            k_all[at, :] = part[1]
            v_all[at, :] = part[2]
            kt_all[:, at] = part[1].T
            vt_all[:, at] = part[2].T
            gt_all[:, at] = part[3]
        dk[...] = jnp.zeros_like(dk)
        dv[...] = jnp.zeros_like(dv)
        lane_block = lax.broadcasted_iota(jnp.int32, (1, chunk), 1) // rows

        def one_chunk(i, carry):
            at = pl.ds(pl.multiple_of(i * chunk, chunk), chunk)
            q_rows = q_all[at, :]
            top = jnp.full((1, chunk), hidden_score, jnp.float32)
            for j in range(blocks):
                frame = frame_ids[j]
                bias = jnp.zeros((1, chunk), jnp.float32)
                for k in range(pair):
                    own = frame_ids[i * pair + k]
                    seen = ((frame <= own) & (frame > own - span)) | ((frame == sink) & (sink <= own))
                    bias = jnp.where(lane_block == k, jnp.where(seen, 0.0, hidden_score), bias)
                keys = pl.ds(j * rows, rows)
                scores = dot(k_all[keys, :], q_rows, NT) * rescale + bias
                weights[keys, :] = scores
                top = jnp.maximum(top, jnp.max(scores, axis=0, keepdims=True))
            total = jnp.zeros((1, chunk), jnp.float32)
            for j in range(blocks):
                keys = pl.ds(j * rows, rows)
                p = jnp.exp2(weights[keys, :] - top)
                total = total + jnp.sum(p, axis=0, keepdims=True)
                weights[keys, :] = p
                weights_low[keys, :] = p.astype(jnp.bfloat16)
            inverse = 1.0 / total
            mixed = (dot(vt_all[...], weights_low[...], NN) * inverse).astype(jnp.bfloat16)
            grad_t = gt_all[:, at].astype(jnp.float32)
            delta = jnp.sum(grad_t * mixed.astype(jnp.float32), axis=0, keepdims=True) * inverse
            grad_low = (grad_t * inverse).astype(jnp.bfloat16)
            for j in range(blocks):
                keys = pl.ds(j * rows, rows)
                g = weights[keys, :] * (dot(v_all[keys, :], grad_low, NN) - delta)
                g = g.astype(jnp.bfloat16)
                grads_low[keys, :] = g
                dk[keys, :] += dot(g, q_rows, NN)
                dv[keys, :] += dot(weights_low[keys, :], grad_low, NT)
            query_grad = (dot(kt_all[...], grads_low[...], NN) * scaling).astype(jnp.bfloat16)
            for k in range(pair):
                res[i * pair + k, 0] = mixed[:, k * rows : (k + 1) * rows]
                res[i * pair + k, 1] = query_grad[:, k * rows : (k + 1) * rows]
            return carry

        if blocks // pair <= 4:
            for i in range(blocks // pair):
                one_chunk(i, 0)
        else:
            lax.fori_loop(0, blocks // pair, one_chunk, 0)
        for out, place in zip(outs, places):
            at = pl.ds(pl.multiple_of(place * rows, rows), rows)
            out[0] = res[place, 0]
            out[1] = res[place, 1]
            out[2] = (dk[at, :] * scaling).astype(jnp.bfloat16)
            out[3] = dv[at, :].astype(jnp.bfloat16)


def per_device(query, key, value, grad_out, frame_ids, sink_frame, window):
    rows, row_width = query.shape
    heads = window.shape[0]
    width = row_width // heads
    blocks = lax.axis_size("tm")
    owned, sent, partner, pairs = plan(blocks, lax.axis_size("head"), heads)
    axes = ("tm", "head")
    smem = pl.BlockSpec(memory_space=pltpu.SMEM)
    vmem = pl.BlockSpec(memory_space=pltpu.VMEM)
    in_place = pl.BlockSpec(memory_space=pltpu.HBM)
    part = jax.ShapeDtypeStruct((4, rows, width), query.dtype)
    local = jax.ShapeDtypeStruct(query.shape, query.dtype)

    parts = pl.pallas_call(
        functools.partial(pack_kernel, sent, width),
        out_shape=[part] * blocks,
        in_specs=[in_place] * 4,
        out_specs=[vmem] * blocks,
        scratch_shapes=[pltpu.VMEM((4, rows, row_width), query.dtype), pltpu.SemaphoreType.DMA((4,))],
        compiler_params=pltpu.CompilerParams(vmem_limit_bytes=62 * MIB),
        name="pack",
    )(query, key, value, grad_out)
    parts = [parts[0]] + [lax.ppermute(parts[s], axes, pairs[s]) for s in range(1, blocks)]

    tokens = blocks * rows
    chunk = (2 if blocks % 2 == 0 else 1) * rows
    low, full = query.dtype, jnp.float32
    parts = pl.pallas_call(
        functools.partial(head_kernel, owned, partner, rows),
        out_shape=[part] * blocks,
        in_specs=[smem] * 3 + [vmem] * blocks,
        out_specs=[vmem] * blocks,
        scratch_shapes=[pltpu.VMEM((tokens, width), low)] * 3
        + [pltpu.VMEM((width, tokens), low)] * 3
        + [
            pltpu.VMEM((tokens, chunk), full),
            pltpu.VMEM((tokens, chunk), low),
            pltpu.VMEM((tokens, chunk), low),
            pltpu.VMEM((tokens, width), full),
            pltpu.VMEM((tokens, width), full),
            pltpu.VMEM((blocks, 2, width, rows), low),
        ],
        compiler_params=pltpu.CompilerParams(vmem_limit_bytes=40 * MIB),
        name="head_attention",
    )(frame_ids, sink_frame, window, *parts)
    back = [[(owner, source) for source, owner in step] for step in pairs]
    parts = [parts[0]] + [lax.ppermute(parts[s], axes, back[s]) for s in range(1, blocks)]

    return pl.pallas_call(
        functools.partial(unpack_kernel, sent, width),
        out_shape=[local] * 4,
        in_specs=[vmem] * blocks,
        out_specs=[vmem] * 4,
        compiler_params=pltpu.CompilerParams(vmem_limit_bytes=24 * MIB),
        name="unpack",
    )(*parts)


def solution(mesh):
    spec = P("tm", "head")
    return jax.shard_map(
        per_device,
        mesh=mesh,
        in_specs=(spec, spec, spec, spec, P(), P(), P("head")),
        out_specs=(spec, spec, spec, spec),
        check_vma=False,
    )
```

```python
import functools
import math

import jax
import jax.numpy as jnp
import numpy as np
from jax import lax
from jax.experimental import pallas as pl
from jax.experimental.pallas import tpu as pltpu
from jax.sharding import PartitionSpec as P

hidden_score = -1e30
MIB = 1 << 20


even_rounds = (
    (
        ((5, 0), (1, 3), (6, 4)),
        ((2, 7), (0, 3), (7, 4), (4, 0), (3, 2)),
        ((1, 0), (6, 7), (5, 2)),
        ((4, 7), (3, 4), (0, 2), (2, 3), (7, 0)),
        ((5, 7), (1, 4), (6, 3)),
        ((3, 7), (0, 4), (4, 3), (7, 2), (2, 0)),
        ((6, 2), (5, 4), (1, 7)),
        ((2, 4), (4, 2), (3, 0), (0, 7), (7, 3)),
        ((1, 2), (6, 0), (5, 3)),
    ),
    (
        ((0, 4), (3, 5), (7, 6)),
        ((6, 5), (2, 6), (4, 1), (1, 4), (5, 2)),
        ((0, 2), (7, 4), (3, 6)),
        ((6, 1), (2, 5), (4, 2), (5, 4), (1, 6)),
        ((7, 2), (0, 5), (3, 1)),
        ((6, 2), (2, 4), (4, 6), (5, 1), (1, 5)),
        ((0, 6), (7, 1), (3, 2)),
        ((6, 4), (2, 1), (4, 5), (5, 6), (1, 2)),
        ((7, 5), (0, 1), (3, 4)),
    ),
)


def plan(blocks, groups, heads):
    laid_out = []
    for group in range(groups):
        if blocks == 8 and heads == 5:
            laid_out.append(even_rounds[group % 2])
        else:
            owners = [(head * blocks // heads + group % 2) % blocks for head in range(heads)]
            laid_out.append([[((u - step) % blocks, u) for u in owners] for step in range(1, blocks)])
    count = 1 + len(laid_out[0])
    owned = np.full((groups, blocks), -1)
    sent = np.full((count, groups, blocks), -1)
    partner = np.full((count, groups, blocks), -1)
    pairs = [[] for _ in range(count)]
    for group, rounds in enumerate(laid_out):
        owners = sorted({owner for step in rounds for _, owner in step})
        for step, exchanges in enumerate([[(u, u) for u in owners], *rounds]):
            for source, owner in exchanges:
                owned[group, owner] = owners.index(owner)
                sent[step, group, source] = owners.index(owner)
                partner[step, group, owner] = source
                pairs[step].append((source * groups + group, owner * groups + group))
    return owned, sent, partner, [sorted(step) for step in pairs]


def looked_up(table, group, block):
    groups, blocks = table.shape
    period = next(p for p in range(1, groups + 1) if (table == table[np.arange(groups) % p]).all())
    bits = int(table.max() + 1).bit_length()
    per_word = 31 // bits
    word = jnp.int32(0)
    for row in range(period):
        for first in range(0, blocks, per_word):
            values = table[row, first : first + per_word] + 1
            packed = sum(int(value) << (bits * n) for n, value in enumerate(values))
            here = (lax.rem(group, period) == row) & (block >= first) & (block < first + per_word)
            word = jnp.where(here, packed, word)
    return ((word >> (bits * lax.rem(block, per_word))) & ((1 << bits) - 1)) - 1


def dot(a, b, contract):
    return lax.dot_general(a, b, (contract, ((), ())), preferred_element_type=jnp.float32)


NN = ((1,), (0,))
NT = ((1,), (1,))


def head_columns(head, width):
    return pl.ds(pl.multiple_of(head * width, width), width)


def pack_kernel(sent, width, query, key, value, grad_out, *refs):
    outs, sems = refs[:-1], refs[-1]
    group, block = lax.axis_index("head"), lax.axis_index("tm")
    heads = [looked_up(table, group, block) for table in sent]

    def copies(step):
        columns = head_columns(jnp.maximum(heads[step], 0), width)
        return [
            pltpu.make_async_copy(array.at[:, columns], outs[step].at[n], sems.at[step, n])
            for n, array in enumerate((query, key, value, grad_out))
        ]

    for step in range(len(outs)):

        @pl.when(heads[step] >= 0)
        def _():
            for copy in copies(step):
                copy.start()

    for step in range(len(outs)):

        @pl.when(heads[step] >= 0)
        def _():
            for copy in copies(step):
                copy.wait()


def unpack_kernel(sent, width, *refs):
    parts, (attended, query_grad, key_grad, value_grad) = refs[:-4], refs[-4:]
    group, block = lax.axis_index("head"), lax.axis_index("tm")
    for step, part in enumerate(parts):
        head = looked_up(sent[step], group, block)

        @pl.when(head >= 0)
        def _():
            columns = head_columns(head, width)
            attended[:, columns] = part[0].T
            query_grad[:, columns] = part[1].T
            key_grad[:, columns] = part[2]
            value_grad[:, columns] = part[3]


def head_kernel(owned, partner, rows, frame_ids, sink_frame, window, *refs):
    count = len(partner)
    blocks = frame_ids.shape[0]
    parts, outs = refs[:count], refs[count : 2 * count]
    (q_all, k_all, v_all, kt_all, vt_all, gt_all, weights, weights_low, grads_low, dk, dv, res) = refs[
        2 * count :
    ]
    group, block = lax.axis_index("head"), lax.axis_index("tm")
    head = looked_up(owned, group, block)
    width = q_all.shape[1]
    scaling = 1.0 / math.sqrt(width)
    rescale = scaling * math.log2(math.e)
    pair = 2 if blocks % 2 == 0 else 1
    chunk = pair * rows

    @pl.when(head >= 0)
    def _():
        span = window[head]
        sink = sink_frame[0]
        places = [looked_up(table, group, block) for table in partner]
        for part, place in zip(parts, places):

            @pl.when(place >= 0)
            def _():
                at = pl.ds(pl.multiple_of(place * rows, rows), rows)
                q_all[at, :] = part[0]
                k_all[at, :] = part[1]
                v_all[at, :] = part[2]
                kt_all[:, at] = part[1].T
                vt_all[:, at] = part[2].T
                gt_all[:, at] = part[3].T

        dk[...] = jnp.zeros_like(dk)
        dv[...] = jnp.zeros_like(dv)
        lane_block = lax.broadcasted_iota(jnp.int32, (1, chunk), 1) // rows

        def one_chunk(i, carry):
            at = pl.ds(pl.multiple_of(i * chunk, chunk), chunk)
            q_rows = q_all[at, :]
            top = jnp.full((1, chunk), hidden_score, jnp.float32)
            for j in range(blocks):
                frame = frame_ids[j]
                bias = jnp.zeros((1, chunk), jnp.float32)
                for k in range(pair):
                    own = frame_ids[i * pair + k]
                    seen = ((frame <= own) & (frame > own - span)) | ((frame == sink) & (sink <= own))
                    bias = jnp.where(lane_block == k, jnp.where(seen, 0.0, hidden_score), bias)
                keys = pl.ds(j * rows, rows)
                scores = dot(k_all[keys, :], q_rows, NT) * rescale + bias
                weights[keys, :] = scores
                top = jnp.maximum(top, jnp.max(scores, axis=0, keepdims=True))
            total = jnp.zeros((1, chunk), jnp.float32)
            for j in range(blocks):
                keys = pl.ds(j * rows, rows)
                p = jnp.exp2(weights[keys, :] - top)
                total = total + jnp.sum(p, axis=0, keepdims=True)
                weights[keys, :] = p
                weights_low[keys, :] = p.astype(jnp.bfloat16)
            inverse = 1.0 / total
            mixed = (dot(vt_all[...], weights_low[...], NN) * inverse).astype(jnp.bfloat16)
            grad_t = gt_all[:, at].astype(jnp.float32)
            delta = jnp.sum(grad_t * mixed.astype(jnp.float32), axis=0, keepdims=True) * inverse
            grad_low = (grad_t * inverse).astype(jnp.bfloat16)
            for j in range(blocks):
                keys = pl.ds(j * rows, rows)
                g = weights[keys, :] * (dot(v_all[keys, :], grad_low, NN) - delta)
                g = g.astype(jnp.bfloat16)
                grads_low[keys, :] = g
                dk[keys, :] += dot(g, q_rows, NN)
                dv[keys, :] += dot(weights_low[keys, :], grad_low, NT)
            query_grad = (dot(kt_all[...], grads_low[...], NN) * scaling).astype(jnp.bfloat16)
            for k in range(pair):
                res[i * pair + k, 0] = mixed[:, k * rows : (k + 1) * rows]
                res[i * pair + k, 1] = query_grad[:, k * rows : (k + 1) * rows]
            return carry

        if blocks // pair <= 4:
            for i in range(blocks // pair):
                one_chunk(i, 0)
        else:
            lax.fori_loop(0, blocks // pair, one_chunk, 0)
        for out, place in zip(outs, places):

            @pl.when(place >= 0)
            def _():
                at = pl.ds(pl.multiple_of(place * rows, rows), rows)
                out[0] = res[place, 0]
                out[1] = res[place, 1]
                out[2] = (dk[at, :] * scaling).astype(jnp.bfloat16)
                out[3] = dv[at, :].astype(jnp.bfloat16)


def per_device(query, key, value, grad_out, frame_ids, sink_frame, window):
    rows, row_width = query.shape
    heads = window.shape[0]
    width = row_width // heads
    blocks = lax.axis_size("tm")
    owned, sent, partner, pairs = plan(blocks, lax.axis_size("head"), heads)
    axes = ("tm", "head")
    smem = pl.BlockSpec(memory_space=pltpu.SMEM)
    vmem = pl.BlockSpec(memory_space=pltpu.VMEM)
    in_place = pl.BlockSpec(memory_space=pltpu.HBM)
    part = jax.ShapeDtypeStruct((4, rows, width), query.dtype)
    local = jax.ShapeDtypeStruct(query.shape, query.dtype)

    count = len(pairs)
    parts = pl.pallas_call(
        functools.partial(pack_kernel, sent, width),
        out_shape=[part] * count,
        in_specs=[in_place] * 4,
        out_specs=[in_place] * count,
        scratch_shapes=[pltpu.SemaphoreType.DMA((count, 4))],
        compiler_params=pltpu.CompilerParams(vmem_limit_bytes=62 * MIB),
        name="pack",
    )(query, key, value, grad_out)
    parts = [parts[0]] + [lax.ppermute(parts[s], axes, pairs[s]) for s in range(1, count)]

    tokens = blocks * rows
    chunk = (2 if blocks % 2 == 0 else 1) * rows
    low, full = query.dtype, jnp.float32
    parts = pl.pallas_call(
        functools.partial(head_kernel, owned, partner, rows),
        out_shape=[part] * count,
        in_specs=[smem] * 3 + [vmem] * count,
        out_specs=[vmem] * count,
        scratch_shapes=[pltpu.VMEM((tokens, width), low)] * 3
        + [pltpu.VMEM((width, tokens), low)] * 3
        + [
            pltpu.VMEM((tokens, chunk), full),
            pltpu.VMEM((tokens, chunk), low),
            pltpu.VMEM((tokens, chunk), low),
            pltpu.VMEM((tokens, width), full),
            pltpu.VMEM((tokens, width), full),
            pltpu.VMEM((blocks, 2, width, rows), low),
        ],
        compiler_params=pltpu.CompilerParams(vmem_limit_bytes=40 * MIB),
        name="head_attention",
    )(frame_ids, sink_frame, window, *parts)
    back = [[(owner, source) for source, owner in step] for step in pairs]
    parts = [parts[0]] + [lax.ppermute(parts[s], axes, back[s]) for s in range(1, count)]

    return pl.pallas_call(
        functools.partial(unpack_kernel, sent, width),
        out_shape=[local] * 4,
        in_specs=[vmem] * count,
        out_specs=[vmem] * 4,
        compiler_params=pltpu.CompilerParams(vmem_limit_bytes=24 * MIB),
        name="unpack",
    )(*parts)


def solution(mesh):
    spec = P("tm", "head")
    return jax.shard_map(
        per_device,
        mesh=mesh,
        in_specs=(spec, spec, spec, spec, P(), P(), P("head")),
        out_specs=(spec, spec, spec, spec),
        check_vma=False,
    )
```

```python
import functools
import math

import jax
import jax.numpy as jnp
from jax import lax
from jax.experimental import pallas as pl
from jax.experimental.pallas import tpu as pltpu
from jax.sharding import PartitionSpec as P

hidden_score = -1e30
MIB = 1 << 20


def dot(a, b, contract):
    return lax.dot_general(a, b, (contract, ((), ())), preferred_element_type=jnp.float32)


NN = ((1,), (0,))
NT = ((1,), (1,))


def head_kernel(blocks, frame_ids, sink_frame, window, query, key, value, grad_out, *refs):
    attended, query_grad, key_grad, value_grad, weights, weights_low, grads_low, kt, vt = refs
    rows, width = query.shape
    scaling = 1.0 / math.sqrt(width)
    rescale = scaling * math.log2(math.e)
    span = window[pl.program_id(0)]
    sink = sink_frame[0]
    own = frame_ids[lax.axis_index("tm")]
    q_rows = query[...]
    top = jnp.full((1, rows), hidden_score, jnp.float32)
    for j in range(blocks):
        frame = frame_ids[j]
        seen = ((frame <= own) & (frame > own - span)) | ((frame == sink) & (sink <= own))
        bias = jnp.where(seen, 0.0, hidden_score)
        keys = pl.ds(j * rows, rows)
        scores = dot(key[keys, :], q_rows, NT) * rescale + bias
        weights[keys, :] = scores
        top = jnp.maximum(top, jnp.max(scores, axis=0, keepdims=True))
        kt[:, keys] = key[keys, :].T
        vt[:, keys] = value[keys, :].T
    total = jnp.zeros((1, rows), jnp.float32)
    for j in range(blocks):
        keys = pl.ds(j * rows, rows)
        p = jnp.exp2(weights[keys, :] - top)
        total = total + jnp.sum(p, axis=0, keepdims=True)
        weights[keys, :] = p
        weights_low[keys, :] = p.astype(jnp.bfloat16)
    inverse = 1.0 / total
    mixed = (dot(vt[...], weights_low[...], NN) * inverse).astype(jnp.bfloat16)
    grad_t = grad_out[...].T.astype(jnp.float32)
    delta = jnp.sum(grad_t * mixed.astype(jnp.float32), axis=0, keepdims=True) * inverse
    grad_low = (grad_t * inverse).astype(jnp.bfloat16)
    attended[...] = mixed.T
    for j in range(blocks):
        keys = pl.ds(j * rows, rows)
        g = weights[keys, :] * (dot(value[keys, :], grad_low, NN) - delta)
        g = g.astype(jnp.bfloat16)
        grads_low[keys, :] = g
        key_grad[keys, :] = (dot(g, q_rows, NN) * scaling).astype(jnp.bfloat16)
        value_grad[keys, :] = dot(weights_low[keys, :], grad_low, NT).astype(jnp.bfloat16)
    query_grad[...] = (dot(kt[...], grads_low[...], NN) * scaling).astype(jnp.bfloat16).T


def per_device(query, key, value, grad_out, frame_ids, sink_frame, window):
    rows, row_width = query.shape
    heads = window.shape[0]
    width = row_width // heads
    blocks = lax.axis_size("tm")
    tokens = blocks * rows
    low, full = query.dtype, jnp.float32
    all_keys = lax.all_gather(key, "tm", axis=0, tiled=True)
    all_values = lax.all_gather(value, "tm", axis=0, tiled=True)
    smem = pl.BlockSpec(memory_space=pltpu.SMEM)
    own = pl.BlockSpec((rows, width), lambda h: (0, h))
    every = pl.BlockSpec((tokens, width), lambda h: (0, h))
    attended, query_grad, key_part, value_part = pl.pallas_call(
        functools.partial(head_kernel, blocks),
        grid=(heads,),
        out_shape=[jax.ShapeDtypeStruct(query.shape, low)] * 2
        + [jax.ShapeDtypeStruct((tokens, row_width), low)] * 2,
        in_specs=[smem] * 3 + [own, every, every, own],
        out_specs=[own, own, every, every],
        scratch_shapes=[
            pltpu.VMEM((tokens, rows), full),
            pltpu.VMEM((tokens, rows), low),
            pltpu.VMEM((tokens, rows), low),
            pltpu.VMEM((width, tokens), low),
            pltpu.VMEM((width, tokens), low),
        ],
        compiler_params=pltpu.CompilerParams(vmem_limit_bytes=56 * MIB),
        name="head_attention",
    )(frame_ids, sink_frame, window, query, all_keys, all_values, grad_out)
    key_grad = lax.psum_scatter(key_part, "tm", scatter_dimension=0, tiled=True)
    value_grad = lax.psum_scatter(value_part, "tm", scatter_dimension=0, tiled=True)
    return attended, query_grad, key_grad, value_grad


def solution(mesh):
    spec = P("tm", "head")
    return jax.shard_map(
        per_device,
        mesh=mesh,
        in_specs=(spec, spec, spec, spec, P(), P(), P("head")),
        out_specs=(spec, spec, spec, spec),
        check_vma=False,
    )
```

```python
import functools
import math

import jax
import jax.numpy as jnp
import numpy as np
from jax import lax
from jax.experimental import pallas as pl
from jax.experimental.pallas import tpu as pltpu
from jax.sharding import PartitionSpec as P

hidden_score = -1e30
MIB = 1 << 20


even_rounds = (
    (
        ((5, 0), (1, 3), (6, 4)),
        ((1, 0), (6, 7), (5, 2)),
        ((5, 7), (1, 4), (6, 3)),
        ((6, 2), (5, 4), (1, 7)),
        ((1, 2), (6, 0), (5, 3)),
        ((2, 7), (0, 3), (7, 4), (4, 0), (3, 2)),
        ((4, 7), (3, 4), (0, 2), (2, 3), (7, 0)),
        ((3, 7), (0, 4), (4, 3), (7, 2), (2, 0)),
        ((2, 4), (4, 2), (3, 0), (0, 7), (7, 3)),
    ),
    (
        ((0, 4), (3, 5), (7, 6)),
        ((0, 2), (7, 4), (3, 6)),
        ((7, 2), (0, 5), (3, 1)),
        ((0, 6), (7, 1), (3, 2)),
        ((7, 5), (0, 1), (3, 4)),
        ((6, 5), (2, 6), (4, 1), (1, 4), (5, 2)),
        ((6, 1), (2, 5), (4, 2), (5, 4), (1, 6)),
        ((6, 2), (2, 4), (4, 6), (5, 1), (1, 5)),
        ((6, 4), (2, 1), (4, 5), (5, 6), (1, 2)),
    ),
)


def plan(blocks, groups, heads):
    laid_out = []
    for group in range(groups):
        if blocks == 8 and heads == 5:
            laid_out.append(even_rounds[group % 2])
        else:
            owners = [(head * blocks // heads + group % 2) % blocks for head in range(heads)]
            laid_out.append([[((u - step) % blocks, u) for u in owners] for step in range(1, blocks)])
    count = 1 + len(laid_out[0])
    owned = np.full((groups, blocks), -1)
    sent = np.full((count, groups, blocks), -1)
    partner = np.full((count, groups, blocks), -1)
    pairs = [[] for _ in range(count)]
    for group, rounds in enumerate(laid_out):
        owners = sorted({owner for step in rounds for _, owner in step})
        for step, exchanges in enumerate([[(u, u) for u in owners], *rounds]):
            for source, owner in exchanges:
                owned[group, owner] = owners.index(owner)
                sent[step, group, source] = owners.index(owner)
                partner[step, group, owner] = source
                pairs[step].append((source * groups + group, owner * groups + group))
    return owned, sent, partner, [sorted(step) for step in pairs]


def looked_up(table, group, block):
    groups, blocks = table.shape
    period = next(p for p in range(1, groups + 1) if (table == table[np.arange(groups) % p]).all())
    bits = int(table.max() + 1).bit_length()
    per_word = 31 // bits
    word = jnp.int32(0)
    for row in range(period):
        for first in range(0, blocks, per_word):
            values = table[row, first : first + per_word] + 1
            packed = sum(int(value) << (bits * n) for n, value in enumerate(values))
            here = (lax.rem(group, period) == row) & (block >= first) & (block < first + per_word)
            word = jnp.where(here, packed, word)
    return ((word >> (bits * lax.rem(block, per_word))) & ((1 << bits) - 1)) - 1


def dot(a, b, contract):
    return lax.dot_general(a, b, (contract, ((), ())), preferred_element_type=jnp.float32)


NN = ((1,), (0,))
NT = ((1,), (1,))


def head_columns(head, width):
    return pl.ds(pl.multiple_of(head * width, width), width)


def pack_kernel(sent, width, query, key, value, grad_out, *refs):
    outs, (staged, sems) = refs[:-2], refs[-2:]
    group, block = lax.axis_index("head"), lax.axis_index("tm")
    arrays = (query, key, value, grad_out)
    copies = [pltpu.make_async_copy(a, staged.at[n], sems.at[n]) for n, a in enumerate(arrays)]
    for copy in copies:
        copy.start()
    for copy in copies:
        copy.wait()
    for step, out in enumerate(outs):
        head = looked_up(sent[step], group, block)

        @pl.when(head >= 0)
        def _():
            columns = head_columns(head, width)
            for n in range(3):
                out[n] = staged[n, :, columns]
            out[3] = staged[3, :, columns].T


def unpack_kernel(sent, width, *refs):
    parts, (attended, query_grad, key_grad, value_grad) = refs[:-4], refs[-4:]
    group, block = lax.axis_index("head"), lax.axis_index("tm")
    for step, part in enumerate(parts):
        head = looked_up(sent[step], group, block)

        @pl.when(head >= 0)
        def _():
            columns = head_columns(head, width)
            attended[:, columns] = part[0].T
            query_grad[:, columns] = part[1].T
            key_grad[:, columns] = part[2]
            value_grad[:, columns] = part[3]


def head_kernel(owned, partner, rows, frame_ids, sink_frame, window, *refs):
    count = len(partner)
    blocks = frame_ids.shape[0]
    parts, outs = refs[:count], refs[count : 2 * count]
    (q_all, k_all, v_all, kt_all, vt_all, gt_all, weights, weights_low, grads_low, dk, dv, res) = refs[
        2 * count :
    ]
    group, block = lax.axis_index("head"), lax.axis_index("tm")
    head = looked_up(owned, group, block)
    width = q_all.shape[1]
    scaling = 1.0 / math.sqrt(width)
    rescale = scaling * math.log2(math.e)
    pair = 2 if blocks % 2 == 0 else 1
    chunk = pair * rows

    @pl.when(head >= 0)
    def _():
        span = window[head]
        sink = sink_frame[0]
        places = [looked_up(table, group, block) for table in partner]
        for part, place in zip(parts, places):

            @pl.when(place >= 0)
            def _():
                at = pl.ds(pl.multiple_of(place * rows, rows), rows)
                q_all[at, :] = part[0]
                k_all[at, :] = part[1]
                v_all[at, :] = part[2]
                kt_all[:, at] = part[1].T
                vt_all[:, at] = part[2].T
                gt_all[:, at] = part[3]

        dk[...] = jnp.zeros_like(dk)
        dv[...] = jnp.zeros_like(dv)
        lane_block = lax.broadcasted_iota(jnp.int32, (1, chunk), 1) // rows

        def one_chunk(i, carry):
            at = pl.ds(pl.multiple_of(i * chunk, chunk), chunk)
            q_rows = q_all[at, :]
            top = jnp.full((1, chunk), hidden_score, jnp.float32)
            for j in range(blocks):
                frame = frame_ids[j]
                bias = jnp.zeros((1, chunk), jnp.float32)
                for k in range(pair):
                    own = frame_ids[i * pair + k]
                    seen = ((frame <= own) & (frame > own - span)) | ((frame == sink) & (sink <= own))
                    bias = jnp.where(lane_block == k, jnp.where(seen, 0.0, hidden_score), bias)
                keys = pl.ds(j * rows, rows)
                scores = dot(k_all[keys, :], q_rows, NT) * rescale + bias
                weights[keys, :] = scores
                top = jnp.maximum(top, jnp.max(scores, axis=0, keepdims=True))
            total = jnp.zeros((1, chunk), jnp.float32)
            for j in range(blocks):
                keys = pl.ds(j * rows, rows)
                p = jnp.exp2(weights[keys, :] - top)
                total = total + jnp.sum(p, axis=0, keepdims=True)
                weights[keys, :] = p
                weights_low[keys, :] = p.astype(jnp.bfloat16)
            inverse = 1.0 / total
            mixed = (dot(vt_all[...], weights_low[...], NN) * inverse).astype(jnp.bfloat16)
            grad_t = gt_all[:, at].astype(jnp.float32)
            delta = jnp.sum(grad_t * mixed.astype(jnp.float32), axis=0, keepdims=True) * inverse
            grad_low = (grad_t * inverse).astype(jnp.bfloat16)
            for j in range(blocks):
                keys = pl.ds(j * rows, rows)
                g = weights[keys, :] * (dot(v_all[keys, :], grad_low, NN) - delta)
                g = g.astype(jnp.bfloat16)
                grads_low[keys, :] = g
                dk[keys, :] += dot(g, q_rows, NN)
                dv[keys, :] += dot(weights_low[keys, :], grad_low, NT)
            query_grad = (dot(kt_all[...], grads_low[...], NN) * scaling).astype(jnp.bfloat16)
            for k in range(pair):
                res[i * pair + k, 0] = mixed[:, k * rows : (k + 1) * rows]
                res[i * pair + k, 1] = query_grad[:, k * rows : (k + 1) * rows]
            return carry

        if blocks // pair <= 4:
            for i in range(blocks // pair):
                one_chunk(i, 0)
        else:
            lax.fori_loop(0, blocks // pair, one_chunk, 0)
        for out, place in zip(outs, places):

            @pl.when(place >= 0)
            def _():
                at = pl.ds(pl.multiple_of(place * rows, rows), rows)
                out[0] = res[place, 0]
                out[1] = res[place, 1]
                out[2] = (dk[at, :] * scaling).astype(jnp.bfloat16)
                out[3] = dv[at, :].astype(jnp.bfloat16)


def per_device(query, key, value, grad_out, frame_ids, sink_frame, window):
    rows, row_width = query.shape
    heads = window.shape[0]
    width = row_width // heads
    blocks = lax.axis_size("tm")
    owned, sent, partner, pairs = plan(blocks, lax.axis_size("head"), heads)
    axes = ("tm", "head")
    smem = pl.BlockSpec(memory_space=pltpu.SMEM)
    vmem = pl.BlockSpec(memory_space=pltpu.VMEM)
    in_place = pl.BlockSpec(memory_space=pltpu.HBM)
    part = jax.ShapeDtypeStruct((4, rows, width), query.dtype)
    local = jax.ShapeDtypeStruct(query.shape, query.dtype)

    count = len(pairs)
    parts = pl.pallas_call(
        functools.partial(pack_kernel, sent, width),
        out_shape=[part] * count,
        in_specs=[in_place] * 4,
        out_specs=[vmem] * count,
        scratch_shapes=[pltpu.VMEM((4, rows, row_width), query.dtype), pltpu.SemaphoreType.DMA((4,))],
        compiler_params=pltpu.CompilerParams(vmem_limit_bytes=62 * MIB),
        name="pack",
    )(query, key, value, grad_out)
    parts = [parts[0]] + [lax.ppermute(parts[s], axes, pairs[s]) for s in range(1, count)]

    tokens = blocks * rows
    chunk = (2 if blocks % 2 == 0 else 1) * rows
    low, full = query.dtype, jnp.float32
    parts = pl.pallas_call(
        functools.partial(head_kernel, owned, partner, rows),
        out_shape=[part] * count,
        in_specs=[smem] * 3 + [vmem] * count,
        out_specs=[vmem] * count,
        scratch_shapes=[pltpu.VMEM((tokens, width), low)] * 3
        + [pltpu.VMEM((width, tokens), low)] * 3
        + [
            pltpu.VMEM((tokens, chunk), full),
            pltpu.VMEM((tokens, chunk), low),
            pltpu.VMEM((tokens, chunk), low),
            pltpu.VMEM((tokens, width), full),
            pltpu.VMEM((tokens, width), full),
            pltpu.VMEM((blocks, 2, width, rows), low),
        ],
        compiler_params=pltpu.CompilerParams(vmem_limit_bytes=40 * MIB),
        name="head_attention",
    )(frame_ids, sink_frame, window, *parts)
    back = [[(owner, source) for source, owner in step] for step in pairs]
    parts = list(parts)
    for step in sorted(range(1, count), key=lambda s: -len(back[s])):
        parts[step] = lax.ppermute(parts[step], axes, back[step])

    return pl.pallas_call(
        functools.partial(unpack_kernel, sent, width),
        out_shape=[local] * 4,
        in_specs=[vmem] * count,
        out_specs=[vmem] * 4,
        compiler_params=pltpu.CompilerParams(vmem_limit_bytes=24 * MIB),
        name="unpack",
    )(*parts)


def solution(mesh):
    spec = P("tm", "head")
    return jax.shard_map(
        per_device,
        mesh=mesh,
        in_specs=(spec, spec, spec, spec, P(), P(), P("head")),
        out_specs=(spec, spec, spec, spec),
        check_vma=False,
    )
```

```python
import functools
import math

import jax
import jax.numpy as jnp
import numpy as np
from jax import lax
from jax.experimental import pallas as pl
from jax.experimental.pallas import tpu as pltpu
from jax.sharding import PartitionSpec as P

hidden_score = -1e30
MIB = 1 << 20


even_rounds = (
    {
        0: (3, 6, 5, 7, 1, 2, 4),
        1: (4, 7, 6, 2, 0, 3, 5),
        3: (7, 2, 0, 4, 6, 5, 1),
        5: (6, 0, 7, 1, 2, 4, 3),
        6: (2, 3, 1, 5, 4, 0, 7),
    },
    {
        2: (5, 6, 7, 1, 0, 4, 3),
        3: (0, 5, 4, 6, 7, 1, 2),
        4: (7, 1, 3, 2, 5, 6, 0),
        5: (3, 4, 2, 0, 1, 7, 6),
        7: (1, 2, 0, 4, 6, 3, 5),
    },
)


def plan(blocks, groups, heads):
    laid_out = []
    for group in range(groups):
        if blocks == 8 and heads == 5:
            laid_out.append(even_rounds[group % 2])
        else:
            owners = [(head * blocks // heads + group % 2) % blocks for head in range(heads)]
            laid_out.append({u: [(u - step) % blocks for step in range(1, blocks)] for u in owners})
    owned = np.full((groups, blocks), -1)
    sent = np.full((blocks, groups, blocks), -1)
    partner = np.full((blocks, groups, blocks), -1)
    pairs = [[] for _ in range(blocks)]
    for group, rounds in enumerate(laid_out):
        for head, (owner, sources) in enumerate(rounds.items()):
            owned[group, owner] = head
            for step, source in enumerate((owner, *sources)):
                sent[step, group, source] = head
                partner[step, group, owner] = source
                pairs[step].append((source * groups + group, owner * groups + group))
    return owned, sent, partner, [sorted(step) for step in pairs]


def looked_up(table, group, block):
    groups, blocks = table.shape
    period = next(p for p in range(1, groups + 1) if (table == table[np.arange(groups) % p]).all())
    bits = int(table.max() + 1).bit_length()
    per_word = 31 // bits
    word = jnp.int32(0)
    for row in range(period):
        for first in range(0, blocks, per_word):
            values = table[row, first : first + per_word] + 1
            packed = sum(int(value) << (bits * n) for n, value in enumerate(values))
            here = (lax.rem(group, period) == row) & (block >= first) & (block < first + per_word)
            word = jnp.where(here, packed, word)
    return ((word >> (bits * lax.rem(block, per_word))) & ((1 << bits) - 1)) - 1


def dot(a, b, contract):
    return lax.dot_general(a, b, (contract, ((), ())), preferred_element_type=jnp.float32)


NN = ((1,), (0,))
NT = ((1,), (1,))


def head_columns(head, width):
    return pl.ds(pl.multiple_of(head * width, width), width)


def pack_kernel(sent, width, query, key, value, grad_out, *refs):
    outs, (staged, packed, in_sems, out_sems) = refs[:-4], refs[-4:]
    group, block = lax.axis_index("head"), lax.axis_index("tm")
    arrays = (query, key, value, grad_out)
    loads = [pltpu.make_async_copy(a, staged.at[n], in_sems.at[n]) for n, a in enumerate(arrays)]
    for load in loads:
        load.start()
    heads = [looked_up(table, group, block) for table in sent]
    stores = [pltpu.make_async_copy(packed.at[n], out, out_sems.at[n]) for n, out in enumerate(outs)]
    for load in loads:
        load.wait()
    for step, head in enumerate(heads):

        @pl.when(head >= 0)
        def _():
            columns = head_columns(head, width)
            for n in range(3):
                packed[step, n] = staged[n, :, columns]
            packed[step, 3] = staged[3, :, columns].T
            stores[step].start()

    for step, head in enumerate(heads):

        @pl.when(head >= 0)
        def _():
            stores[step].wait()


def unpack_kernel(sent, width, *refs):
    parts, (attended, query_grad, key_grad, value_grad) = refs[:-4], refs[-4:]
    group, block = lax.axis_index("head"), lax.axis_index("tm")
    for step, part in enumerate(parts):
        head = looked_up(sent[step], group, block)

        @pl.when(head >= 0)
        def _():
            columns = head_columns(head, width)
            attended[:, columns] = part[0].T
            query_grad[:, columns] = part[1].T
            key_grad[:, columns] = part[2]
            value_grad[:, columns] = part[3]


def head_kernel(owned, partner, rows, frame_ids, sink_frame, window, local, *refs):
    blocks = len(partner)
    parts, outs, scratch = refs[: blocks - 1], refs[blocks - 1 : 2 * blocks - 1], refs[2 * blocks - 1 :]
    (here, q_all, kt_all, vt_all, gt_all, weights, weights_low, grads_low, grad_scaled, dk, dv, res, sem) = scratch
    parts = (here, *parts)
    group, block = lax.axis_index("head"), lax.axis_index("tm")
    head = looked_up(owned, group, block)
    width = q_all.shape[1]
    scaling = 1.0 / math.sqrt(width)
    rescale = scaling * math.log2(math.e)
    stretch = weights.shape[1]
    half = stretch // 2
    each = half // rows

    @pl.when(head >= 0)
    def _():
        fetch = pltpu.make_async_copy(local, here, sem)
        fetch.start()
        span = window[head]
        sink = sink_frame[0]
        frames = [frame_ids[looked_up(table, group, block)] for table in partner]

        def placed(j):
            at = pl.ds(j * rows, rows)
            q_all[at, :] = parts[j][0]
            kt_all[:, at] = parts[j][1].T
            vt_all[:, at] = parts[j][2].T
            gt_all[:, at] = parts[j][3]

        for j in range(1, blocks):
            placed(j)
        fetch.wait()
        placed(0)
        dk[...] = jnp.zeros_like(dk)
        dv[...] = jnp.zeros_like(dv)
        lane_block = lax.broadcasted_iota(jnp.int32, (1, half), 1) // rows

        def one_stretch(i, carry):
            at = [pl.ds(pl.multiple_of(i * stretch + h * half, half), half) for h in range(2)]
            lanes = [pl.ds(h * half, half) for h in range(2)]
            keys = [pl.ds(j * rows, rows) for j in range(blocks)]
            q_rows = [q_all[at[h], :] for h in range(2)]
            top = [jnp.full((1, half), hidden_score, jnp.float32)] * 2
            total = [jnp.zeros((1, half), jnp.float32)] * 2
            delta = [None] * 2
            own = [[], []]
            for h in range(2):
                for k in range(each):
                    n = i * 2 * each + h * each + k
                    own[h].append(sum(jnp.where(n == j, frames[j], 0) for j in range(blocks)))

            def score(h, j):
                bias = jnp.zeros((1, half), jnp.float32)
                for k in range(each):
                    seen = (frames[j] <= own[h][k]) & (frames[j] > own[h][k] - span)
                    seen = seen | ((frames[j] == sink) & (sink <= own[h][k]))
                    bias = jnp.where(lane_block == k, jnp.where(seen, 0.0, hidden_score), bias)
                scores = dot(parts[j][1], q_rows[h], NT) * rescale + bias
                weights[keys[j], lanes[h]] = scores
                top[h] = jnp.maximum(top[h], jnp.max(scores, axis=0, keepdims=True))

            def weigh(h, j):
                p = jnp.exp2(weights[keys[j], lanes[h]] - top[h])
                total[h] = total[h] + jnp.sum(p, axis=0, keepdims=True)
                weights[keys[j], lanes[h]] = p
                weights_low[keys[j], lanes[h]] = p.astype(jnp.bfloat16)

            def attend(h):
                inverse = 1.0 / total[h]
                mixed = (dot(vt_all[...], weights_low[:, lanes[h]], NN) * inverse).astype(jnp.bfloat16)
                grad_t = gt_all[:, at[h]].astype(jnp.float32)
                delta[h] = jnp.sum(grad_t * mixed.astype(jnp.float32), axis=0, keepdims=True) * inverse
                grad_scaled[:, lanes[h]] = (grad_t * inverse).astype(jnp.bfloat16)
                for k in range(each):
                    res[i * 2 * each + h * each + k, 0] = mixed[:, k * rows : (k + 1) * rows]

            def differ(h, j):
                g = dot(parts[j][2], grad_scaled[:, lanes[h]], NN) - delta[h]
                grads_low[keys[j], lanes[h]] = (weights[keys[j], lanes[h]] * g).astype(jnp.bfloat16)

            def query_part(h):
                grad = (dot(kt_all[...], grads_low[:, lanes[h]], NN) * scaling).astype(jnp.bfloat16)
                for k in range(each):
                    res[i * 2 * each + h * each + k, 1] = grad[:, k * rows : (k + 1) * rows]

            for j in range(blocks):
                score(0, j)
            for j in range(blocks):
                score(1, j)
                weigh(0, j)
            attend(0)
            for j in range(blocks):
                weigh(1, j)
                differ(0, j)
            attend(1)
            query_part(0)
            q_both = jnp.concatenate(q_rows, axis=0)
            for j in range(blocks):
                differ(1, j)
                dk[keys[j], :] += dot(grads_low[keys[j], :], q_both, NN)
                dv[keys[j], :] += dot(weights_low[keys[j], :], grad_scaled[...], NT)
            query_part(1)
            return carry

        lax.fori_loop(0, blocks * rows // stretch, one_stretch, 0)
        for j, out in enumerate(outs):
            at = pl.ds(j * rows, rows)
            out[0] = res[j, 0]
            out[1] = res[j, 1]
            out[2] = (dk[at, :] * scaling).astype(jnp.bfloat16)
            out[3] = dv[at, :].astype(jnp.bfloat16)


def per_device(query, key, value, grad_out, frame_ids, sink_frame, window):
    rows, row_width = query.shape
    heads = window.shape[0]
    width = row_width // heads
    blocks = lax.axis_size("tm")
    owned, sent, partner, pairs = plan(blocks, lax.axis_size("head"), heads)
    axes = ("tm", "head")
    smem = pl.BlockSpec(memory_space=pltpu.SMEM)
    vmem = pl.BlockSpec(memory_space=pltpu.VMEM)
    in_place = pl.BlockSpec(memory_space=pltpu.HBM)
    part = jax.ShapeDtypeStruct((4, rows, width), query.dtype)
    local = jax.ShapeDtypeStruct(query.shape, query.dtype)

    parts = pl.pallas_call(
        functools.partial(pack_kernel, sent, width),
        out_shape=[part] * blocks,
        in_specs=[in_place] * 4,
        out_specs=[in_place] * blocks,
        scratch_shapes=[
            pltpu.VMEM((4, rows, row_width), query.dtype),
            pltpu.VMEM((blocks, 4, rows, width), query.dtype),
            pltpu.SemaphoreType.DMA((4,)),
            pltpu.SemaphoreType.DMA((blocks,)),
        ],
        compiler_params=pltpu.CompilerParams(vmem_limit_bytes=62 * MIB),
        name="pack",
    )(query, key, value, grad_out)
    parts = [parts[0]] + [lax.ppermute(parts[s], axes, pairs[s]) for s in range(1, blocks)]

    tokens = blocks * rows
    stretch = (4 if blocks % 4 == 0 else 2) * rows
    low, full = query.dtype, jnp.float32
    parts = pl.pallas_call(
        functools.partial(head_kernel, owned, partner, rows),
        out_shape=[part] * blocks,
        in_specs=[smem] * 3 + [pl.BlockSpec(memory_space=pl.ANY)] + [vmem] * (blocks - 1),
        out_specs=[vmem] * blocks,
        scratch_shapes=[
            pltpu.VMEM((4, rows, width), low),
            pltpu.VMEM((tokens, width), low),
            pltpu.VMEM((width, tokens), low),
            pltpu.VMEM((width, tokens), low),
            pltpu.VMEM((width, tokens), low),
            pltpu.VMEM((tokens, stretch), full),
            pltpu.VMEM((tokens, stretch), low),
            pltpu.VMEM((tokens, stretch), low),
            pltpu.VMEM((width, stretch), low),
            pltpu.VMEM((tokens, width), full),
            pltpu.VMEM((tokens, width), full),
            pltpu.VMEM((blocks, 2, width, rows), low),
            pltpu.SemaphoreType.DMA,
        ],
        compiler_params=pltpu.CompilerParams(vmem_limit_bytes=48 * MIB),
        name="head_attention",
    )(frame_ids, sink_frame, window, *parts)
    back = [[(owner, source) for source, owner in step] for step in pairs]
    parts = [parts[0]] + [lax.ppermute(parts[s], axes, back[s]) for s in range(1, blocks)]

    return pl.pallas_call(
        functools.partial(unpack_kernel, sent, width),
        out_shape=[local] * 4,
        in_specs=[vmem] * blocks,
        out_specs=[vmem] * 4,
        compiler_params=pltpu.CompilerParams(vmem_limit_bytes=24 * MIB),
        name="unpack",
    )(*parts)


def solution(mesh):
    spec = P("tm", "head")
    return jax.shard_map(
        per_device,
        mesh=mesh,
        in_specs=(spec, spec, spec, spec, P(), P(), P("head")),
        out_specs=(spec, spec, spec, spec),
        check_vma=False,
    )
```

```python
import functools
import math

import jax
import jax.numpy as jnp
import numpy as np
from jax import lax
from jax.experimental import pallas as pl
from jax.experimental.pallas import tpu as pltpu
from jax.sharding import PartitionSpec as P

hidden_score = -1e30
MIB = 1 << 20


rounds_in = (
    (
        ((2, 6), (3, 1), (4, 5), (6, 3), (7, 0)),
        ((0, 3), (1, 6), (2, 5), (5, 0), (7, 1)),
        ((0, 1), (1, 5), (2, 0), (4, 3), (5, 6)),
        ((0, 6), (1, 3), (3, 5), (4, 0), (5, 1)),
        ((1, 0), (3, 6), (4, 1), (6, 5), (7, 3)),
        ((0, 5), (2, 1), (5, 3), (6, 0), (7, 6)),
        ((2, 3), (3, 0), (4, 6), (6, 1), (7, 5)),
    ),
    (
        ((0, 5), (1, 2), (3, 4), (5, 7), (6, 3)),
        ((0, 2), (2, 4), (3, 7), (4, 3), (7, 5)),
        ((1, 4), (2, 7), (3, 2), (6, 5), (7, 3)),
        ((0, 3), (2, 5), (4, 7), (6, 2), (7, 4)),
        ((0, 7), (1, 5), (4, 2), (5, 3), (6, 4)),
        ((1, 7), (2, 3), (4, 5), (5, 4), (7, 2)),
        ((0, 4), (1, 3), (3, 5), (5, 2), (6, 7)),
    ),
)
rounds_back = (
    (
        ((2, 3), (4, 1), (5, 6), (6, 5), (7, 0)),
        ((0, 6), (1, 0), (2, 1), (3, 5), (7, 3)),
        ((0, 1), (1, 5), (5, 0), (6, 3), (7, 6)),
        ((2, 6), (3, 1), (4, 5), (5, 3), (6, 0)),
        ((1, 3), (3, 0), (4, 6), (6, 1), (7, 5)),
        ((0, 5), (1, 6), (2, 0), (4, 3), (7, 1)),
        ((0, 3), (2, 5), (3, 6), (4, 0), (5, 1)),
    ),
    (
        ((0, 4), (1, 7), (3, 2), (4, 3), (6, 5)),
        ((0, 7), (2, 4), (4, 5), (5, 3), (6, 2)),
        ((0, 5), (1, 2), (3, 4), (6, 7), (7, 3)),
        ((1, 3), (2, 7), (3, 5), (5, 4), (7, 2)),
        ((1, 4), (2, 5), (3, 7), (5, 2), (6, 3)),
        ((0, 3), (4, 2), (5, 7), (6, 4), (7, 5)),
        ((0, 2), (1, 5), (2, 3), (4, 7), (7, 4)),
    ),
)


def plan(blocks, groups, heads):
    by_shift = []
    for group in range(groups):
        owners = [(head * blocks // heads + group % 2) % blocks for head in range(heads)]
        by_shift.append([[((u - step) % blocks, u) for u in owners] for step in range(1, blocks)])
    special = blocks == 8 and heads == 5
    ways = []
    for table in (rounds_in, rounds_back):
        laid_out = [table[group % 2] for group in range(groups)] if special else by_shift
        count = 1 + len(laid_out[0])
        owned = np.full((groups, blocks), -1)
        sent = np.full((count, groups, blocks), -1)
        partner = np.full((count, groups, blocks), -1)
        pairs = [[] for _ in range(count)]
        for group, rounds in enumerate(laid_out):
            owners = sorted({owner for step in rounds for _, owner in step})
            for step, exchanges in enumerate([[(u, u) for u in owners], *rounds]):
                for source, owner in exchanges:
                    owned[group, owner] = owners.index(owner)
                    sent[step, group, source] = owners.index(owner)
                    partner[step, group, owner] = source
                    pairs[step].append((source * groups + group, owner * groups + group))
        ways.append((sent, partner, [sorted(step) for step in pairs]))
    return owned, *ways


def looked_up(table, group, block):
    groups, blocks = table.shape
    period = next(p for p in range(1, groups + 1) if (table == table[np.arange(groups) % p]).all())
    bits = int(table.max() + 1).bit_length()
    per_word = 31 // bits
    word = jnp.int32(0)
    for row in range(period):
        for first in range(0, blocks, per_word):
            values = table[row, first : first + per_word] + 1
            packed = sum(int(value) << (bits * n) for n, value in enumerate(values))
            here = (lax.rem(group, period) == row) & (block >= first) & (block < first + per_word)
            word = jnp.where(here, packed, word)
    return ((word >> (bits * lax.rem(block, per_word))) & ((1 << bits) - 1)) - 1


def dot(a, b, contract):
    return lax.dot_general(a, b, (contract, ((), ())), preferred_element_type=jnp.float32)


NN = ((1,), (0,))
NT = ((1,), (1,))


def head_columns(head, width):
    return pl.ds(pl.multiple_of(head * width, width), width)


def pack_kernel(sent, width, query, key, value, grad_out, *refs):
    outs, (staged, packed, in_sems, out_sems) = refs[:-4], refs[-4:]
    group, block = lax.axis_index("head"), lax.axis_index("tm")
    arrays = (query, key, value, grad_out)
    loads = [pltpu.make_async_copy(a, staged.at[n], in_sems.at[n]) for n, a in enumerate(arrays)]
    for load in loads:
        load.start()
    heads = [looked_up(table, group, block) for table in sent]
    stores = [pltpu.make_async_copy(packed.at[n], out, out_sems.at[n]) for n, out in enumerate(outs)]
    for load in loads:
        load.wait()
    for step, head in enumerate(heads):

        @pl.when(head >= 0)
        def _():
            columns = head_columns(head, width)
            for n in range(3):
                packed[step, n] = staged[n, :, columns]
            packed[step, 3] = staged[3, :, columns].T
            stores[step].start()

    for step, head in enumerate(heads):

        @pl.when(head >= 0)
        def _():
            stores[step].wait()


def unpack_kernel(sent, width, *refs):
    parts, (attended, query_grad, key_grad, value_grad) = refs[:-4], refs[-4:]
    group, block = lax.axis_index("head"), lax.axis_index("tm")
    for step, part in enumerate(parts):
        head = looked_up(sent[step], group, block)

        @pl.when(head >= 0)
        def _():
            columns = head_columns(head, width)
            attended[:, columns] = part[0].T
            query_grad[:, columns] = part[1].T
            key_grad[:, columns] = part[2]
            value_grad[:, columns] = part[3]


def head_kernel(owned, partner, partner_back, rows, frame_ids, sink_frame, window, local, *refs):
    blocks = len(partner)
    parts, refs = refs[: blocks - 1], refs[blocks - 1 :]
    outs, scratch = refs[: len(partner_back)], refs[len(partner_back) :]
    (here, q_all, kt_all, vt_all, gt_all, weights, weights_low, grads_low, grad_scaled, dk, dv, res, sem) = scratch
    parts = (here, *parts)
    group, block = lax.axis_index("head"), lax.axis_index("tm")
    head = looked_up(owned, group, block)
    width = q_all.shape[1]
    scaling = 1.0 / math.sqrt(width)
    rescale = scaling * math.log2(math.e)
    stretch = weights.shape[1]
    half = stretch // 2
    each = half // rows

    @pl.when(head >= 0)
    def _():
        fetch = pltpu.make_async_copy(local, here, sem)
        fetch.start()
        span = window[head]
        sink = sink_frame[0]
        frames = [frame_ids[looked_up(table, group, block)] for table in partner]

        def placed(j):
            at = pl.ds(j * rows, rows)
            q_all[at, :] = parts[j][0]
            kt_all[:, at] = parts[j][1].T
            vt_all[:, at] = parts[j][2].T
            gt_all[:, at] = parts[j][3]

        for j in range(1, blocks):
            placed(j)
        fetch.wait()
        placed(0)
        dk[...] = jnp.zeros_like(dk)
        dv[...] = jnp.zeros_like(dv)
        lane_block = lax.broadcasted_iota(jnp.int32, (1, half), 1) // rows

        def one_stretch(i, carry):
            at = [pl.ds(pl.multiple_of(i * stretch + h * half, half), half) for h in range(2)]
            lanes = [pl.ds(h * half, half) for h in range(2)]
            keys = [pl.ds(j * rows, rows) for j in range(blocks)]
            q_rows = [q_all[at[h], :] for h in range(2)]
            top = [jnp.full((1, half), hidden_score, jnp.float32)] * 2
            total = [jnp.zeros((1, half), jnp.float32)] * 2
            delta = [None] * 2
            own = [[], []]
            for h in range(2):
                for k in range(each):
                    n = i * 2 * each + h * each + k
                    own[h].append(sum(jnp.where(n == j, frames[j], 0) for j in range(blocks)))

            def score(h, j):
                bias = jnp.zeros((1, half), jnp.float32)
                for k in range(each):
                    seen = (frames[j] <= own[h][k]) & (frames[j] > own[h][k] - span)
                    seen = seen | ((frames[j] == sink) & (sink <= own[h][k]))
                    bias = jnp.where(lane_block == k, jnp.where(seen, 0.0, hidden_score), bias)
                scores = dot(parts[j][1], q_rows[h], NT) * rescale + bias
                weights[keys[j], lanes[h]] = scores
                top[h] = jnp.maximum(top[h], jnp.max(scores, axis=0, keepdims=True))

            def weigh(h, j):
                p = jnp.exp2(weights[keys[j], lanes[h]] - top[h])
                total[h] = total[h] + jnp.sum(p, axis=0, keepdims=True)
                weights[keys[j], lanes[h]] = p
                weights_low[keys[j], lanes[h]] = p.astype(jnp.bfloat16)

            def attend(h):
                inverse = 1.0 / total[h]
                mixed = (dot(vt_all[...], weights_low[:, lanes[h]], NN) * inverse).astype(jnp.bfloat16)
                grad_t = gt_all[:, at[h]].astype(jnp.float32)
                delta[h] = jnp.sum(grad_t * mixed.astype(jnp.float32), axis=0, keepdims=True) * inverse
                grad_scaled[:, lanes[h]] = (grad_t * inverse).astype(jnp.bfloat16)
                for k in range(each):
                    res[i * 2 * each + h * each + k, 0] = mixed[:, k * rows : (k + 1) * rows]

            def differ(h, j):
                g = dot(parts[j][2], grad_scaled[:, lanes[h]], NN) - delta[h]
                grads_low[keys[j], lanes[h]] = (weights[keys[j], lanes[h]] * g).astype(jnp.bfloat16)

            def query_part(h):
                grad = (dot(kt_all[...], grads_low[:, lanes[h]], NN) * scaling).astype(jnp.bfloat16)
                for k in range(each):
                    res[i * 2 * each + h * each + k, 1] = grad[:, k * rows : (k + 1) * rows]

            for j in range(blocks):
                score(0, j)
            for j in range(blocks):
                score(1, j)
                weigh(0, j)
            attend(0)
            for j in range(blocks):
                weigh(1, j)
                differ(0, j)
            attend(1)
            query_part(0)
            q_both = jnp.concatenate(q_rows, axis=0)
            for j in range(blocks):
                differ(1, j)
                dk[keys[j], :] += dot(grads_low[keys[j], :], q_both, NN)
                dv[keys[j], :] += dot(weights_low[keys[j], :], grad_scaled[...], NT)
            query_part(1)
            return carry

        lax.fori_loop(0, blocks * rows // stretch, one_stretch, 0)
        places = [looked_up(table, group, block) for table in partner]
        for step, out in enumerate(outs):
            place = looked_up(partner_back[step], group, block)
            slot = sum(jnp.where(places[j] == place, j, 0) for j in range(blocks))
            at = pl.ds(pl.multiple_of(slot * rows, rows), rows)

            @pl.when(place >= 0)
            def _():
                out[0] = res[slot, 0]
                out[1] = res[slot, 1]
                out[2] = (dk[at, :] * scaling).astype(jnp.bfloat16)
                out[3] = dv[at, :].astype(jnp.bfloat16)


def per_device(query, key, value, grad_out, frame_ids, sink_frame, window):
    rows, row_width = query.shape
    heads = window.shape[0]
    width = row_width // heads
    blocks = lax.axis_size("tm")
    owned, (sent, partner, pairs), (sent_back, partner_back, pairs_back) = plan(
        blocks, lax.axis_size("head"), heads
    )
    axes = ("tm", "head")
    smem = pl.BlockSpec(memory_space=pltpu.SMEM)
    vmem = pl.BlockSpec(memory_space=pltpu.VMEM)
    in_place = pl.BlockSpec(memory_space=pltpu.HBM)
    part = jax.ShapeDtypeStruct((4, rows, width), query.dtype)
    local = jax.ShapeDtypeStruct(query.shape, query.dtype)

    parts = pl.pallas_call(
        functools.partial(pack_kernel, sent, width),
        out_shape=[part] * blocks,
        in_specs=[in_place] * 4,
        out_specs=[in_place] * blocks,
        scratch_shapes=[
            pltpu.VMEM((4, rows, row_width), query.dtype),
            pltpu.VMEM((blocks, 4, rows, width), query.dtype),
            pltpu.SemaphoreType.DMA((4,)),
            pltpu.SemaphoreType.DMA((blocks,)),
        ],
        compiler_params=pltpu.CompilerParams(vmem_limit_bytes=62 * MIB),
        name="pack",
    )(query, key, value, grad_out)
    parts = [parts[0]] + [lax.ppermute(parts[s], axes, pairs[s]) for s in range(1, blocks)]

    tokens = blocks * rows
    stretch = (4 if blocks % 4 == 0 else 2) * rows
    low, full = query.dtype, jnp.float32
    parts = pl.pallas_call(
        functools.partial(head_kernel, owned, partner, partner_back, rows),
        out_shape=[part] * len(pairs_back),
        in_specs=[smem] * 3 + [pl.BlockSpec(memory_space=pl.ANY)] + [vmem] * (blocks - 1),
        out_specs=[vmem] * len(pairs_back),
        scratch_shapes=[
            pltpu.VMEM((4, rows, width), low),
            pltpu.VMEM((tokens, width), low),
            pltpu.VMEM((width, tokens), low),
            pltpu.VMEM((width, tokens), low),
            pltpu.VMEM((width, tokens), low),
            pltpu.VMEM((tokens, stretch), full),
            pltpu.VMEM((tokens, stretch), low),
            pltpu.VMEM((tokens, stretch), low),
            pltpu.VMEM((width, stretch), low),
            pltpu.VMEM((tokens, width), full),
            pltpu.VMEM((tokens, width), full),
            pltpu.VMEM((blocks, 2, width, rows), low),
            pltpu.SemaphoreType.DMA,
        ],
        compiler_params=pltpu.CompilerParams(vmem_limit_bytes=48 * MIB),
        name="head_attention",
    )(frame_ids, sink_frame, window, *parts)
    back = [[(owner, source) for source, owner in step] for step in pairs_back]
    count = len(back)
    parts = [parts[0]] + [lax.ppermute(parts[s], axes, back[s]) for s in range(1, count)]

    return pl.pallas_call(
        functools.partial(unpack_kernel, sent_back, width),
        out_shape=[local] * 4,
        in_specs=[vmem] * count,
        out_specs=[vmem] * 4,
        compiler_params=pltpu.CompilerParams(vmem_limit_bytes=24 * MIB),
        name="unpack",
    )(*parts)


def solution(mesh):
    spec = P("tm", "head")
    return jax.shard_map(
        per_device,
        mesh=mesh,
        in_specs=(spec, spec, spec, spec, P(), P(), P("head")),
        out_specs=(spec, spec, spec, spec),
        check_vma=False,
    )
```

```python
import functools
import math

import jax
import jax.numpy as jnp
import numpy as np
from jax import lax
from jax.experimental import pallas as pl
from jax.experimental.pallas import tpu as pltpu
from jax.sharding import PartitionSpec as P

hidden_score = -1e30
MIB = 1 << 20
split_limit = 1024


even_rounds = (
    {
        0: (3, 6, 5, 7, 1, 2, 4),
        1: (4, 7, 6, 2, 0, 3, 5),
        3: (7, 2, 0, 4, 6, 5, 1),
        5: (6, 0, 7, 1, 2, 4, 3),
        6: (2, 3, 1, 5, 4, 0, 7),
    },
    {
        2: (5, 6, 7, 1, 0, 4, 3),
        3: (0, 5, 4, 6, 7, 1, 2),
        4: (7, 1, 3, 2, 5, 6, 0),
        5: (3, 4, 2, 0, 1, 7, 6),
        7: (1, 2, 0, 4, 6, 3, 5),
    },
)


def plan(blocks, groups, heads):
    laid_out = []
    for group in range(groups):
        if blocks == 8 and heads == 5:
            laid_out.append(even_rounds[group % 2])
        else:
            owners = [(head * blocks // heads + group % 2) % blocks for head in range(heads)]
            laid_out.append({u: [(u - step) % blocks for step in range(1, blocks)] for u in owners})
    owned = np.full((groups, blocks), -1)
    sent = np.full((blocks, groups, blocks), -1)
    partner = np.full((blocks, groups, blocks), -1)
    pairs = [[] for _ in range(blocks)]
    for group, rounds in enumerate(laid_out):
        for head, (owner, sources) in enumerate(rounds.items()):
            owned[group, owner] = head
            for step, source in enumerate((owner, *sources)):
                sent[step, group, source] = head
                partner[step, group, owner] = source
                pairs[step].append((source * groups + group, owner * groups + group))
    return owned, sent, partner, [sorted(step) for step in pairs]


def looked_up(table, group, block):
    groups, blocks = table.shape
    period = next(p for p in range(1, groups + 1) if (table == table[np.arange(groups) % p]).all())
    bits = int(table.max() + 1).bit_length()
    per_word = 31 // bits
    word = jnp.int32(0)
    for row in range(period):
        for first in range(0, blocks, per_word):
            values = table[row, first : first + per_word] + 1
            packed = sum(int(value) << (bits * n) for n, value in enumerate(values))
            here = (lax.rem(group, period) == row) & (block >= first) & (block < first + per_word)
            word = jnp.where(here, packed, word)
    return ((word >> (bits * lax.rem(block, per_word))) & ((1 << bits) - 1)) - 1


def dot(a, b, contract):
    return lax.dot_general(a, b, (contract, ((), ())), preferred_element_type=jnp.float32)


NN = ((1,), (0,))
NT = ((1,), (1,))


def head_columns(head, width):
    return pl.ds(pl.multiple_of(head * width, width), width)


def pack_kernel(sent, width, query, key, value, grad_out, *refs):
    outs, (staged, packed, in_sems, out_sems) = refs[:-4], refs[-4:]
    group, block = lax.axis_index("head"), lax.axis_index("tm")
    arrays = (query, key, value, grad_out)
    loads = [pltpu.make_async_copy(a, staged.at[n], in_sems.at[n]) for n, a in enumerate(arrays)]
    for load in loads:
        load.start()
    heads = [looked_up(table, group, block) for table in sent]
    stores = [pltpu.make_async_copy(packed.at[n], out, out_sems.at[n]) for n, out in enumerate(outs)]
    for load in loads:
        load.wait()
    for step, head in enumerate(heads):

        @pl.when(head >= 0)
        def _():
            columns = head_columns(head, width)
            for n in range(3):
                packed[step, n] = staged[n, :, columns]
            packed[step, 3] = staged[3, :, columns].T
            stores[step].start()

    for step, head in enumerate(heads):

        @pl.when(head >= 0)
        def _():
            stores[step].wait()


def unpack_kernel(sent, width, *refs):
    parts, (attended, query_grad, key_grad, value_grad) = refs[:-4], refs[-4:]
    group, block = lax.axis_index("head"), lax.axis_index("tm")
    for step, part in enumerate(parts):
        head = looked_up(sent[step], group, block)

        @pl.when(head >= 0)
        def _():
            columns = head_columns(head, width)
            attended[:, columns] = part[0].T
            query_grad[:, columns] = part[1].T
            key_grad[:, columns] = part[2]
            value_grad[:, columns] = part[3]


def head_kernel(owned, partner, rows, frame_ids, sink_frame, window, local, *refs):
    blocks = len(partner)
    parts, outs, scratch = refs[: blocks - 1], refs[blocks - 1 : 2 * blocks - 1], refs[2 * blocks - 1 :]
    (here, q_all, kt_all, vt_all, gt_all, weights, weights_low, grads_low, grad_scaled, dk, dv, res, sem) = scratch
    parts = (here, *parts)
    group, block = lax.axis_index("head"), lax.axis_index("tm")
    head = looked_up(owned, group, block)
    width = q_all.shape[1]
    scaling = 1.0 / math.sqrt(width)
    rescale = scaling * math.log2(math.e)
    stretch = weights.shape[1]
    half = stretch // 2
    each = half // rows

    @pl.when(head >= 0)
    def _():
        fetch = pltpu.make_async_copy(local, here, sem)
        fetch.start()
        span = window[head]
        sink = sink_frame[0]
        frames = [frame_ids[looked_up(table, group, block)] for table in partner]

        def placed(j):
            at = pl.ds(j * rows, rows)
            q_all[at, :] = parts[j][0]
            kt_all[:, at] = parts[j][1].T
            vt_all[:, at] = parts[j][2].T
            gt_all[:, at] = parts[j][3]

        for j in range(1, blocks):
            placed(j)
        fetch.wait()
        placed(0)
        dk[...] = jnp.zeros_like(dk)
        dv[...] = jnp.zeros_like(dv)
        lane_block = lax.broadcasted_iota(jnp.int32, (1, half), 1) // rows

        def one_stretch(i, carry):
            at = [pl.ds(pl.multiple_of(i * stretch + h * half, half), half) for h in range(2)]
            lanes = [pl.ds(h * half, half) for h in range(2)]
            keys = [pl.ds(j * rows, rows) for j in range(blocks)]
            q_rows = [q_all[at[h], :] for h in range(2)]
            top = [jnp.full((1, half), hidden_score, jnp.float32)] * 2
            total = [jnp.zeros((1, half), jnp.float32)] * 2
            delta = [None] * 2
            own = [[], []]
            for h in range(2):
                for k in range(each):
                    n = i * 2 * each + h * each + k
                    own[h].append(sum(jnp.where(n == j, frames[j], 0) for j in range(blocks)))

            def score(h, j):
                bias = jnp.zeros((1, half), jnp.float32)
                for k in range(each):
                    seen = (frames[j] <= own[h][k]) & (frames[j] > own[h][k] - span)
                    seen = seen | ((frames[j] == sink) & (sink <= own[h][k]))
                    bias = jnp.where(lane_block == k, jnp.where(seen, 0.0, hidden_score), bias)
                scores = dot(parts[j][1], q_rows[h], NT) * rescale + bias
                weights[keys[j], lanes[h]] = scores
                top[h] = jnp.maximum(top[h], jnp.max(scores, axis=0, keepdims=True))

            def weigh(h, j):
                p = jnp.exp2(weights[keys[j], lanes[h]] - top[h])
                total[h] = total[h] + jnp.sum(p, axis=0, keepdims=True)
                weights[keys[j], lanes[h]] = p
                weights_low[keys[j], lanes[h]] = p.astype(jnp.bfloat16)

            def attend(h):
                inverse = 1.0 / total[h]
                mixed = (dot(vt_all[...], weights_low[:, lanes[h]], NN) * inverse).astype(jnp.bfloat16)
                grad_t = gt_all[:, at[h]].astype(jnp.float32)
                delta[h] = jnp.sum(grad_t * mixed.astype(jnp.float32), axis=0, keepdims=True) * inverse
                grad_scaled[:, lanes[h]] = (grad_t * inverse).astype(jnp.bfloat16)
                for k in range(each):
                    res[i * 2 * each + h * each + k, 0] = mixed[:, k * rows : (k + 1) * rows]

            def differ(h, j):
                g = dot(parts[j][2], grad_scaled[:, lanes[h]], NN) - delta[h]
                grads_low[keys[j], lanes[h]] = (weights[keys[j], lanes[h]] * g).astype(jnp.bfloat16)

            def query_part(h):
                grad = (dot(kt_all[...], grads_low[:, lanes[h]], NN) * scaling).astype(jnp.bfloat16)
                for k in range(each):
                    res[i * 2 * each + h * each + k, 1] = grad[:, k * rows : (k + 1) * rows]

            for j in range(blocks):
                score(0, j)
            for j in range(blocks):
                score(1, j)
                weigh(0, j)
            attend(0)
            for j in range(blocks):
                weigh(1, j)
                differ(0, j)
            attend(1)
            query_part(0)
            q_both = jnp.concatenate(q_rows, axis=0)
            for j in range(blocks):
                differ(1, j)
                dk[keys[j], :] += dot(grads_low[keys[j], :], q_both, NN)
                dv[keys[j], :] += dot(weights_low[keys[j], :], grad_scaled[...], NT)
            query_part(1)
            return carry

        lax.fori_loop(0, blocks * rows // stretch, one_stretch, 0)
        for j, out in enumerate(outs):
            at = pl.ds(j * rows, rows)
            out[0] = res[j, 0]
            out[1] = res[j, 1]
            out[2] = (dk[at, :] * scaling).astype(jnp.bfloat16)
            out[3] = dv[at, :].astype(jnp.bfloat16)


def seen_bias(frame, own, span, sink):
    seen = ((frame <= own) & (frame > own - span)) | ((frame == sink) & (sink <= own))
    return jnp.where(seen, 0.0, hidden_score)


def frames_by_lane(frames, rows):
    lane_block = lax.broadcasted_iota(jnp.int32, (1, len(frames) * rows), 1) // rows
    row = jnp.zeros_like(lane_block)
    for n, frame in enumerate(frames):
        row = jnp.where(lane_block == n, frame, row)
    return row


def place_block(part, j, rows, q_all, kt_all, vt_all, gt_all):
    at = pl.ds(j * rows, rows)
    q_all[at, :] = part[0]
    kt_all[:, at] = part[1].T
    vt_all[:, at] = part[2].T
    gt_all[:, at] = part[3]


def early_kernel(owned, partner, rows, frame_ids, sink_frame, window, *refs):
    blocks = len(partner)
    early = blocks - 1
    parts, (scores, dots, q_all, kt_all, vt_all, gt_all, local, bias) = refs[:early], refs[early:]
    group, block = lax.axis_index("head"), lax.axis_index("tm")
    head = looked_up(owned, group, block)
    width = q_all.shape[1]
    rescale = math.log2(math.e) / math.sqrt(width)

    @pl.when(head >= 0)
    def _():
        span = window[head]
        sink = sink_frame[0]
        frames = [frame_ids[looked_up(table, group, block)] for table in partner]
        local[0] = parts[0][1]
        local[1] = parts[0][2]
        for j in range(early):
            place_block(parts[j], j, rows, q_all, kt_all, vt_all, gt_all)
        every = frames_by_lane(frames, rows)
        bias[pl.ds(early, 1), :] = seen_bias(frames[early], every, span, sink)
        own = every[:, : early * rows]
        lanes = pl.ds(0, early * rows)
        for j in range(early):
            keys = pl.ds(j * rows, rows)
            product = dot(parts[j][1], q_all[lanes, :], NT) * rescale
            scores[keys, lanes] = product + seen_bias(frames[j], own, span, sink)
            bias[pl.ds(j, 1), :] = jnp.full_like(every, 0.0, jnp.float32) + seen_bias(
                frames[j], frames[early], span, sink
            )
            dots[keys, lanes] = dot(parts[j][2], gt_all[:, lanes], NN)


def late_kernel(owned, blocks, rows, *refs):
    parts, (local, bias), refs = refs[: blocks - 1], refs[blocks - 1 : blocks + 1], refs[blocks + 7 :]
    outs, refs = refs[:blocks], refs[blocks:]
    scores, dots, q_all, kt_all, vt_all, gt_all, weights_low, grads_low, grad_scaled, dk, dv, res = refs
    group, block = lax.axis_index("head"), lax.axis_index("tm")
    head = looked_up(owned, group, block)
    width = q_all.shape[1]
    scaling = 1.0 / math.sqrt(width)
    rescale = scaling * math.log2(math.e)
    stretch = weights_low.shape[1]
    half = stretch // 2
    each = half // rows

    @pl.when(head >= 0)
    def _():
        last = blocks - 1
        newest = parts[-1]
        keys_of = [local.at[0], *(part.at[1] for part in parts)]
        values_of = [local.at[1], *(part.at[2] for part in parts)]
        place_block(newest, last, rows, q_all, kt_all, vt_all, gt_all)
        at_last = pl.ds(last * rows, rows)
        for j in range(last):
            keys = pl.ds(j * rows, rows)
            product = dot(keys_of[j][...], newest[0], NT) * rescale
            scores[keys, at_last] = product + bias[pl.ds(j, 1), pl.ds(0, rows)]
            dots[keys, at_last] = dot(values_of[j][...], newest[3], NN)
        product = dot(newest[1], q_all[...], NT) * rescale
        scores[at_last, :] = product + bias[pl.ds(last, 1), :]
        dots[at_last, :] = dot(newest[2], gt_all[...], NN)

        keys = [pl.ds(j * rows, rows) for j in range(blocks)]

        def one_stretch(i, carry):
            at = [pl.ds(pl.multiple_of(i * stretch + h * half, half), half) for h in range(2)]
            lanes = [pl.ds(h * half, half) for h in range(2)]
            top = [None] * 2
            total = [jnp.zeros((1, half), jnp.float32)] * 2
            inverse = [None] * 2
            delta = [None] * 2

            def highest(h):
                top[h] = jnp.max(scores[:, at[h]], axis=0, keepdims=True)

            def weigh(h, j):
                p = jnp.exp2(scores[keys[j], at[h]] - top[h])
                total[h] = total[h] + jnp.sum(p, axis=0, keepdims=True)
                scores[keys[j], at[h]] = p
                weights_low[keys[j], lanes[h]] = p.astype(jnp.bfloat16)

            def attend(h):
                inverse[h] = 1.0 / total[h]
                mixed = (dot(vt_all[...], weights_low[:, lanes[h]], NN) * inverse[h]).astype(jnp.bfloat16)
                grad_t = gt_all[:, at[h]].astype(jnp.float32)
                delta[h] = jnp.sum(grad_t * mixed.astype(jnp.float32), axis=0, keepdims=True) * inverse[h]
                grad_scaled[:, lanes[h]] = (grad_t * inverse[h]).astype(jnp.bfloat16)
                for k in range(each):
                    res[i * 2 * each + h * each + k, 0] = mixed[:, k * rows : (k + 1) * rows]

            def differ(h, j):
                g = scores[keys[j], at[h]] * (dots[keys[j], at[h]] * inverse[h] - delta[h])
                grads_low[keys[j], lanes[h]] = g.astype(jnp.bfloat16)

            def query_part(h):
                grad = (dot(kt_all[...], grads_low[:, lanes[h]], NN) * scaling).astype(jnp.bfloat16)
                for k in range(each):
                    res[i * 2 * each + h * each + k, 1] = grad[:, k * rows : (k + 1) * rows]

            highest(0)
            highest(1)
            for j in range(blocks):
                weigh(0, j)
            attend(0)
            for j in range(blocks):
                weigh(1, j)
                differ(0, j)
            attend(1)
            query_part(0)
            q_both = q_all[pl.ds(pl.multiple_of(i * stretch, stretch), stretch), :]
            for j in range(blocks):
                differ(1, j)
                dk[keys[j], :] += dot(grads_low[keys[j], :], q_both, NN)
                dv[keys[j], :] += dot(weights_low[keys[j], :], grad_scaled[...], NT)
            query_part(1)
            return carry

        dk[...] = jnp.zeros_like(dk)
        dv[...] = jnp.zeros_like(dv)
        lax.fori_loop(0, blocks * rows // stretch, one_stretch, 0)
        for j, out in enumerate(outs):
            out[0] = res[j, 0]
            out[1] = res[j, 1]
            out[2] = (dk[keys[j], :] * scaling).astype(jnp.bfloat16)
            out[3] = dv[keys[j], :].astype(jnp.bfloat16)


def per_device(query, key, value, grad_out, frame_ids, sink_frame, window):
    rows, row_width = query.shape
    heads = window.shape[0]
    width = row_width // heads
    blocks = lax.axis_size("tm")
    owned, sent, partner, pairs = plan(blocks, lax.axis_size("head"), heads)
    axes = ("tm", "head")
    smem = pl.BlockSpec(memory_space=pltpu.SMEM)
    vmem = pl.BlockSpec(memory_space=pltpu.VMEM)
    in_place = pl.BlockSpec(memory_space=pltpu.HBM)
    part = jax.ShapeDtypeStruct((4, rows, width), query.dtype)
    local = jax.ShapeDtypeStruct(query.shape, query.dtype)

    parts = pl.pallas_call(
        functools.partial(pack_kernel, sent, width),
        out_shape=[part] * blocks,
        in_specs=[in_place] * 4,
        out_specs=[in_place] * blocks,
        scratch_shapes=[
            pltpu.VMEM((4, rows, row_width), query.dtype),
            pltpu.VMEM((blocks, 4, rows, width), query.dtype),
            pltpu.SemaphoreType.DMA((4,)),
            pltpu.SemaphoreType.DMA((blocks,)),
        ],
        compiler_params=pltpu.CompilerParams(vmem_limit_bytes=62 * MIB),
        name="pack",
    )(query, key, value, grad_out)
    parts = [parts[0]] + [lax.ppermute(parts[s], axes, pairs[s]) for s in range(1, blocks)]

    tokens = blocks * rows
    stretch = (4 if blocks % 4 == 0 else 2) * rows
    low, full = query.dtype, jnp.float32
    if tokens <= split_limit:
        kept = [jax.ShapeDtypeStruct((tokens, tokens), full)] * 2
        kept += [jax.ShapeDtypeStruct((tokens, width), low)]
        kept += [jax.ShapeDtypeStruct((width, tokens), low)] * 3
        pairs_early = (blocks - 1) ** 2
        handed = [jax.ShapeDtypeStruct((2, rows, width), low), jax.ShapeDtypeStruct((blocks, tokens), full)]
        *early, here, bias = pl.pallas_call(
            functools.partial(early_kernel, owned, partner, rows),
            out_shape=kept + handed,
            in_specs=[smem] * 3 + [vmem] * (blocks - 1),
            out_specs=[vmem] * 8,
            compiler_params=pltpu.CompilerParams(vmem_limit_bytes=20 * MIB),
            cost_estimate=pl.CostEstimate(
                flops=4 * pairs_early * rows * rows * width, bytes_accessed=8 * tokens * tokens, transcendentals=0
            ),
            name="early_products",
        )(frame_ids, sink_frame, window, *parts[:-1])
        results = pl.pallas_call(
            functools.partial(late_kernel, owned, blocks, rows),
            out_shape=[part] * blocks + kept,
            in_specs=[vmem] * (blocks + 7),
            out_specs=[vmem] * (blocks + 6),
            input_output_aliases={blocks + 1 + n: blocks + n for n in range(6)},
            scratch_shapes=[
                pltpu.VMEM((tokens, stretch), low),
                pltpu.VMEM((tokens, stretch), low),
                pltpu.VMEM((width, stretch), low),
                pltpu.VMEM((tokens, width), full),
                pltpu.VMEM((tokens, width), full),
                pltpu.VMEM((blocks, 2, width, rows), low),
            ],
            compiler_params=pltpu.CompilerParams(vmem_limit_bytes=32 * MIB),
            name="head_attention",
        )(*parts[1:], here, bias, *early)
        parts = results[:blocks]
    else:
        parts = pl.pallas_call(
            functools.partial(head_kernel, owned, partner, rows),
            out_shape=[part] * blocks,
            in_specs=[smem] * 3 + [pl.BlockSpec(memory_space=pl.ANY)] + [vmem] * (blocks - 1),
            out_specs=[vmem] * blocks,
            scratch_shapes=[
                pltpu.VMEM((4, rows, width), low),
                pltpu.VMEM((tokens, width), low),
                pltpu.VMEM((width, tokens), low),
                pltpu.VMEM((width, tokens), low),
                pltpu.VMEM((width, tokens), low),
                pltpu.VMEM((tokens, stretch), full),
                pltpu.VMEM((tokens, stretch), low),
                pltpu.VMEM((tokens, stretch), low),
                pltpu.VMEM((width, stretch), low),
                pltpu.VMEM((tokens, width), full),
                pltpu.VMEM((tokens, width), full),
                pltpu.VMEM((blocks, 2, width, rows), low),
                pltpu.SemaphoreType.DMA,
            ],
            compiler_params=pltpu.CompilerParams(vmem_limit_bytes=48 * MIB),
            name="head_attention",
        )(frame_ids, sink_frame, window, *parts)
    back = [[(owner, source) for source, owner in step] for step in pairs]
    parts = [parts[0]] + [lax.ppermute(parts[s], axes, back[s]) for s in range(1, blocks)]

    return pl.pallas_call(
        functools.partial(unpack_kernel, sent, width),
        out_shape=[local] * 4,
        in_specs=[vmem] * blocks,
        out_specs=[vmem] * 4,
        compiler_params=pltpu.CompilerParams(vmem_limit_bytes=24 * MIB),
        name="unpack",
    )(*parts)


def solution(mesh):
    spec = P("tm", "head")
    return jax.shard_map(
        per_device,
        mesh=mesh,
        in_specs=(spec, spec, spec, spec, P(), P(), P("head")),
        out_specs=(spec, spec, spec, spec),
        check_vma=False,
    )
```

```python
import functools
import math

import jax
import jax.numpy as jnp
import numpy as np
from jax import lax
from jax.experimental import pallas as pl
from jax.experimental.pallas import tpu as pltpu
from jax.sharding import PartitionSpec as P

hidden_score = -1e30
MIB = 1 << 20
split_limit = 1024


even_rounds = (
    {
        0: (3, 6, 5, 7, 1, 2, 4),
        1: (4, 7, 6, 2, 0, 3, 5),
        3: (7, 2, 0, 4, 6, 5, 1),
        5: (6, 0, 7, 1, 2, 4, 3),
        6: (2, 3, 1, 5, 4, 0, 7),
    },
    {
        2: (5, 6, 7, 1, 0, 4, 3),
        3: (0, 5, 4, 6, 7, 1, 2),
        4: (7, 1, 3, 2, 5, 6, 0),
        5: (3, 4, 2, 0, 1, 7, 6),
        7: (1, 2, 0, 4, 6, 3, 5),
    },
)


def plan(blocks, groups, heads):
    laid_out = []
    for group in range(groups):
        if blocks == 8 and heads == 5:
            laid_out.append(even_rounds[group % 2])
        else:
            owners = [(head * blocks // heads + group % 2) % blocks for head in range(heads)]
            laid_out.append({u: [(u - step) % blocks for step in range(1, blocks)] for u in owners})
    owned = np.full((groups, blocks), -1)
    sent = np.full((blocks, groups, blocks), -1)
    partner = np.full((blocks, groups, blocks), -1)
    pairs = [[] for _ in range(blocks)]
    for group, rounds in enumerate(laid_out):
        for head, (owner, sources) in enumerate(rounds.items()):
            owned[group, owner] = head
            for step, source in enumerate((owner, *sources)):
                sent[step, group, source] = head
                partner[step, group, owner] = source
                pairs[step].append((source * groups + group, owner * groups + group))
    return owned, sent, partner, [sorted(step) for step in pairs]


def looked_up(table, group, block):
    groups, blocks = table.shape
    period = next(p for p in range(1, groups + 1) if (table == table[np.arange(groups) % p]).all())
    bits = int(table.max() + 1).bit_length()
    per_word = 31 // bits
    word = jnp.int32(0)
    for row in range(period):
        for first in range(0, blocks, per_word):
            values = table[row, first : first + per_word] + 1
            packed = sum(int(value) << (bits * n) for n, value in enumerate(values))
            here = (lax.rem(group, period) == row) & (block >= first) & (block < first + per_word)
            word = jnp.where(here, packed, word)
    return ((word >> (bits * lax.rem(block, per_word))) & ((1 << bits) - 1)) - 1


def dot(a, b, contract):
    return lax.dot_general(a, b, (contract, ((), ())), preferred_element_type=jnp.float32)


NN = ((1,), (0,))
NT = ((1,), (1,))


def head_columns(head, width):
    return pl.ds(pl.multiple_of(head * width, width), width)


def pack_kernel(sent, width, query, key, value, grad_out, *refs):
    outs, (staged, packed, in_sems, out_sems) = refs[:-4], refs[-4:]
    group, block = lax.axis_index("head"), lax.axis_index("tm")
    arrays = (query, key, value, grad_out)
    loads = [pltpu.make_async_copy(a, staged.at[n], in_sems.at[n]) for n, a in enumerate(arrays)]
    for load in loads:
        load.start()
    heads = [looked_up(table, group, block) for table in sent]
    stores = [pltpu.make_async_copy(packed.at[n], out, out_sems.at[n]) for n, out in enumerate(outs)]
    for load in loads:
        load.wait()
    for step, head in enumerate(heads):

        @pl.when(head >= 0)
        def _():
            columns = head_columns(head, width)
            for n in range(3):
                packed[step, n] = staged[n, :, columns]
            packed[step, 3] = staged[3, :, columns].T
            stores[step].start()

    for step, head in enumerate(heads):

        @pl.when(head >= 0)
        def _():
            stores[step].wait()


def unpack_kernel(sent, width, *refs):
    parts, (attended, query_grad, key_grad, value_grad) = refs[:-4], refs[-4:]
    group, block = lax.axis_index("head"), lax.axis_index("tm")
    for step, part in enumerate(parts):
        head = looked_up(sent[step], group, block)

        @pl.when(head >= 0)
        def _():
            columns = head_columns(head, width)
            attended[:, columns] = part[0].T
            query_grad[:, columns] = part[1].T
            key_grad[:, columns] = part[2]
            value_grad[:, columns] = part[3]


def head_kernel(owned, partner, rows, frame_ids, sink_frame, window, local, *refs):
    blocks = len(partner)
    parts, outs, scratch = refs[: blocks - 1], refs[blocks - 1 : 2 * blocks - 1], refs[2 * blocks - 1 :]
    (here, q_all, kt_all, vt_all, gt_all, weights, weights_low, grads_low, grad_scaled, dk, dv, res, sem) = scratch
    parts = (here, *parts)
    group, block = lax.axis_index("head"), lax.axis_index("tm")
    head = looked_up(owned, group, block)
    width = q_all.shape[1]
    scaling = 1.0 / math.sqrt(width)
    rescale = scaling * math.log2(math.e)
    stretch = weights.shape[1]
    half = stretch // 2
    each = half // rows

    @pl.when(head >= 0)
    def _():
        fetch = pltpu.make_async_copy(local, here, sem)
        fetch.start()
        span = window[head]
        sink = sink_frame[0]
        frames = [frame_ids[looked_up(table, group, block)] for table in partner]

        def placed(j):
            at = pl.ds(j * rows, rows)
            q_all[at, :] = parts[j][0]
            kt_all[:, at] = parts[j][1].T
            vt_all[:, at] = parts[j][2].T
            gt_all[:, at] = parts[j][3]

        for j in range(1, blocks):
            placed(j)
        fetch.wait()
        placed(0)
        dk[...] = jnp.zeros_like(dk)
        dv[...] = jnp.zeros_like(dv)
        lane_block = lax.broadcasted_iota(jnp.int32, (1, half), 1) // rows

        def one_stretch(i, carry):
            at = [pl.ds(pl.multiple_of(i * stretch + h * half, half), half) for h in range(2)]
            lanes = [pl.ds(h * half, half) for h in range(2)]
            keys = [pl.ds(j * rows, rows) for j in range(blocks)]
            q_rows = [q_all[at[h], :] for h in range(2)]
            top = [jnp.full((1, half), hidden_score, jnp.float32)] * 2
            total = [jnp.zeros((1, half), jnp.float32)] * 2
            delta = [None] * 2
            own = [[], []]
            for h in range(2):
                for k in range(each):
                    n = i * 2 * each + h * each + k
                    own[h].append(sum(jnp.where(n == j, frames[j], 0) for j in range(blocks)))

            def score(h, j):
                bias = jnp.zeros((1, half), jnp.float32)
                for k in range(each):
                    seen = (frames[j] <= own[h][k]) & (frames[j] > own[h][k] - span)
                    seen = seen | ((frames[j] == sink) & (sink <= own[h][k]))
                    bias = jnp.where(lane_block == k, jnp.where(seen, 0.0, hidden_score), bias)
                scores = dot(parts[j][1], q_rows[h], NT) * rescale + bias
                weights[keys[j], lanes[h]] = scores
                top[h] = jnp.maximum(top[h], jnp.max(scores, axis=0, keepdims=True))

            def weigh(h, j):
                p = jnp.exp2(weights[keys[j], lanes[h]] - top[h])
                total[h] = total[h] + jnp.sum(p, axis=0, keepdims=True)
                weights[keys[j], lanes[h]] = p
                weights_low[keys[j], lanes[h]] = p.astype(jnp.bfloat16)

            def attend(h):
                inverse = 1.0 / total[h]
                mixed = (dot(vt_all[...], weights_low[:, lanes[h]], NN) * inverse).astype(jnp.bfloat16)
                grad_t = gt_all[:, at[h]].astype(jnp.float32)
                delta[h] = jnp.sum(grad_t * mixed.astype(jnp.float32), axis=0, keepdims=True) * inverse
                grad_scaled[:, lanes[h]] = (grad_t * inverse).astype(jnp.bfloat16)
                for k in range(each):
                    res[i * 2 * each + h * each + k, 0] = mixed[:, k * rows : (k + 1) * rows]

            def differ(h, j):
                g = dot(parts[j][2], grad_scaled[:, lanes[h]], NN) - delta[h]
                grads_low[keys[j], lanes[h]] = (weights[keys[j], lanes[h]] * g).astype(jnp.bfloat16)

            def query_part(h):
                grad = (dot(kt_all[...], grads_low[:, lanes[h]], NN) * scaling).astype(jnp.bfloat16)
                for k in range(each):
                    res[i * 2 * each + h * each + k, 1] = grad[:, k * rows : (k + 1) * rows]

            for j in range(blocks):
                score(0, j)
            for j in range(blocks):
                score(1, j)
                weigh(0, j)
            attend(0)
            for j in range(blocks):
                weigh(1, j)
                differ(0, j)
            attend(1)
            query_part(0)
            q_both = jnp.concatenate(q_rows, axis=0)
            for j in range(blocks):
                differ(1, j)
                dk[keys[j], :] += dot(grads_low[keys[j], :], q_both, NN)
                dv[keys[j], :] += dot(weights_low[keys[j], :], grad_scaled[...], NT)
            query_part(1)
            return carry

        lax.fori_loop(0, blocks * rows // stretch, one_stretch, 0)
        for j, out in enumerate(outs):
            at = pl.ds(j * rows, rows)
            out[0] = res[j, 0]
            out[1] = res[j, 1]
            out[2] = (dk[at, :] * scaling).astype(jnp.bfloat16)
            out[3] = dv[at, :].astype(jnp.bfloat16)


def seen_bias(frame, own, span, sink):
    seen = ((frame <= own) & (frame > own - span)) | ((frame == sink) & (sink <= own))
    return jnp.where(seen, 0.0, hidden_score)


def frames_by_lane(frames, rows):
    lane_block = lax.broadcasted_iota(jnp.int32, (1, len(frames) * rows), 1) // rows
    row = jnp.zeros_like(lane_block)
    for n, frame in enumerate(frames):
        row = jnp.where(lane_block == n, frame, row)
    return row


def place_block(part, j, rows, q_all, k_all, v_all, kt_all, vt_all, gt_all):
    at = pl.ds(j * rows, rows)
    q_all[at, :] = part[0]
    k_all[at, :] = part[1]
    v_all[at, :] = part[2]
    kt_all[:, at] = part[1].T
    vt_all[:, at] = part[2].T
    gt_all[:, at] = part[3]


def pair_products(j, held, rows, bias, scores, dots, q_all, k_all, v_all, gt_all):
    width = q_all.shape[1]
    rescale = math.log2(math.e) / math.sqrt(width)
    before = held * rows
    at = pl.ds(j * rows, rows)
    every = pl.ds(0, before + rows)
    scores[at, every] = dot(k_all[at, :], q_all[every, :], NT) * rescale + bias[pl.ds(j, 1), every]
    dots[at, every] = dot(v_all[at, :], gt_all[:, every], NN)
    column = dot(k_all[pl.ds(0, before), :], q_all[at, :], NT) * rescale
    for n in range(held):
        keys = pl.ds(n * rows, rows)
        scores[keys, at] = column[n * rows : (n + 1) * rows, :] + bias[pl.ds(n, 1), at]
    dots[pl.ds(0, before), at] = dot(v_all[pl.ds(0, before), :], gt_all[:, at], NN)


def lane_chunks(start, stop, size):
    return [pl.ds(first, min(size, stop - first)) for first in range(start, stop, size)]


def products_kernel(owned, partner, rows, frame_ids, sink_frame, window, *refs):
    blocks = len(partner)
    held = blocks - 2
    parts, (bias, scores, dots, *places) = refs[:held], refs[held:]
    group, block = lax.axis_index("head"), lax.axis_index("tm")
    head = looked_up(owned, group, block)

    @pl.when(head >= 0)
    def _():
        span = window[head]
        sink = sink_frame[0]
        frames = [frame_ids[looked_up(table, group, block)] for table in partner]
        every = frames_by_lane(frames, rows)
        for j in range(blocks):
            bias[pl.ds(j, 1), :] = seen_bias(frames[j], every, span, sink)
        for j in range(held):
            place_block(parts[j], j, rows, *places)
        q_all, k_all, v_all, _, _, gt_all = places
        lanes = pl.ds(0, held * rows)
        rescale = math.log2(math.e) / math.sqrt(q_all.shape[1])
        for j in range(held):
            keys = pl.ds(j * rows, rows)
            scores[keys, lanes] = dot(parts[j][1], q_all[lanes, :], NT) * rescale + bias[pl.ds(j, 1), lanes]
            dots[keys, lanes] = dot(parts[j][2], gt_all[:, lanes], NN)


def softmax_kernel(owned, blocks, rows, bias, *refs):
    part, refs = refs[0], refs[9:]
    scores, dots, q_all, k_all, v_all, kt_all, vt_all, gt_all, low, stats, mixed = refs
    head = looked_up(owned, lax.axis_index("head"), lax.axis_index("tm"))

    @pl.when(head >= 0)
    def _():
        newest = blocks - 2
        held = pl.ds(0, (newest + 1) * rows)
        place_block(part, newest, rows, q_all, k_all, v_all, kt_all, vt_all, gt_all)
        pair_products(newest, newest, rows, bias, scores, dots, q_all, k_all, v_all, gt_all)
        for lanes in lane_chunks(0, (newest + 1) * rows, 2 * rows):
            top = jnp.max(scores[held, lanes], axis=0, keepdims=True)
            total = jnp.zeros_like(top)
            for j in range(newest + 1):
                keys = pl.ds(j * rows, rows)
                p = jnp.exp2(scores[keys, lanes] - top)
                total = total + jnp.sum(p, axis=0, keepdims=True)
                scores[keys, lanes] = p
                low[keys, lanes] = p.astype(jnp.bfloat16)
            stats[pl.ds(0, 1), lanes] = top
            stats[pl.ds(1, 1), lanes] = total
            mixed[:, lanes] = dot(vt_all[:, held], low[held, lanes], NN)


def finish_kernel(owned, blocks, rows, bias, stats, mixed, *refs):
    part, refs = refs[0], refs[10:]
    outs, refs = refs[:blocks], refs[blocks:]
    scores, dots, q_all, k_all, v_all, kt_all, vt_all, gt_all, low, grads_low, old_scaled, new_scaled, factors = refs
    head = looked_up(owned, lax.axis_index("head"), lax.axis_index("tm"))
    width = q_all.shape[1]
    scaling = 1.0 / math.sqrt(width)

    @pl.when(head >= 0)
    def _():
        newest = blocks - 1
        at = pl.ds(newest * rows, rows)
        place_block(part, newest, rows, q_all, k_all, v_all, kt_all, vt_all, gt_all)
        pair_products(newest, newest, rows, bias, scores, dots, q_all, k_all, v_all, gt_all)

        def settle(lanes, total, old_factor, weighted):
            inverse = 1.0 / total
            attended = (weighted * inverse).astype(jnp.bfloat16)
            grad_t = gt_all[:, lanes].astype(jnp.float32)
            delta = jnp.sum(grad_t * attended.astype(jnp.float32), axis=0, keepdims=True)
            old = inverse * old_factor
            old_scaled[:, lanes] = (grad_t * old).astype(jnp.bfloat16)
            new_scaled[:, lanes] = (grad_t * inverse).astype(jnp.bfloat16)
            factors[pl.ds(0, 1), lanes] = old
            factors[pl.ds(1, 1), lanes] = delta * old
            factors[pl.ds(2, 1), lanes] = inverse
            factors[pl.ds(3, 1), lanes] = delta * inverse
            for k in range(lanes.size // rows):
                outs[lanes.start // rows + k][0] = attended[:, k * rows : (k + 1) * rows]

        for lanes in lane_chunks(0, newest * rows, 2 * rows):
            fresh = scores[at, lanes]
            before = stats[pl.ds(0, 1), lanes]
            top = jnp.maximum(before, jnp.max(fresh, axis=0, keepdims=True))
            correction = jnp.exp2(before - top)
            p = jnp.exp2(fresh - top)
            p_low = p.astype(jnp.bfloat16)
            scores[at, lanes] = p
            low[at, lanes] = p_low
            total = stats[pl.ds(1, 1), lanes] * correction + jnp.sum(p, axis=0, keepdims=True)
            weighted = mixed[:, lanes] * correction + dot(vt_all[:, at], p_low, NN)
            settle(lanes, total, correction, weighted)
        column = scores[:, at]
        p = jnp.exp2(column - jnp.max(column, axis=0, keepdims=True))
        p_low = p.astype(jnp.bfloat16)
        scores[:, at] = p
        low[:, at] = p_low
        settle(at, jnp.sum(p, axis=0, keepdims=True), 1.0, dot(vt_all[...], p_low, NN))

        for j, out in enumerate(outs):
            keys = pl.ds(j * rows, rows)
            row = 0 if j < newest else 2
            scaled = old_scaled if j < newest else new_scaled
            for lanes in lane_chunks(0, blocks * rows, 4 * rows):
                g = dots[keys, lanes] * factors[pl.ds(row, 1), lanes] - factors[pl.ds(row + 1, 1), lanes]
                grads_low[keys, lanes] = (scores[keys, lanes] * g).astype(jnp.bfloat16)
            out[2] = (dot(grads_low[keys, :], q_all[...], NN) * scaling).astype(jnp.bfloat16)
            out[3] = dot(low[keys, :], scaled[...], NT).astype(jnp.bfloat16)
        for lanes in lane_chunks(0, blocks * rows, 2 * rows):
            grad = (dot(kt_all[...], grads_low[:, lanes], NN) * scaling).astype(jnp.bfloat16)
            for k in range(lanes.size // rows):
                outs[lanes.start // rows + k][1] = grad[:, k * rows : (k + 1) * rows]


def per_device(query, key, value, grad_out, frame_ids, sink_frame, window):
    rows, row_width = query.shape
    heads = window.shape[0]
    width = row_width // heads
    blocks = lax.axis_size("tm")
    owned, sent, partner, pairs = plan(blocks, lax.axis_size("head"), heads)
    axes = ("tm", "head")
    smem = pl.BlockSpec(memory_space=pltpu.SMEM)
    vmem = pl.BlockSpec(memory_space=pltpu.VMEM)
    in_place = pl.BlockSpec(memory_space=pltpu.HBM)
    part = jax.ShapeDtypeStruct((4, rows, width), query.dtype)
    local = jax.ShapeDtypeStruct(query.shape, query.dtype)

    parts = pl.pallas_call(
        functools.partial(pack_kernel, sent, width),
        out_shape=[part] * blocks,
        in_specs=[in_place] * 4,
        out_specs=[in_place] * blocks,
        scratch_shapes=[
            pltpu.VMEM((4, rows, row_width), query.dtype),
            pltpu.VMEM((blocks, 4, rows, width), query.dtype),
            pltpu.SemaphoreType.DMA((4,)),
            pltpu.SemaphoreType.DMA((blocks,)),
        ],
        compiler_params=pltpu.CompilerParams(vmem_limit_bytes=62 * MIB),
        name="pack",
    )(query, key, value, grad_out)
    parts = [parts[0]] + [lax.ppermute(parts[s], axes, pairs[s]) for s in range(1, blocks)]

    tokens = blocks * rows
    stretch = (4 if blocks % 4 == 0 else 2) * rows
    low, full = query.dtype, jnp.float32
    if tokens <= split_limit:
        square = jax.ShapeDtypeStruct((tokens, tokens), full)
        tall = jax.ShapeDtypeStruct((tokens, width), low)
        wide = jax.ShapeDtypeStruct((width, tokens), low)
        table = jax.ShapeDtypeStruct((blocks, tokens), full)
        held = [square] * 2 + [tall] * 3 + [wide] * 3
        flops = 2 * rows * rows * width
        bias, *state = pl.pallas_call(
            functools.partial(products_kernel, owned, partner, rows),
            out_shape=[table, *held],
            in_specs=[smem] * 3 + [vmem] * (blocks - 2),
            out_specs=[vmem] * 9,
            compiler_params=pltpu.CompilerParams(vmem_limit_bytes=20 * MIB),
            cost_estimate=pl.CostEstimate(
                flops=2 * flops * (blocks - 2) ** 2, bytes_accessed=8 * tokens * tokens, transcendentals=0
            ),
            name="products",
        )(frame_ids, sink_frame, window, *parts[:-2])
        *state, weights_low, stats, mixed = pl.pallas_call(
            functools.partial(softmax_kernel, owned, blocks, rows),
            out_shape=[
                *held,
                jax.ShapeDtypeStruct((tokens, tokens), low),
                table,
                jax.ShapeDtypeStruct((width, tokens), full),
            ],
            in_specs=[vmem] * 10,
            out_specs=[vmem] * 11,
            input_output_aliases={2 + n: n for n in range(8)},
            compiler_params=pltpu.CompilerParams(vmem_limit_bytes=20 * MIB),
            cost_estimate=pl.CostEstimate(
                flops=3 * flops * blocks**2, bytes_accessed=8 * tokens * tokens, transcendentals=tokens * tokens
            ),
            name="softmax",
        )(bias, parts[-2], *state)
        parts = pl.pallas_call(
            functools.partial(finish_kernel, owned, blocks, rows),
            out_shape=[part] * blocks + held + [jax.ShapeDtypeStruct((tokens, tokens), low)],
            in_specs=[vmem] * 13,
            out_specs=[vmem] * (blocks + 9),
            input_output_aliases={4 + n: blocks + n for n in range(9)},
            scratch_shapes=[
                pltpu.VMEM((tokens, tokens), low),
                pltpu.VMEM((width, tokens), low),
                pltpu.VMEM((width, tokens), low),
                pltpu.VMEM((8, tokens), full),
            ],
            compiler_params=pltpu.CompilerParams(vmem_limit_bytes=24 * MIB),
            name="finish",
        )(bias, stats, mixed, parts[-1], *state, weights_low)[:blocks]
    else:
        parts = pl.pallas_call(
            functools.partial(head_kernel, owned, partner, rows),
            out_shape=[part] * blocks,
            in_specs=[smem] * 3 + [pl.BlockSpec(memory_space=pl.ANY)] + [vmem] * (blocks - 1),
            out_specs=[vmem] * blocks,
            scratch_shapes=[
                pltpu.VMEM((4, rows, width), low),
                pltpu.VMEM((tokens, width), low),
                pltpu.VMEM((width, tokens), low),
                pltpu.VMEM((width, tokens), low),
                pltpu.VMEM((width, tokens), low),
                pltpu.VMEM((tokens, stretch), full),
                pltpu.VMEM((tokens, stretch), low),
                pltpu.VMEM((tokens, stretch), low),
                pltpu.VMEM((width, stretch), low),
                pltpu.VMEM((tokens, width), full),
                pltpu.VMEM((tokens, width), full),
                pltpu.VMEM((blocks, 2, width, rows), low),
                pltpu.SemaphoreType.DMA,
            ],
            compiler_params=pltpu.CompilerParams(vmem_limit_bytes=48 * MIB),
            name="head_attention",
        )(frame_ids, sink_frame, window, *parts)
    back = [[(owner, source) for source, owner in step] for step in pairs]
    parts = [parts[0]] + [lax.ppermute(parts[s], axes, back[s]) for s in range(1, blocks)]

    return pl.pallas_call(
        functools.partial(unpack_kernel, sent, width),
        out_shape=[local] * 4,
        in_specs=[vmem] * blocks,
        out_specs=[vmem] * 4,
        compiler_params=pltpu.CompilerParams(vmem_limit_bytes=24 * MIB),
        name="unpack",
    )(*parts)


def solution(mesh):
    spec = P("tm", "head")
    return jax.shard_map(
        per_device,
        mesh=mesh,
        in_specs=(spec, spec, spec, spec, P(), P(), P("head")),
        out_specs=(spec, spec, spec, spec),
        check_vma=False,
    )
```

```python
import functools
import math

import jax
import jax.numpy as jnp
import numpy as np
from jax import lax
from jax.experimental import pallas as pl
from jax.experimental.pallas import tpu as pltpu
from jax.sharding import PartitionSpec as P

hidden_score = -1e30
MIB = 1 << 20
vmem_bytes = 64 * MIB
split_limit = 1024


even_rounds = (
    {
        0: (3, 6, 5, 7, 1, 2, 4),
        1: (4, 7, 6, 2, 0, 3, 5),
        3: (7, 2, 0, 4, 6, 5, 1),
        5: (6, 0, 7, 1, 2, 4, 3),
        6: (2, 3, 1, 5, 4, 0, 7),
    },
    {
        2: (5, 6, 7, 1, 0, 4, 3),
        3: (0, 5, 4, 6, 7, 1, 2),
        4: (7, 1, 3, 2, 5, 6, 0),
        5: (3, 4, 2, 0, 1, 7, 6),
        7: (1, 2, 0, 4, 6, 3, 5),
    },
)


def plan(blocks, groups, heads):
    laid_out = []
    for group in range(groups):
        if blocks == 8 and heads == 5:
            laid_out.append(even_rounds[group % 2])
        else:
            owners = [(head * blocks // heads + group % 2) % blocks for head in range(heads)]
            laid_out.append({u: [(u - step) % blocks for step in range(1, blocks)] for u in owners})
    owned = np.full((groups, blocks), -1)
    sent = np.full((blocks, groups, blocks), -1)
    partner = np.full((blocks, groups, blocks), -1)
    pairs = [[] for _ in range(blocks)]
    for group, rounds in enumerate(laid_out):
        for head, (owner, sources) in enumerate(rounds.items()):
            owned[group, owner] = head
            for step, source in enumerate((owner, *sources)):
                sent[step, group, source] = head
                partner[step, group, owner] = source
                pairs[step].append((source * groups + group, owner * groups + group))
    return owned, sent, partner, [sorted(step) for step in pairs]


def looked_up(table, group, block):
    groups, blocks = table.shape
    period = next(p for p in range(1, groups + 1) if (table == table[np.arange(groups) % p]).all())
    bits = int(table.max() + 1).bit_length()
    per_word = 31 // bits
    word = jnp.int32(0)
    for row in range(period):
        for first in range(0, blocks, per_word):
            values = table[row, first : first + per_word] + 1
            packed = sum(int(value) << (bits * n) for n, value in enumerate(values))
            here = (lax.rem(group, period) == row) & (block >= first) & (block < first + per_word)
            word = jnp.where(here, packed, word)
    return ((word >> (bits * lax.rem(block, per_word))) & ((1 << bits) - 1)) - 1


def dot(a, b, contract):
    return lax.dot_general(a, b, (contract, ((), ())), preferred_element_type=jnp.float32)


NN = ((1,), (0,))
NT = ((1,), (1,))


def head_columns(head, width):
    return pl.ds(pl.multiple_of(head * width, width), width)


def pack_kernel(owned, partner, sent, width, query, key, value, grad_out, frame_ids, sink_frame, window, *refs):
    blocks = len(sent)
    home, outs, refs = refs[0], refs[1:blocks], refs[blocks:]
    staged, tiles, packed, frames_here, sink_here, window_here, in_sems, out_sems = refs
    group, block = lax.axis_index("head"), lax.axis_index("tm")
    arrays = (query, key, value, grad_out)
    loads = [pltpu.make_async_copy(a, staged.at[n], in_sems.at[n]) for n, a in enumerate(arrays)]
    small = ((frame_ids, frames_here), (sink_frame, sink_here), (window, window_here))
    loads += [pltpu.make_async_copy(a, here, in_sems.at[4 + n]) for n, (a, here) in enumerate(small)]
    for load in loads:
        load.start()
    heads = [looked_up(table, group, block) for table in sent]
    stores = [pltpu.make_async_copy(packed.at[n], out, out_sems.at[1 + n]) for n, out in enumerate(outs)]
    keep = pltpu.make_async_copy(tiles, home.at[pl.ds(0, tiles.shape[0])], out_sems.at[0])
    for load in loads:
        load.wait()

    def fill(target, head):
        columns = head_columns(head, width)
        for n in range(3):
            target[n] = staged[n, :, columns]
        target[3] = staged[3, :, columns].T

    for step, head in enumerate(heads[1:]):

        @pl.when(head >= 0)
        def _():
            fill(packed.at[step], head)
            stores[step].start()

    @pl.when(heads[0] >= 0)
    def _():
        fill(tiles, heads[0])
        if tiles.shape[0] > 4:
            frames = [frames_here[looked_up(table, group, block)] for table in partner]
            row = lax.broadcasted_iota(jnp.int32, tiles.shape[1:], 0)
            theirs, own = jnp.zeros_like(row), jnp.zeros_like(row)
            for n, frame in enumerate(frames):
                theirs = jnp.where(row // blocks == n, frame, theirs)
                own = jnp.where(lax.rem(row, blocks) == n, frame, own)
            tiles[4] = seen_bias(theirs, own, window_here[heads[0]], sink_here[0]).astype(tiles.dtype)
        keep.start()

    for step, head in enumerate(heads[1:]):

        @pl.when(head >= 0)
        def _():
            stores[step].wait()

    @pl.when(heads[0] >= 0)
    def _():
        keep.wait()


def unpack_kernel(sent, width, *refs):
    parts, (attended, query_grad, key_grad, value_grad) = refs[:-4], refs[-4:]
    group, block = lax.axis_index("head"), lax.axis_index("tm")
    for step, part in enumerate(parts):
        head = looked_up(sent[step], group, block)

        @pl.when(head >= 0)
        def _():
            columns = head_columns(head, width)
            attended[:, columns] = part[0].T
            query_grad[:, columns] = part[1].T
            key_grad[:, columns] = part[2]
            value_grad[:, columns] = part[3]


def head_kernel(owned, partner, rows, frame_ids, sink_frame, window, local, *refs):
    blocks = len(partner)
    parts, outs, scratch = refs[: blocks - 1], refs[blocks - 1 : 2 * blocks - 1], refs[2 * blocks - 1 :]
    (here, q_all, kt_all, vt_all, gt_all, weights, weights_low, grads_low, grad_scaled, dk, dv, res, sem) = scratch
    parts = (here, *parts)
    group, block = lax.axis_index("head"), lax.axis_index("tm")
    head = looked_up(owned, group, block)
    width = q_all.shape[1]
    scaling = 1.0 / math.sqrt(width)
    rescale = scaling * math.log2(math.e)
    stretch = weights.shape[1]
    half = stretch // 2
    each = half // rows

    @pl.when(head >= 0)
    def _():
        fetch = pltpu.make_async_copy(local.at[pl.ds(0, 4)], here, sem)
        fetch.start()
        span = window[head]
        sink = sink_frame[0]
        frames = [frame_ids[looked_up(table, group, block)] for table in partner]

        def placed(j):
            at = pl.ds(j * rows, rows)
            q_all[at, :] = parts[j][0]
            kt_all[:, at] = parts[j][1].T
            vt_all[:, at] = parts[j][2].T
            gt_all[:, at] = parts[j][3]

        for j in range(1, blocks):
            placed(j)
        fetch.wait()
        placed(0)
        dk[...] = jnp.zeros_like(dk)
        dv[...] = jnp.zeros_like(dv)
        lane_block = lax.broadcasted_iota(jnp.int32, (1, half), 1) // rows

        def one_stretch(i, carry):
            at = [pl.ds(pl.multiple_of(i * stretch + h * half, half), half) for h in range(2)]
            lanes = [pl.ds(h * half, half) for h in range(2)]
            keys = [pl.ds(j * rows, rows) for j in range(blocks)]
            q_rows = [q_all[at[h], :] for h in range(2)]
            top = [jnp.full((1, half), hidden_score, jnp.float32)] * 2
            total = [jnp.zeros((1, half), jnp.float32)] * 2
            delta = [None] * 2
            own = [[], []]
            for h in range(2):
                for k in range(each):
                    n = i * 2 * each + h * each + k
                    own[h].append(sum(jnp.where(n == j, frames[j], 0) for j in range(blocks)))

            def score(h, j):
                bias = jnp.zeros((1, half), jnp.float32)
                for k in range(each):
                    seen = (frames[j] <= own[h][k]) & (frames[j] > own[h][k] - span)
                    seen = seen | ((frames[j] == sink) & (sink <= own[h][k]))
                    bias = jnp.where(lane_block == k, jnp.where(seen, 0.0, hidden_score), bias)
                scores = dot(parts[j][1], q_rows[h], NT) * rescale + bias
                weights[keys[j], lanes[h]] = scores
                top[h] = jnp.maximum(top[h], jnp.max(scores, axis=0, keepdims=True))

            def weigh(h, j):
                p = jnp.exp2(weights[keys[j], lanes[h]] - top[h])
                total[h] = total[h] + jnp.sum(p, axis=0, keepdims=True)
                weights[keys[j], lanes[h]] = p
                weights_low[keys[j], lanes[h]] = p.astype(jnp.bfloat16)

            def attend(h):
                inverse = 1.0 / total[h]
                mixed = (dot(vt_all[...], weights_low[:, lanes[h]], NN) * inverse).astype(jnp.bfloat16)
                grad_t = gt_all[:, at[h]].astype(jnp.float32)
                delta[h] = jnp.sum(grad_t * mixed.astype(jnp.float32), axis=0, keepdims=True) * inverse
                grad_scaled[:, lanes[h]] = (grad_t * inverse).astype(jnp.bfloat16)
                for k in range(each):
                    res[i * 2 * each + h * each + k, 0] = mixed[:, k * rows : (k + 1) * rows]

            def differ(h, j):
                g = dot(parts[j][2], grad_scaled[:, lanes[h]], NN) - delta[h]
                grads_low[keys[j], lanes[h]] = (weights[keys[j], lanes[h]] * g).astype(jnp.bfloat16)

            def query_part(h):
                grad = (dot(kt_all[...], grads_low[:, lanes[h]], NN) * scaling).astype(jnp.bfloat16)
                for k in range(each):
                    res[i * 2 * each + h * each + k, 1] = grad[:, k * rows : (k + 1) * rows]

            for j in range(blocks):
                score(0, j)
            for j in range(blocks):
                score(1, j)
                weigh(0, j)
            attend(0)
            for j in range(blocks):
                weigh(1, j)
                differ(0, j)
            attend(1)
            query_part(0)
            q_both = jnp.concatenate(q_rows, axis=0)
            for j in range(blocks):
                differ(1, j)
                dk[keys[j], :] += dot(grads_low[keys[j], :], q_both, NN)
                dv[keys[j], :] += dot(weights_low[keys[j], :], grad_scaled[...], NT)
            query_part(1)
            return carry

        lax.fori_loop(0, blocks * rows // stretch, one_stretch, 0)
        for j, out in enumerate(outs):
            at = pl.ds(j * rows, rows)
            out[0] = res[j, 0]
            out[1] = res[j, 1]
            out[2] = (dk[at, :] * scaling).astype(jnp.bfloat16)
            out[3] = dv[at, :].astype(jnp.bfloat16)


def seen_bias(frame, own, span, sink):
    seen = ((frame <= own) & (frame > own - span)) | ((frame == sink) & (sink <= own))
    return jnp.where(seen, 0.0, hidden_score)


def frames_by_lane(frames, rows):
    lane_block = lax.broadcasted_iota(jnp.int32, (1, len(frames) * rows), 1) // rows
    row = jnp.zeros_like(lane_block)
    for n, frame in enumerate(frames):
        row = jnp.where(lane_block == n, frame, row)
    return row


def place_block(part, j, rows, q_all, k_all, v_all, kt_all, vt_all, gt_all):
    at = pl.ds(j * rows, rows)
    q_all[at, :] = part[0]
    k_all[at, :] = part[1]
    v_all[at, :] = part[2]
    kt_all[:, at] = part[1].T
    vt_all[:, at] = part[2].T
    gt_all[:, at] = part[3]


def pair_products(j, held, rows, bias, scores, dots, q_all, k_all, v_all, gt_all):
    width = q_all.shape[1]
    rescale = math.log2(math.e) / math.sqrt(width)
    before = held * rows
    at = pl.ds(j * rows, rows)
    every = pl.ds(0, before + rows)
    scores[at, every] = dot(k_all[at, :], q_all[every, :], NT) * rescale + bias[pl.ds(j, 1), every]
    dots[at, every] = dot(v_all[at, :], gt_all[:, every], NN)
    column = dot(k_all[pl.ds(0, before), :], q_all[at, :], NT) * rescale
    for n in range(held):
        keys = pl.ds(n * rows, rows)
        scores[keys, at] = column[n * rows : (n + 1) * rows, :] + bias[pl.ds(n, 1), at]
    dots[pl.ds(0, before), at] = dot(v_all[pl.ds(0, before), :], gt_all[:, at], NN)


def lane_chunks(start, stop, size):
    return [pl.ds(first, min(size, stop - first)) for first in range(start, stop, size)]


def products_kernel(owned, blocks, rows, home, *refs):
    held = blocks - 2
    parts, refs = refs[: held - 1], refs[held - 1 :]
    bias, scores, dots, *places, tiles, sem = refs
    head = looked_up(owned, lax.axis_index("head"), lax.axis_index("tm"))

    @pl.when(head >= 0)
    def _():
        fetch = pltpu.make_async_copy(home.at[pl.ds(0, tiles.shape[0])], tiles, sem)
        fetch.start()
        for j, part in enumerate(parts):
            place_block(part, j + 1, rows, *places)
        fetch.wait()
        place_block(tiles, 0, rows, *places)
        mask = tiles[4].astype(jnp.float32)
        for j in range(blocks):
            for n in range(blocks):
                row = j * blocks + n
                bias[pl.ds(j, 1), pl.ds(n * rows, rows)] = mask[row : row + 1, :]
        q_all, k_all, v_all, _, _, gt_all = places
        lanes = pl.ds(0, held * rows)
        rescale = math.log2(math.e) / math.sqrt(q_all.shape[1])
        for j in range(held):
            keys = pl.ds(j * rows, rows)
            scores[keys, lanes] = dot(k_all[keys, :], q_all[lanes, :], NT) * rescale + bias[pl.ds(j, 1), lanes]
            dots[keys, lanes] = dot(v_all[keys, :], gt_all[:, lanes], NN)


def softmax_kernel(owned, blocks, rows, bias, *refs):
    part, refs = refs[0], refs[9:]
    scores, dots, q_all, k_all, v_all, kt_all, vt_all, gt_all, low, stats, mixed = refs
    head = looked_up(owned, lax.axis_index("head"), lax.axis_index("tm"))

    @pl.when(head >= 0)
    def _():
        newest = blocks - 2
        held = pl.ds(0, (newest + 1) * rows)
        place_block(part, newest, rows, q_all, k_all, v_all, kt_all, vt_all, gt_all)
        pair_products(newest, newest, rows, bias, scores, dots, q_all, k_all, v_all, gt_all)
        for lanes in lane_chunks(0, (newest + 1) * rows, 2 * rows):
            top = jnp.max(scores[held, lanes], axis=0, keepdims=True)
            total = jnp.zeros_like(top)
            for j in range(newest + 1):
                keys = pl.ds(j * rows, rows)
                p = jnp.exp2(scores[keys, lanes] - top)
                total = total + jnp.sum(p, axis=0, keepdims=True)
                scores[keys, lanes] = p
                low[keys, lanes] = p.astype(jnp.bfloat16)
            stats[pl.ds(0, 1), lanes] = top
            stats[pl.ds(1, 1), lanes] = total
            mixed[:, lanes] = dot(vt_all[:, held], low[held, lanes], NN)


def finish_kernel(owned, blocks, rows, bias, stats, mixed, *refs):
    part, refs = refs[0], refs[10:]
    outs, refs = refs[:blocks], refs[blocks:]
    scores, dots, q_all, k_all, v_all, kt_all, vt_all, gt_all, low, grads_low, old_scaled, new_scaled, factors = refs
    head = looked_up(owned, lax.axis_index("head"), lax.axis_index("tm"))
    width = q_all.shape[1]
    scaling = 1.0 / math.sqrt(width)

    @pl.when(head >= 0)
    def _():
        newest = blocks - 1
        at = pl.ds(newest * rows, rows)
        place_block(part, newest, rows, q_all, k_all, v_all, kt_all, vt_all, gt_all)
        pair_products(newest, newest, rows, bias, scores, dots, q_all, k_all, v_all, gt_all)

        def settle(lanes, total, old_factor, weighted):
            inverse = 1.0 / total
            attended = (weighted * inverse).astype(jnp.bfloat16)
            grad_t = gt_all[:, lanes].astype(jnp.float32)
            delta = jnp.sum(grad_t * attended.astype(jnp.float32), axis=0, keepdims=True)
            old = inverse * old_factor
            old_scaled[:, lanes] = (grad_t * old).astype(jnp.bfloat16)
            new_scaled[:, lanes] = (grad_t * inverse).astype(jnp.bfloat16)
            factors[pl.ds(0, 1), lanes] = old
            factors[pl.ds(1, 1), lanes] = delta * old
            factors[pl.ds(2, 1), lanes] = inverse
            factors[pl.ds(3, 1), lanes] = delta * inverse
            for k in range(lanes.size // rows):
                outs[lanes.start // rows + k][0] = attended[:, k * rows : (k + 1) * rows]

        for lanes in lane_chunks(0, newest * rows, 2 * rows):
            fresh = scores[at, lanes]
            before = stats[pl.ds(0, 1), lanes]
            top = jnp.maximum(before, jnp.max(fresh, axis=0, keepdims=True))
            correction = jnp.exp2(before - top)
            p = jnp.exp2(fresh - top)
            p_low = p.astype(jnp.bfloat16)
            scores[at, lanes] = p
            low[at, lanes] = p_low
            total = stats[pl.ds(1, 1), lanes] * correction + jnp.sum(p, axis=0, keepdims=True)
            weighted = mixed[:, lanes] * correction + dot(vt_all[:, at], p_low, NN)
            settle(lanes, total, correction, weighted)
        column = scores[:, at]
        p = jnp.exp2(column - jnp.max(column, axis=0, keepdims=True))
        p_low = p.astype(jnp.bfloat16)
        scores[:, at] = p
        low[:, at] = p_low
        settle(at, jnp.sum(p, axis=0, keepdims=True), 1.0, dot(vt_all[...], p_low, NN))

        for j, out in enumerate(outs):
            keys = pl.ds(j * rows, rows)
            row = 0 if j < newest else 2
            scaled = old_scaled if j < newest else new_scaled
            for lanes in lane_chunks(0, blocks * rows, 4 * rows):
                g = dots[keys, lanes] * factors[pl.ds(row, 1), lanes] - factors[pl.ds(row + 1, 1), lanes]
                grads_low[keys, lanes] = (scores[keys, lanes] * g).astype(jnp.bfloat16)
            out[2] = (dot(grads_low[keys, :], q_all[...], NN) * scaling).astype(jnp.bfloat16)
            out[3] = dot(low[keys, :], scaled[...], NT).astype(jnp.bfloat16)
        for lanes in lane_chunks(0, blocks * rows, 2 * rows):
            grad = (dot(kt_all[...], grads_low[:, lanes], NN) * scaling).astype(jnp.bfloat16)
            for k in range(lanes.size // rows):
                outs[lanes.start // rows + k][1] = grad[:, k * rows : (k + 1) * rows]


def per_device(query, key, value, grad_out, frame_ids, sink_frame, window):
    rows, row_width = query.shape
    heads = window.shape[0]
    width = row_width // heads
    blocks = lax.axis_size("tm")
    owned, sent, partner, pairs = plan(blocks, lax.axis_size("head"), heads)
    axes = ("tm", "head")
    smem = pl.BlockSpec(memory_space=pltpu.SMEM)
    vmem = pl.BlockSpec(memory_space=pltpu.VMEM)
    in_place = pl.BlockSpec(memory_space=pltpu.HBM)
    part = jax.ShapeDtypeStruct((4, rows, width), query.dtype)
    local = jax.ShapeDtypeStruct(query.shape, query.dtype)

    tokens = blocks * rows
    split = tokens <= split_limit
    tiles = 5 if split else 4
    home_tiles = vmem_bytes // (2 * rows * width)
    home, *parts = pl.pallas_call(
        functools.partial(pack_kernel, owned, partner, sent, width),
        out_shape=[jax.ShapeDtypeStruct((home_tiles, rows, width), query.dtype)] + [part] * (blocks - 1),
        in_specs=[in_place] * 7,
        out_specs=[in_place] * blocks,
        scratch_shapes=[
            pltpu.VMEM((4, rows, row_width), query.dtype),
            pltpu.VMEM((tiles, rows, width), query.dtype),
            pltpu.VMEM((blocks - 1, 4, rows, width), query.dtype),
            pltpu.SMEM(frame_ids.shape, jnp.int32),
            pltpu.SMEM(sink_frame.shape, jnp.int32),
            pltpu.SMEM(window.shape, jnp.int32),
            pltpu.SemaphoreType.DMA((7,)),
            pltpu.SemaphoreType.DMA((blocks,)),
        ],
        compiler_params=pltpu.CompilerParams(vmem_limit_bytes=62 * MIB),
        name="pack",
    )(query, key, value, grad_out, frame_ids, sink_frame, window)
    parts = [lax.ppermute(parts[s - 1], axes, pairs[s]) for s in range(1, blocks)]

    stretch = (4 if blocks % 4 == 0 else 2) * rows
    low, full = query.dtype, jnp.float32
    if split:
        square = jax.ShapeDtypeStruct((tokens, tokens), full)
        tall = jax.ShapeDtypeStruct((tokens, width), low)
        wide = jax.ShapeDtypeStruct((width, tokens), low)
        table = jax.ShapeDtypeStruct((blocks, tokens), full)
        held = [square] * 2 + [tall] * 3 + [wide] * 3
        flops = 2 * rows * rows * width
        bias, *state = pl.pallas_call(
            functools.partial(products_kernel, owned, blocks, rows),
            out_shape=[table, *held],
            in_specs=[in_place] + [vmem] * (blocks - 3),
            out_specs=[vmem] * 9,
            scratch_shapes=[pltpu.VMEM((tiles, rows, width), low), pltpu.SemaphoreType.DMA],
            compiler_params=pltpu.CompilerParams(vmem_limit_bytes=20 * MIB),
            cost_estimate=pl.CostEstimate(
                flops=2 * flops * (blocks - 2) ** 2, bytes_accessed=8 * tokens * tokens, transcendentals=0
            ),
            name="products",
        )(home, *parts[:-2])
        *state, weights_low, stats, mixed = pl.pallas_call(
            functools.partial(softmax_kernel, owned, blocks, rows),
            out_shape=[
                *held,
                jax.ShapeDtypeStruct((tokens, tokens), low),
                table,
                jax.ShapeDtypeStruct((width, tokens), full),
            ],
            in_specs=[vmem] * 10,
            out_specs=[vmem] * 11,
            input_output_aliases={2 + n: n for n in range(8)},
            compiler_params=pltpu.CompilerParams(vmem_limit_bytes=20 * MIB),
            cost_estimate=pl.CostEstimate(
                flops=3 * flops * blocks**2, bytes_accessed=8 * tokens * tokens, transcendentals=tokens * tokens
            ),
            name="softmax",
        )(bias, parts[-2], *state)
        parts = pl.pallas_call(
            functools.partial(finish_kernel, owned, blocks, rows),
            out_shape=[part] * blocks + held + [jax.ShapeDtypeStruct((tokens, tokens), low)],
            in_specs=[vmem] * 13,
            out_specs=[vmem] * (blocks + 9),
            input_output_aliases={4 + n: blocks + n for n in range(9)},
            scratch_shapes=[
                pltpu.VMEM((tokens, tokens), low),
                pltpu.VMEM((width, tokens), low),
                pltpu.VMEM((width, tokens), low),
                pltpu.VMEM((8, tokens), full),
            ],
            compiler_params=pltpu.CompilerParams(vmem_limit_bytes=24 * MIB),
            name="finish",
        )(bias, stats, mixed, parts[-1], *state, weights_low)[:blocks]
    else:
        parts = pl.pallas_call(
            functools.partial(head_kernel, owned, partner, rows),
            out_shape=[part] * blocks,
            in_specs=[smem] * 3 + [pl.BlockSpec(memory_space=pl.ANY)] + [vmem] * (blocks - 1),
            out_specs=[vmem] * blocks,
            scratch_shapes=[
                pltpu.VMEM((4, rows, width), low),
                pltpu.VMEM((tokens, width), low),
                pltpu.VMEM((width, tokens), low),
                pltpu.VMEM((width, tokens), low),
                pltpu.VMEM((width, tokens), low),
                pltpu.VMEM((tokens, stretch), full),
                pltpu.VMEM((tokens, stretch), low),
                pltpu.VMEM((tokens, stretch), low),
                pltpu.VMEM((width, stretch), low),
                pltpu.VMEM((tokens, width), full),
                pltpu.VMEM((tokens, width), full),
                pltpu.VMEM((blocks, 2, width, rows), low),
                pltpu.SemaphoreType.DMA,
            ],
            compiler_params=pltpu.CompilerParams(vmem_limit_bytes=48 * MIB),
            name="head_attention",
        )(frame_ids, sink_frame, window, home, *parts)
    back = [[(owner, source) for source, owner in step] for step in pairs]
    parts = [parts[0]] + [lax.ppermute(parts[s], axes, back[s]) for s in range(1, blocks)]

    return pl.pallas_call(
        functools.partial(unpack_kernel, sent, width),
        out_shape=[local] * 4,
        in_specs=[vmem] * blocks,
        out_specs=[vmem] * 4,
        compiler_params=pltpu.CompilerParams(vmem_limit_bytes=24 * MIB),
        name="unpack",
    )(*parts)


def solution(mesh):
    spec = P("tm", "head")
    return jax.shard_map(
        per_device,
        mesh=mesh,
        in_specs=(spec, spec, spec, spec, P(), P(), P("head")),
        out_specs=(spec, spec, spec, spec),
        check_vma=False,
    )
```

```python
import functools
import math

import jax
import jax.numpy as jnp
import numpy as np
from jax import lax
from jax.experimental import pallas as pl
from jax.experimental.pallas import tpu as pltpu
from jax.sharding import PartitionSpec as P

hidden_score = -1e30
MIB = 1 << 20
vmem_bytes = 64 * MIB
split_limit = 1024


even_rounds = (
    {
        0: (6, 5, 7, 3, 1, 4, 2),
        2: (4, 3, 5, 7, 6, 0, 1),
        3: (0, 6, 4, 5, 2, 1, 7),
        4: (7, 2, 3, 1, 0, 6, 5),
        5: (2, 1, 0, 6, 7, 3, 4),
    },
    {
        2: (5, 6, 7, 1, 0, 4, 3),
        3: (0, 5, 4, 6, 7, 1, 2),
        4: (7, 1, 3, 2, 5, 6, 0),
        5: (3, 4, 2, 0, 1, 7, 6),
        7: (1, 2, 0, 4, 6, 3, 5),
    },
)


def plan(blocks, groups, heads):
    laid_out = []
    for group in range(groups):
        if blocks == 8 and heads == 5:
            laid_out.append(even_rounds[group % 2])
        else:
            owners = [(head * blocks // heads + group % 2) % blocks for head in range(heads)]
            laid_out.append({u: [(u - step) % blocks for step in range(1, blocks)] for u in owners})
    owned = np.full((groups, blocks), -1)
    sent = np.full((blocks, groups, blocks), -1)
    partner = np.full((blocks, groups, blocks), -1)
    pairs = [[] for _ in range(blocks)]
    for group, rounds in enumerate(laid_out):
        for head, (owner, sources) in enumerate(rounds.items()):
            owned[group, owner] = head
            for step, source in enumerate((owner, *sources)):
                sent[step, group, source] = head
                partner[step, group, owner] = source
                pairs[step].append((source * groups + group, owner * groups + group))
    return owned, sent, partner, [sorted(step) for step in pairs]


def looked_up(table, group, block):
    groups, blocks = table.shape
    period = next(p for p in range(1, groups + 1) if (table == table[np.arange(groups) % p]).all())
    bits = int(table.max() + 1).bit_length()
    per_word = 31 // bits
    word = jnp.int32(0)
    for row in range(period):
        for first in range(0, blocks, per_word):
            values = table[row, first : first + per_word] + 1
            packed = sum(int(value) << (bits * n) for n, value in enumerate(values))
            here = (lax.rem(group, period) == row) & (block >= first) & (block < first + per_word)
            word = jnp.where(here, packed, word)
    return ((word >> (bits * lax.rem(block, per_word))) & ((1 << bits) - 1)) - 1


def dot(a, b, contract):
    return lax.dot_general(a, b, (contract, ((), ())), preferred_element_type=jnp.float32)


NN = ((1,), (0,))
NT = ((1,), (1,))


def head_columns(head, width):
    return pl.ds(pl.multiple_of(head * width, width), width)


def pack_kernel(owned, partner, sent, width, query, key, value, grad_out, frame_ids, sink_frame, window, *refs):
    blocks = len(sent)
    home, outs, refs = refs[0], refs[1:blocks], refs[blocks:]
    staged, tiles, packed, frames_here, sink_here, window_here, in_sems, out_sems = refs
    group, block = lax.axis_index("head"), lax.axis_index("tm")
    arrays = (query, key, value, grad_out)
    loads = [pltpu.make_async_copy(a, staged.at[n], in_sems.at[n]) for n, a in enumerate(arrays)]
    small = ((frame_ids, frames_here), (sink_frame, sink_here), (window, window_here))
    loads += [pltpu.make_async_copy(a, here, in_sems.at[4 + n]) for n, (a, here) in enumerate(small)]
    for load in loads:
        load.start()
    heads = [looked_up(table, group, block) for table in sent]
    stores = [pltpu.make_async_copy(packed.at[n], out, out_sems.at[1 + n]) for n, out in enumerate(outs)]
    keep = pltpu.make_async_copy(tiles, home.at[pl.ds(0, tiles.shape[0])], out_sems.at[0])
    for load in loads:
        load.wait()

    def fill(target, head):
        columns = head_columns(head, width)
        for n in range(3):
            target[n] = staged[n, :, columns]
        target[3] = staged[3, :, columns].T

    for step, head in enumerate(heads[1:]):

        @pl.when(head >= 0)
        def _():
            fill(packed.at[step], head)
            stores[step].start()

    @pl.when(heads[0] >= 0)
    def _():
        fill(tiles, heads[0])
        if tiles.shape[0] > 4:
            frames = [frames_here[looked_up(table, group, block)] for table in partner]
            row = lax.broadcasted_iota(jnp.int32, tiles.shape[1:], 0)
            theirs, own = jnp.zeros_like(row), jnp.zeros_like(row)
            for n, frame in enumerate(frames):
                theirs = jnp.where(row // blocks == n, frame, theirs)
                own = jnp.where(lax.rem(row, blocks) == n, frame, own)
            tiles[4] = seen_bias(theirs, own, window_here[heads[0]], sink_here[0]).astype(tiles.dtype)
        keep.start()

    for step, head in enumerate(heads[1:]):

        @pl.when(head >= 0)
        def _():
            stores[step].wait()

    @pl.when(heads[0] >= 0)
    def _():
        keep.wait()


def unpack_kernel(sent, width, *refs):
    parts, (attended, query_grad, key_grad, value_grad) = refs[:-4], refs[-4:]
    group, block = lax.axis_index("head"), lax.axis_index("tm")
    for step, part in enumerate(parts):
        head = looked_up(sent[step], group, block)

        @pl.when(head >= 0)
        def _():
            columns = head_columns(head, width)
            attended[:, columns] = part[0].T
            query_grad[:, columns] = part[1].T
            key_grad[:, columns] = part[2]
            value_grad[:, columns] = part[3]


def head_kernel(owned, partner, rows, frame_ids, sink_frame, window, local, *refs):
    blocks = len(partner)
    parts, outs, scratch = refs[: blocks - 1], refs[blocks - 1 : 2 * blocks - 1], refs[2 * blocks - 1 :]
    (here, q_all, kt_all, vt_all, gt_all, weights, weights_low, grads_low, grad_scaled, dk, dv, res, sem) = scratch
    parts = (here, *parts)
    group, block = lax.axis_index("head"), lax.axis_index("tm")
    head = looked_up(owned, group, block)
    width = q_all.shape[1]
    scaling = 1.0 / math.sqrt(width)
    rescale = scaling * math.log2(math.e)
    stretch = weights.shape[1]
    half = stretch // 2
    each = half // rows

    @pl.when(head >= 0)
    def _():
        fetch = pltpu.make_async_copy(local.at[pl.ds(0, 4)], here, sem)
        fetch.start()
        span = window[head]
        sink = sink_frame[0]
        frames = [frame_ids[looked_up(table, group, block)] for table in partner]

        def placed(j):
            at = pl.ds(j * rows, rows)
            q_all[at, :] = parts[j][0]
            kt_all[:, at] = parts[j][1].T
            vt_all[:, at] = parts[j][2].T
            gt_all[:, at] = parts[j][3]

        for j in range(1, blocks):
            placed(j)
        fetch.wait()
        placed(0)
        dk[...] = jnp.zeros_like(dk)
        dv[...] = jnp.zeros_like(dv)
        lane_block = lax.broadcasted_iota(jnp.int32, (1, half), 1) // rows

        def one_stretch(i, carry):
            at = [pl.ds(pl.multiple_of(i * stretch + h * half, half), half) for h in range(2)]
            lanes = [pl.ds(h * half, half) for h in range(2)]
            keys = [pl.ds(j * rows, rows) for j in range(blocks)]
            q_rows = [q_all[at[h], :] for h in range(2)]
            top = [jnp.full((1, half), hidden_score, jnp.float32)] * 2
            total = [jnp.zeros((1, half), jnp.float32)] * 2
            delta = [None] * 2
            own = [[], []]
            for h in range(2):
                for k in range(each):
                    n = i * 2 * each + h * each + k
                    own[h].append(sum(jnp.where(n == j, frames[j], 0) for j in range(blocks)))

            def score(h, j):
                bias = jnp.zeros((1, half), jnp.float32)
                for k in range(each):
                    seen = (frames[j] <= own[h][k]) & (frames[j] > own[h][k] - span)
                    seen = seen | ((frames[j] == sink) & (sink <= own[h][k]))
                    bias = jnp.where(lane_block == k, jnp.where(seen, 0.0, hidden_score), bias)
                scores = dot(parts[j][1], q_rows[h], NT) * rescale + bias
                weights[keys[j], lanes[h]] = scores
                top[h] = jnp.maximum(top[h], jnp.max(scores, axis=0, keepdims=True))

            def weigh(h, j):
                p = jnp.exp2(weights[keys[j], lanes[h]] - top[h])
                total[h] = total[h] + jnp.sum(p, axis=0, keepdims=True)
                weights[keys[j], lanes[h]] = p
                weights_low[keys[j], lanes[h]] = p.astype(jnp.bfloat16)

            def attend(h):
                inverse = 1.0 / total[h]
                mixed = (dot(vt_all[...], weights_low[:, lanes[h]], NN) * inverse).astype(jnp.bfloat16)
                grad_t = gt_all[:, at[h]].astype(jnp.float32)
                delta[h] = jnp.sum(grad_t * mixed.astype(jnp.float32), axis=0, keepdims=True) * inverse
                grad_scaled[:, lanes[h]] = (grad_t * inverse).astype(jnp.bfloat16)
                for k in range(each):
                    res[i * 2 * each + h * each + k, 0] = mixed[:, k * rows : (k + 1) * rows]

            def differ(h, j):
                g = dot(parts[j][2], grad_scaled[:, lanes[h]], NN) - delta[h]
                grads_low[keys[j], lanes[h]] = (weights[keys[j], lanes[h]] * g).astype(jnp.bfloat16)

            def query_part(h):
                grad = (dot(kt_all[...], grads_low[:, lanes[h]], NN) * scaling).astype(jnp.bfloat16)
                for k in range(each):
                    res[i * 2 * each + h * each + k, 1] = grad[:, k * rows : (k + 1) * rows]

            for j in range(blocks):
                score(0, j)
            for j in range(blocks):
                score(1, j)
                weigh(0, j)
            attend(0)
            for j in range(blocks):
                weigh(1, j)
                differ(0, j)
            attend(1)
            query_part(0)
            q_both = jnp.concatenate(q_rows, axis=0)
            for j in range(blocks):
                differ(1, j)
                dk[keys[j], :] += dot(grads_low[keys[j], :], q_both, NN)
                dv[keys[j], :] += dot(weights_low[keys[j], :], grad_scaled[...], NT)
            query_part(1)
            return carry

        lax.fori_loop(0, blocks * rows // stretch, one_stretch, 0)
        for j, out in enumerate(outs):
            at = pl.ds(j * rows, rows)
            out[0] = res[j, 0]
            out[1] = res[j, 1]
            out[2] = (dk[at, :] * scaling).astype(jnp.bfloat16)
            out[3] = dv[at, :].astype(jnp.bfloat16)


def seen_bias(frame, own, span, sink):
    seen = ((frame <= own) & (frame > own - span)) | ((frame == sink) & (sink <= own))
    return jnp.where(seen, 0.0, hidden_score)


def frames_by_lane(frames, rows):
    lane_block = lax.broadcasted_iota(jnp.int32, (1, len(frames) * rows), 1) // rows
    row = jnp.zeros_like(lane_block)
    for n, frame in enumerate(frames):
        row = jnp.where(lane_block == n, frame, row)
    return row


def place_block(part, j, rows, q_all, k_all, v_all, kt_all, vt_all, gt_all):
    at = pl.ds(j * rows, rows)
    q_all[at, :] = part[0]
    k_all[at, :] = part[1]
    v_all[at, :] = part[2]
    kt_all[:, at] = part[1].T
    vt_all[:, at] = part[2].T
    gt_all[:, at] = part[3]


def pair_products(j, held, rows, bias, scores, dots, q_all, k_all, v_all, gt_all):
    width = q_all.shape[1]
    rescale = math.log2(math.e) / math.sqrt(width)
    before = held * rows
    at = pl.ds(j * rows, rows)
    every = pl.ds(0, before + rows)
    scores[at, every] = dot(k_all[at, :], q_all[every, :], NT) * rescale + bias[pl.ds(j, 1), every]
    dots[at, every] = dot(v_all[at, :], gt_all[:, every], NN)
    column = dot(k_all[pl.ds(0, before), :], q_all[at, :], NT) * rescale
    for n in range(held):
        keys = pl.ds(n * rows, rows)
        scores[keys, at] = column[n * rows : (n + 1) * rows, :] + bias[pl.ds(n, 1), at]
    dots[pl.ds(0, before), at] = dot(v_all[pl.ds(0, before), :], gt_all[:, at], NN)


def lane_chunks(start, stop, size):
    return [pl.ds(first, min(size, stop - first)) for first in range(start, stop, size)]


def products_kernel(owned, blocks, rows, home, *refs):
    held = blocks - 2
    parts, refs = refs[: held - 1], refs[held - 1 :]
    bias, scores, dots, *places, tiles, sem = refs
    head = looked_up(owned, lax.axis_index("head"), lax.axis_index("tm"))

    @pl.when(head >= 0)
    def _():
        fetch = pltpu.make_async_copy(home.at[pl.ds(0, tiles.shape[0])], tiles, sem)
        fetch.start()
        for j, part in enumerate(parts):
            place_block(part, j + 1, rows, *places)
        fetch.wait()
        place_block(tiles, 0, rows, *places)
        mask = tiles[4].astype(jnp.float32)
        for j in range(blocks):
            for n in range(blocks):
                row = j * blocks + n
                bias[pl.ds(j, 1), pl.ds(n * rows, rows)] = mask[row : row + 1, :]
        q_all, k_all, v_all, _, _, gt_all = places
        lanes = pl.ds(0, held * rows)
        rescale = math.log2(math.e) / math.sqrt(q_all.shape[1])
        for j in range(held):
            keys = pl.ds(j * rows, rows)
            scores[keys, lanes] = dot(k_all[keys, :], q_all[lanes, :], NT) * rescale + bias[pl.ds(j, 1), lanes]
            dots[keys, lanes] = dot(v_all[keys, :], gt_all[:, lanes], NN)


def softmax_kernel(owned, blocks, rows, bias, *refs):
    part, refs = refs[0], refs[9:]
    scores, dots, q_all, k_all, v_all, kt_all, vt_all, gt_all, low, stats, mixed = refs
    head = looked_up(owned, lax.axis_index("head"), lax.axis_index("tm"))

    @pl.when(head >= 0)
    def _():
        newest = blocks - 2
        held = pl.ds(0, (newest + 1) * rows)
        place_block(part, newest, rows, q_all, k_all, v_all, kt_all, vt_all, gt_all)
        pair_products(newest, newest, rows, bias, scores, dots, q_all, k_all, v_all, gt_all)
        for lanes in lane_chunks(0, (newest + 1) * rows, 2 * rows):
            top = jnp.max(scores[held, lanes], axis=0, keepdims=True)
            total = jnp.zeros_like(top)
            for j in range(newest + 1):
                keys = pl.ds(j * rows, rows)
                p = jnp.exp2(scores[keys, lanes] - top)
                total = total + jnp.sum(p, axis=0, keepdims=True)
                scores[keys, lanes] = p
                low[keys, lanes] = p.astype(jnp.bfloat16)
            stats[pl.ds(0, 1), lanes] = top
            stats[pl.ds(1, 1), lanes] = total
            mixed[:, lanes] = dot(vt_all[:, held], low[held, lanes], NN)


def finish_kernel(owned, blocks, rows, bias, stats, mixed, *refs):
    part, refs = refs[0], refs[10:]
    outs, refs = refs[:blocks], refs[blocks:]
    scores, dots, q_all, k_all, v_all, kt_all, vt_all, gt_all, low, grads_low, old_scaled, new_scaled, factors = refs
    head = looked_up(owned, lax.axis_index("head"), lax.axis_index("tm"))
    width = q_all.shape[1]
    scaling = 1.0 / math.sqrt(width)

    @pl.when(head >= 0)
    def _():
        newest = blocks - 1
        at = pl.ds(newest * rows, rows)
        place_block(part, newest, rows, q_all, k_all, v_all, kt_all, vt_all, gt_all)
        pair_products(newest, newest, rows, bias, scores, dots, q_all, k_all, v_all, gt_all)

        def settle(lanes, total, old_factor, weighted):
            inverse = 1.0 / total
            attended = (weighted * inverse).astype(jnp.bfloat16)
            grad_t = gt_all[:, lanes].astype(jnp.float32)
            delta = jnp.sum(grad_t * attended.astype(jnp.float32), axis=0, keepdims=True)
            old = inverse * old_factor
            old_scaled[:, lanes] = (grad_t * old).astype(jnp.bfloat16)
            new_scaled[:, lanes] = (grad_t * inverse).astype(jnp.bfloat16)
            factors[pl.ds(0, 1), lanes] = old
            factors[pl.ds(1, 1), lanes] = delta * old
            factors[pl.ds(2, 1), lanes] = inverse
            factors[pl.ds(3, 1), lanes] = delta * inverse
            for k in range(lanes.size // rows):
                outs[lanes.start // rows + k][0] = attended[:, k * rows : (k + 1) * rows]

        for lanes in lane_chunks(0, newest * rows, 2 * rows):
            fresh = scores[at, lanes]
            before = stats[pl.ds(0, 1), lanes]
            top = jnp.maximum(before, jnp.max(fresh, axis=0, keepdims=True))
            correction = jnp.exp2(before - top)
            p = jnp.exp2(fresh - top)
            p_low = p.astype(jnp.bfloat16)
            scores[at, lanes] = p
            low[at, lanes] = p_low
            total = stats[pl.ds(1, 1), lanes] * correction + jnp.sum(p, axis=0, keepdims=True)
            weighted = mixed[:, lanes] * correction + dot(vt_all[:, at], p_low, NN)
            settle(lanes, total, correction, weighted)
        column = scores[:, at]
        p = jnp.exp2(column - jnp.max(column, axis=0, keepdims=True))
        p_low = p.astype(jnp.bfloat16)
        scores[:, at] = p
        low[:, at] = p_low
        settle(at, jnp.sum(p, axis=0, keepdims=True), 1.0, dot(vt_all[...], p_low, NN))

        for j, out in enumerate(outs):
            keys = pl.ds(j * rows, rows)
            row = 0 if j < newest else 2
            scaled = old_scaled if j < newest else new_scaled
            for lanes in lane_chunks(0, blocks * rows, 4 * rows):
                g = dots[keys, lanes] * factors[pl.ds(row, 1), lanes] - factors[pl.ds(row + 1, 1), lanes]
                grads_low[keys, lanes] = (scores[keys, lanes] * g).astype(jnp.bfloat16)
            out[2] = (dot(grads_low[keys, :], q_all[...], NN) * scaling).astype(jnp.bfloat16)
            out[3] = dot(low[keys, :], scaled[...], NT).astype(jnp.bfloat16)
        for lanes in lane_chunks(0, blocks * rows, 2 * rows):
            grad = (dot(kt_all[...], grads_low[:, lanes], NN) * scaling).astype(jnp.bfloat16)
            for k in range(lanes.size // rows):
                outs[lanes.start // rows + k][1] = grad[:, k * rows : (k + 1) * rows]


def per_device(query, key, value, grad_out, frame_ids, sink_frame, window):
    rows, row_width = query.shape
    heads = window.shape[0]
    width = row_width // heads
    blocks = lax.axis_size("tm")
    owned, sent, partner, pairs = plan(blocks, lax.axis_size("head"), heads)
    axes = ("tm", "head")
    smem = pl.BlockSpec(memory_space=pltpu.SMEM)
    vmem = pl.BlockSpec(memory_space=pltpu.VMEM)
    in_place = pl.BlockSpec(memory_space=pltpu.HBM)
    part = jax.ShapeDtypeStruct((4, rows, width), query.dtype)
    local = jax.ShapeDtypeStruct(query.shape, query.dtype)

    tokens = blocks * rows
    split = tokens <= split_limit
    tiles = 5 if split else 4
    home_tiles = vmem_bytes // (2 * rows * width)
    home, *parts = pl.pallas_call(
        functools.partial(pack_kernel, owned, partner, sent, width),
        out_shape=[jax.ShapeDtypeStruct((home_tiles, rows, width), query.dtype)] + [part] * (blocks - 1),
        in_specs=[in_place] * 7,
        out_specs=[in_place] * blocks,
        scratch_shapes=[
            pltpu.VMEM((4, rows, row_width), query.dtype),
            pltpu.VMEM((tiles, rows, width), query.dtype),
            pltpu.VMEM((blocks - 1, 4, rows, width), query.dtype),
            pltpu.SMEM(frame_ids.shape, jnp.int32),
            pltpu.SMEM(sink_frame.shape, jnp.int32),
            pltpu.SMEM(window.shape, jnp.int32),
            pltpu.SemaphoreType.DMA((7,)),
            pltpu.SemaphoreType.DMA((blocks,)),
        ],
        compiler_params=pltpu.CompilerParams(vmem_limit_bytes=62 * MIB),
        name="pack",
    )(query, key, value, grad_out, frame_ids, sink_frame, window)
    parts = [lax.ppermute(parts[s - 1], axes, pairs[s]) for s in range(1, blocks)]

    stretch = (4 if blocks % 4 == 0 else 2) * rows
    low, full = query.dtype, jnp.float32
    if split:
        square = jax.ShapeDtypeStruct((tokens, tokens), full)
        tall = jax.ShapeDtypeStruct((tokens, width), low)
        wide = jax.ShapeDtypeStruct((width, tokens), low)
        table = jax.ShapeDtypeStruct((blocks, tokens), full)
        held = [square] * 2 + [tall] * 3 + [wide] * 3
        flops = 2 * rows * rows * width
        bias, *state = pl.pallas_call(
            functools.partial(products_kernel, owned, blocks, rows),
            out_shape=[table, *held],
            in_specs=[in_place] + [vmem] * (blocks - 3),
            out_specs=[vmem] * 9,
            scratch_shapes=[pltpu.VMEM((tiles, rows, width), low), pltpu.SemaphoreType.DMA],
            compiler_params=pltpu.CompilerParams(vmem_limit_bytes=20 * MIB),
            cost_estimate=pl.CostEstimate(
                flops=2 * flops * (blocks - 2) ** 2, bytes_accessed=8 * tokens * tokens, transcendentals=0
            ),
            name="products",
        )(home, *parts[:-2])
        *state, weights_low, stats, mixed = pl.pallas_call(
            functools.partial(softmax_kernel, owned, blocks, rows),
            out_shape=[
                *held,
                jax.ShapeDtypeStruct((tokens, tokens), low),
                table,
                jax.ShapeDtypeStruct((width, tokens), full),
            ],
            in_specs=[vmem] * 10,
            out_specs=[vmem] * 11,
            input_output_aliases={2 + n: n for n in range(8)},
            compiler_params=pltpu.CompilerParams(vmem_limit_bytes=20 * MIB),
            cost_estimate=pl.CostEstimate(
                flops=3 * flops * blocks**2, bytes_accessed=8 * tokens * tokens, transcendentals=tokens * tokens
            ),
            name="softmax",
        )(bias, parts[-2], *state)
        parts = pl.pallas_call(
            functools.partial(finish_kernel, owned, blocks, rows),
            out_shape=[part] * blocks + held + [jax.ShapeDtypeStruct((tokens, tokens), low)],
            in_specs=[vmem] * 13,
            out_specs=[vmem] * (blocks + 9),
            input_output_aliases={4 + n: blocks + n for n in range(9)},
            scratch_shapes=[
                pltpu.VMEM((tokens, tokens), low),
                pltpu.VMEM((width, tokens), low),
                pltpu.VMEM((width, tokens), low),
                pltpu.VMEM((8, tokens), full),
            ],
            compiler_params=pltpu.CompilerParams(vmem_limit_bytes=24 * MIB),
            name="finish",
        )(bias, stats, mixed, parts[-1], *state, weights_low)[:blocks]
    else:
        parts = pl.pallas_call(
            functools.partial(head_kernel, owned, partner, rows),
            out_shape=[part] * blocks,
            in_specs=[smem] * 3 + [pl.BlockSpec(memory_space=pl.ANY)] + [vmem] * (blocks - 1),
            out_specs=[vmem] * blocks,
            scratch_shapes=[
                pltpu.VMEM((4, rows, width), low),
                pltpu.VMEM((tokens, width), low),
                pltpu.VMEM((width, tokens), low),
                pltpu.VMEM((width, tokens), low),
                pltpu.VMEM((width, tokens), low),
                pltpu.VMEM((tokens, stretch), full),
                pltpu.VMEM((tokens, stretch), low),
                pltpu.VMEM((tokens, stretch), low),
                pltpu.VMEM((width, stretch), low),
                pltpu.VMEM((tokens, width), full),
                pltpu.VMEM((tokens, width), full),
                pltpu.VMEM((blocks, 2, width, rows), low),
                pltpu.SemaphoreType.DMA,
            ],
            compiler_params=pltpu.CompilerParams(vmem_limit_bytes=48 * MIB),
            name="head_attention",
        )(frame_ids, sink_frame, window, home, *parts)
    back = [[(owner, source) for source, owner in step] for step in pairs]
    parts = [parts[0]] + [lax.ppermute(parts[s], axes, back[s]) for s in range(1, blocks)]

    return pl.pallas_call(
        functools.partial(unpack_kernel, sent, width),
        out_shape=[local] * 4,
        in_specs=[vmem] * blocks,
        out_specs=[vmem] * 4,
        compiler_params=pltpu.CompilerParams(vmem_limit_bytes=24 * MIB),
        name="unpack",
    )(*parts)


def solution(mesh):
    spec = P("tm", "head")
    return jax.shard_map(
        per_device,
        mesh=mesh,
        in_specs=(spec, spec, spec, spec, P(), P(), P("head")),
        out_specs=(spec, spec, spec, spec),
        check_vma=False,
    )
```

```python
import functools
import math

import jax
import jax.numpy as jnp
import numpy as np
from jax import lax
from jax.experimental import pallas as pl
from jax.experimental.pallas import tpu as pltpu
from jax.sharding import PartitionSpec as P

hidden_score = -1e30
MIB = 1 << 20
vmem_bytes = 64 * MIB
split_limit = 1024


even_rounds = (
    {
        2: (5, 6, 7, 1, 0, 4, 3),
        3: (0, 5, 4, 6, 7, 1, 2),
        4: (7, 1, 3, 2, 5, 6, 0),
        5: (3, 4, 2, 0, 1, 7, 6),
        7: (1, 2, 0, 4, 6, 3, 5),
    },
    {
        0: (6, 5, 7, 3, 1, 4, 2),
        2: (4, 3, 5, 7, 6, 0, 1),
        3: (0, 6, 4, 5, 2, 1, 7),
        4: (7, 2, 3, 1, 0, 6, 5),
        5: (2, 1, 0, 6, 7, 3, 4),
    },
)


def plan(blocks, groups, heads):
    laid_out = []
    for group in range(groups):
        if blocks == 8 and heads == 5:
            laid_out.append(even_rounds[group % 2])
        else:
            owners = [(head * blocks // heads + group % 2) % blocks for head in range(heads)]
            laid_out.append({u: [(u - step) % blocks for step in range(1, blocks)] for u in owners})
    owned = np.full((groups, blocks), -1)
    sent = np.full((blocks, groups, blocks), -1)
    partner = np.full((blocks, groups, blocks), -1)
    pairs = [[] for _ in range(blocks)]
    for group, rounds in enumerate(laid_out):
        for head, (owner, sources) in enumerate(rounds.items()):
            owned[group, owner] = head
            for step, source in enumerate((owner, *sources)):
                sent[step, group, source] = head
                partner[step, group, owner] = source
                pairs[step].append((source * groups + group, owner * groups + group))
    return owned, sent, partner, [sorted(step) for step in pairs]


def looked_up(table, group, block):
    groups, blocks = table.shape
    period = next(p for p in range(1, groups + 1) if (table == table[np.arange(groups) % p]).all())
    bits = int(table.max() + 1).bit_length()
    per_word = 31 // bits
    word = jnp.int32(0)
    for row in range(period):
        for first in range(0, blocks, per_word):
            values = table[row, first : first + per_word] + 1
            packed = sum(int(value) << (bits * n) for n, value in enumerate(values))
            here = (lax.rem(group, period) == row) & (block >= first) & (block < first + per_word)
            word = jnp.where(here, packed, word)
    return ((word >> (bits * lax.rem(block, per_word))) & ((1 << bits) - 1)) - 1


def dot(a, b, contract):
    return lax.dot_general(a, b, (contract, ((), ())), preferred_element_type=jnp.float32)


NN = ((1,), (0,))
NT = ((1,), (1,))


def head_columns(head, width):
    return pl.ds(pl.multiple_of(head * width, width), width)


def pack_kernel(owned, partner, sent, width, query, key, value, grad_out, frame_ids, sink_frame, window, *refs):
    blocks = len(sent)
    home, outs, refs = refs[0], refs[1:blocks], refs[blocks:]
    staged, tiles, packed, frames_here, sink_here, window_here, in_sems, out_sems = refs
    group, block = lax.axis_index("head"), lax.axis_index("tm")
    arrays = (query, key, value, grad_out)
    loads = [pltpu.make_async_copy(a, staged.at[n], in_sems.at[n]) for n, a in enumerate(arrays)]
    small = ((frame_ids, frames_here), (sink_frame, sink_here), (window, window_here))
    loads += [pltpu.make_async_copy(a, here, in_sems.at[4 + n]) for n, (a, here) in enumerate(small)]
    for load in loads:
        load.start()
    heads = [looked_up(table, group, block) for table in sent]
    stores = [pltpu.make_async_copy(packed.at[n], out, out_sems.at[1 + n]) for n, out in enumerate(outs)]
    keep = pltpu.make_async_copy(tiles, home.at[pl.ds(0, tiles.shape[0])], out_sems.at[0])
    for load in loads:
        load.wait()

    def fill(target, head):
        columns = head_columns(head, width)
        for n in range(3):
            target[n] = staged[n, :, columns]
        target[3] = staged[3, :, columns].T

    for step, head in enumerate(heads[1:]):

        @pl.when(head >= 0)
        def _():
            fill(packed.at[step], head)
            stores[step].start()

    @pl.when(heads[0] >= 0)
    def _():
        fill(tiles, heads[0])
        if tiles.shape[0] > 4:
            frames = [frames_here[looked_up(table, group, block)] for table in partner]
            row = lax.broadcasted_iota(jnp.int32, tiles.shape[1:], 0)
            theirs, own = jnp.zeros_like(row), jnp.zeros_like(row)
            for n, frame in enumerate(frames):
                theirs = jnp.where(row // blocks == n, frame, theirs)
                own = jnp.where(lax.rem(row, blocks) == n, frame, own)
            tiles[4] = seen_bias(theirs, own, window_here[heads[0]], sink_here[0]).astype(tiles.dtype)
        keep.start()

    for step, head in enumerate(heads[1:]):

        @pl.when(head >= 0)
        def _():
            stores[step].wait()

    @pl.when(heads[0] >= 0)
    def _():
        keep.wait()


def unpack_kernel(sent, width, *refs):
    parts, (attended, query_grad, key_grad, value_grad) = refs[:-4], refs[-4:]
    group, block = lax.axis_index("head"), lax.axis_index("tm")
    for step, part in enumerate(parts):
        head = looked_up(sent[step], group, block)

        @pl.when(head >= 0)
        def _():
            columns = head_columns(head, width)
            attended[:, columns] = part[0].T
            query_grad[:, columns] = part[1].T
            key_grad[:, columns] = part[2]
            value_grad[:, columns] = part[3]


def head_kernel(owned, partner, rows, frame_ids, sink_frame, window, local, *refs):
    blocks = len(partner)
    parts, outs, scratch = refs[: blocks - 1], refs[blocks - 1 : 2 * blocks - 1], refs[2 * blocks - 1 :]
    (here, q_all, kt_all, vt_all, gt_all, weights, weights_low, grads_low, grad_scaled, dk, dv, res, sem) = scratch
    parts = (here, *parts)
    group, block = lax.axis_index("head"), lax.axis_index("tm")
    head = looked_up(owned, group, block)
    width = q_all.shape[1]
    scaling = 1.0 / math.sqrt(width)
    rescale = scaling * math.log2(math.e)
    stretch = weights.shape[1]
    half = stretch // 2
    each = half // rows

    @pl.when(head >= 0)
    def _():
        fetch = pltpu.make_async_copy(local.at[pl.ds(0, 4)], here, sem)
        fetch.start()
        span = window[head]
        sink = sink_frame[0]
        frames = [frame_ids[looked_up(table, group, block)] for table in partner]

        def placed(j):
            at = pl.ds(j * rows, rows)
            q_all[at, :] = parts[j][0]
            kt_all[:, at] = parts[j][1].T
            vt_all[:, at] = parts[j][2].T
            gt_all[:, at] = parts[j][3]

        for j in range(1, blocks):
            placed(j)
        fetch.wait()
        placed(0)
        dk[...] = jnp.zeros_like(dk)
        dv[...] = jnp.zeros_like(dv)
        lane_block = lax.broadcasted_iota(jnp.int32, (1, half), 1) // rows

        def one_stretch(i, carry):
            at = [pl.ds(pl.multiple_of(i * stretch + h * half, half), half) for h in range(2)]
            lanes = [pl.ds(h * half, half) for h in range(2)]
            keys = [pl.ds(j * rows, rows) for j in range(blocks)]
            q_rows = [q_all[at[h], :] for h in range(2)]
            top = [jnp.full((1, half), hidden_score, jnp.float32)] * 2
            total = [jnp.zeros((1, half), jnp.float32)] * 2
            delta = [None] * 2
            own = [[], []]
            for h in range(2):
                for k in range(each):
                    n = i * 2 * each + h * each + k
                    own[h].append(sum(jnp.where(n == j, frames[j], 0) for j in range(blocks)))

            def score(h, j):
                bias = jnp.zeros((1, half), jnp.float32)
                for k in range(each):
                    seen = (frames[j] <= own[h][k]) & (frames[j] > own[h][k] - span)
                    seen = seen | ((frames[j] == sink) & (sink <= own[h][k]))
                    bias = jnp.where(lane_block == k, jnp.where(seen, 0.0, hidden_score), bias)
                scores = dot(parts[j][1], q_rows[h], NT) * rescale + bias
                weights[keys[j], lanes[h]] = scores
                top[h] = jnp.maximum(top[h], jnp.max(scores, axis=0, keepdims=True))

            def weigh(h, j):
                p = jnp.exp2(weights[keys[j], lanes[h]] - top[h])
                total[h] = total[h] + jnp.sum(p, axis=0, keepdims=True)
                weights[keys[j], lanes[h]] = p
                weights_low[keys[j], lanes[h]] = p.astype(jnp.bfloat16)

            def attend(h):
                inverse = 1.0 / total[h]
                mixed = (dot(vt_all[...], weights_low[:, lanes[h]], NN) * inverse).astype(jnp.bfloat16)
                grad_t = gt_all[:, at[h]].astype(jnp.float32)
                delta[h] = jnp.sum(grad_t * mixed.astype(jnp.float32), axis=0, keepdims=True) * inverse
                grad_scaled[:, lanes[h]] = (grad_t * inverse).astype(jnp.bfloat16)
                for k in range(each):
                    res[i * 2 * each + h * each + k, 0] = mixed[:, k * rows : (k + 1) * rows]

            def differ(h, j):
                g = dot(parts[j][2], grad_scaled[:, lanes[h]], NN) - delta[h]
                grads_low[keys[j], lanes[h]] = (weights[keys[j], lanes[h]] * g).astype(jnp.bfloat16)

            def query_part(h):
                grad = (dot(kt_all[...], grads_low[:, lanes[h]], NN) * scaling).astype(jnp.bfloat16)
                for k in range(each):
                    res[i * 2 * each + h * each + k, 1] = grad[:, k * rows : (k + 1) * rows]

            for j in range(blocks):
                score(0, j)
            for j in range(blocks):
                score(1, j)
                weigh(0, j)
            attend(0)
            for j in range(blocks):
                weigh(1, j)
                differ(0, j)
            attend(1)
            query_part(0)
            q_both = jnp.concatenate(q_rows, axis=0)
            for j in range(blocks):
                differ(1, j)
                dk[keys[j], :] += dot(grads_low[keys[j], :], q_both, NN)
                dv[keys[j], :] += dot(weights_low[keys[j], :], grad_scaled[...], NT)
            query_part(1)
            return carry

        lax.fori_loop(0, blocks * rows // stretch, one_stretch, 0)
        for j, out in enumerate(outs):
            at = pl.ds(j * rows, rows)
            out[0] = res[j, 0]
            out[1] = res[j, 1]
            out[2] = (dk[at, :] * scaling).astype(jnp.bfloat16)
            out[3] = dv[at, :].astype(jnp.bfloat16)


def seen_bias(frame, own, span, sink):
    seen = ((frame <= own) & (frame > own - span)) | ((frame == sink) & (sink <= own))
    return jnp.where(seen, 0.0, hidden_score)


def frames_by_lane(frames, rows):
    lane_block = lax.broadcasted_iota(jnp.int32, (1, len(frames) * rows), 1) // rows
    row = jnp.zeros_like(lane_block)
    for n, frame in enumerate(frames):
        row = jnp.where(lane_block == n, frame, row)
    return row


def place_block(part, j, rows, q_all, k_all, v_all, kt_all, vt_all, gt_all):
    at = pl.ds(j * rows, rows)
    q_all[at, :] = part[0]
    k_all[at, :] = part[1]
    v_all[at, :] = part[2]
    kt_all[:, at] = part[1].T
    vt_all[:, at] = part[2].T
    gt_all[:, at] = part[3]


def pair_products(j, held, rows, bias, scores, dots, q_all, k_all, v_all, gt_all):
    width = q_all.shape[1]
    rescale = math.log2(math.e) / math.sqrt(width)
    before = held * rows
    at = pl.ds(j * rows, rows)
    every = pl.ds(0, before + rows)
    scores[at, every] = dot(k_all[at, :], q_all[every, :], NT) * rescale + bias[pl.ds(j, 1), every]
    dots[at, every] = dot(v_all[at, :], gt_all[:, every], NN)
    column = dot(k_all[pl.ds(0, before), :], q_all[at, :], NT) * rescale
    for n in range(held):
        keys = pl.ds(n * rows, rows)
        scores[keys, at] = column[n * rows : (n + 1) * rows, :] + bias[pl.ds(n, 1), at]
    dots[pl.ds(0, before), at] = dot(v_all[pl.ds(0, before), :], gt_all[:, at], NN)


def lane_chunks(start, stop, size):
    return [pl.ds(first, min(size, stop - first)) for first in range(start, stop, size)]


def products_kernel(owned, blocks, rows, home, *refs):
    held = blocks - 2
    parts, refs = refs[: held - 1], refs[held - 1 :]
    bias, scores, dots, *places, tiles, sem = refs
    head = looked_up(owned, lax.axis_index("head"), lax.axis_index("tm"))

    @pl.when(head >= 0)
    def _():
        fetch = pltpu.make_async_copy(home.at[pl.ds(0, tiles.shape[0])], tiles, sem)
        fetch.start()
        for j, part in enumerate(parts):
            place_block(part, j + 1, rows, *places)
        fetch.wait()
        place_block(tiles, 0, rows, *places)
        mask = tiles[4].astype(jnp.float32)
        for j in range(blocks):
            for n in range(blocks):
                row = j * blocks + n
                bias[pl.ds(j, 1), pl.ds(n * rows, rows)] = mask[row : row + 1, :]
        q_all, k_all, v_all, _, _, gt_all = places
        lanes = pl.ds(0, held * rows)
        rescale = math.log2(math.e) / math.sqrt(q_all.shape[1])
        for j in range(held):
            keys = pl.ds(j * rows, rows)
            scores[keys, lanes] = dot(k_all[keys, :], q_all[lanes, :], NT) * rescale + bias[pl.ds(j, 1), lanes]
            dots[keys, lanes] = dot(v_all[keys, :], gt_all[:, lanes], NN)


def softmax_kernel(owned, blocks, rows, bias, *refs):
    part, refs = refs[0], refs[9:]
    scores, dots, q_all, k_all, v_all, kt_all, vt_all, gt_all, low, stats, mixed = refs
    head = looked_up(owned, lax.axis_index("head"), lax.axis_index("tm"))

    @pl.when(head >= 0)
    def _():
        newest = blocks - 2
        held = pl.ds(0, (newest + 1) * rows)
        place_block(part, newest, rows, q_all, k_all, v_all, kt_all, vt_all, gt_all)
        pair_products(newest, newest, rows, bias, scores, dots, q_all, k_all, v_all, gt_all)
        for lanes in lane_chunks(0, (newest + 1) * rows, 2 * rows):
            top = jnp.max(scores[held, lanes], axis=0, keepdims=True)
            total = jnp.zeros_like(top)
            for j in range(newest + 1):
                keys = pl.ds(j * rows, rows)
                p = jnp.exp2(scores[keys, lanes] - top)
                total = total + jnp.sum(p, axis=0, keepdims=True)
                scores[keys, lanes] = p
                low[keys, lanes] = p.astype(jnp.bfloat16)
            stats[pl.ds(0, 1), lanes] = top
            stats[pl.ds(1, 1), lanes] = total
            mixed[:, lanes] = dot(vt_all[:, held], low[held, lanes], NN)


def finish_kernel(owned, blocks, rows, bias, stats, mixed, *refs):
    part, refs = refs[0], refs[10:]
    outs, refs = refs[:blocks], refs[blocks:]
    scores, dots, q_all, k_all, v_all, kt_all, vt_all, gt_all, low, grads_low, old_scaled, new_scaled, factors = refs
    head = looked_up(owned, lax.axis_index("head"), lax.axis_index("tm"))
    width = q_all.shape[1]
    scaling = 1.0 / math.sqrt(width)

    @pl.when(head >= 0)
    def _():
        newest = blocks - 1
        at = pl.ds(newest * rows, rows)
        place_block(part, newest, rows, q_all, k_all, v_all, kt_all, vt_all, gt_all)
        pair_products(newest, newest, rows, bias, scores, dots, q_all, k_all, v_all, gt_all)

        def settle(lanes, total, old_factor, weighted):
            inverse = 1.0 / total
            attended = (weighted * inverse).astype(jnp.bfloat16)
            grad_t = gt_all[:, lanes].astype(jnp.float32)
            delta = jnp.sum(grad_t * attended.astype(jnp.float32), axis=0, keepdims=True)
            old = inverse * old_factor
            old_scaled[:, lanes] = (grad_t * old).astype(jnp.bfloat16)
            new_scaled[:, lanes] = (grad_t * inverse).astype(jnp.bfloat16)
            factors[pl.ds(0, 1), lanes] = old
            factors[pl.ds(1, 1), lanes] = delta * old
            factors[pl.ds(2, 1), lanes] = inverse
            factors[pl.ds(3, 1), lanes] = delta * inverse
            for k in range(lanes.size // rows):
                outs[lanes.start // rows + k][0] = attended[:, k * rows : (k + 1) * rows]

        for lanes in lane_chunks(0, newest * rows, 2 * rows):
            fresh = scores[at, lanes]
            before = stats[pl.ds(0, 1), lanes]
            top = jnp.maximum(before, jnp.max(fresh, axis=0, keepdims=True))
            correction = jnp.exp2(before - top)
            p = jnp.exp2(fresh - top)
            p_low = p.astype(jnp.bfloat16)
            scores[at, lanes] = p
            low[at, lanes] = p_low
            total = stats[pl.ds(1, 1), lanes] * correction + jnp.sum(p, axis=0, keepdims=True)
            weighted = mixed[:, lanes] * correction + dot(vt_all[:, at], p_low, NN)
            settle(lanes, total, correction, weighted)
        column = scores[:, at]
        p = jnp.exp2(column - jnp.max(column, axis=0, keepdims=True))
        p_low = p.astype(jnp.bfloat16)
        scores[:, at] = p
        low[:, at] = p_low
        settle(at, jnp.sum(p, axis=0, keepdims=True), 1.0, dot(vt_all[...], p_low, NN))

        for j, out in enumerate(outs):
            keys = pl.ds(j * rows, rows)
            row = 0 if j < newest else 2
            scaled = old_scaled if j < newest else new_scaled
            for lanes in lane_chunks(0, blocks * rows, 4 * rows):
                g = dots[keys, lanes] * factors[pl.ds(row, 1), lanes] - factors[pl.ds(row + 1, 1), lanes]
                grads_low[keys, lanes] = (scores[keys, lanes] * g).astype(jnp.bfloat16)
            out[2] = (dot(grads_low[keys, :], q_all[...], NN) * scaling).astype(jnp.bfloat16)
            out[3] = dot(low[keys, :], scaled[...], NT).astype(jnp.bfloat16)
        for lanes in lane_chunks(0, blocks * rows, 2 * rows):
            grad = (dot(kt_all[...], grads_low[:, lanes], NN) * scaling).astype(jnp.bfloat16)
            for k in range(lanes.size // rows):
                outs[lanes.start // rows + k][1] = grad[:, k * rows : (k + 1) * rows]


def per_device(query, key, value, grad_out, frame_ids, sink_frame, window):
    rows, row_width = query.shape
    heads = window.shape[0]
    width = row_width // heads
    blocks = lax.axis_size("tm")
    owned, sent, partner, pairs = plan(blocks, lax.axis_size("head"), heads)
    axes = ("tm", "head")
    smem = pl.BlockSpec(memory_space=pltpu.SMEM)
    vmem = pl.BlockSpec(memory_space=pltpu.VMEM)
    in_place = pl.BlockSpec(memory_space=pltpu.HBM)
    part = jax.ShapeDtypeStruct((4, rows, width), query.dtype)
    local = jax.ShapeDtypeStruct(query.shape, query.dtype)

    tokens = blocks * rows
    split = tokens <= split_limit
    tiles = 5 if split else 4
    home_tiles = vmem_bytes // (2 * rows * width)
    home, *parts = pl.pallas_call(
        functools.partial(pack_kernel, owned, partner, sent, width),
        out_shape=[jax.ShapeDtypeStruct((home_tiles, rows, width), query.dtype)] + [part] * (blocks - 1),
        in_specs=[in_place] * 7,
        out_specs=[in_place] * blocks,
        scratch_shapes=[
            pltpu.VMEM((4, rows, row_width), query.dtype),
            pltpu.VMEM((tiles, rows, width), query.dtype),
            pltpu.VMEM((blocks - 1, 4, rows, width), query.dtype),
            pltpu.SMEM(frame_ids.shape, jnp.int32),
            pltpu.SMEM(sink_frame.shape, jnp.int32),
            pltpu.SMEM(window.shape, jnp.int32),
            pltpu.SemaphoreType.DMA((7,)),
            pltpu.SemaphoreType.DMA((blocks,)),
        ],
        compiler_params=pltpu.CompilerParams(vmem_limit_bytes=62 * MIB),
        name="pack",
    )(query, key, value, grad_out, frame_ids, sink_frame, window)
    parts = [lax.ppermute(parts[s - 1], axes, pairs[s]) for s in range(1, blocks)]

    stretch = (4 if blocks % 4 == 0 else 2) * rows
    low, full = query.dtype, jnp.float32
    if split:
        square = jax.ShapeDtypeStruct((tokens, tokens), full)
        tall = jax.ShapeDtypeStruct((tokens, width), low)
        wide = jax.ShapeDtypeStruct((width, tokens), low)
        table = jax.ShapeDtypeStruct((blocks, tokens), full)
        held = [square] * 2 + [tall] * 3 + [wide] * 3
        flops = 2 * rows * rows * width
        bias, *state = pl.pallas_call(
            functools.partial(products_kernel, owned, blocks, rows),
            out_shape=[table, *held],
            in_specs=[in_place] + [vmem] * (blocks - 3),
            out_specs=[vmem] * 9,
            scratch_shapes=[pltpu.VMEM((tiles, rows, width), low), pltpu.SemaphoreType.DMA],
            compiler_params=pltpu.CompilerParams(vmem_limit_bytes=20 * MIB),
            cost_estimate=pl.CostEstimate(
                flops=2 * flops * (blocks - 2) ** 2, bytes_accessed=8 * tokens * tokens, transcendentals=0
            ),
            name="products",
        )(home, *parts[:-2])
        *state, weights_low, stats, mixed = pl.pallas_call(
            functools.partial(softmax_kernel, owned, blocks, rows),
            out_shape=[
                *held,
                jax.ShapeDtypeStruct((tokens, tokens), low),
                table,
                jax.ShapeDtypeStruct((width, tokens), full),
            ],
            in_specs=[vmem] * 10,
            out_specs=[vmem] * 11,
            input_output_aliases={2 + n: n for n in range(8)},
            compiler_params=pltpu.CompilerParams(vmem_limit_bytes=20 * MIB),
            cost_estimate=pl.CostEstimate(
                flops=3 * flops * blocks**2, bytes_accessed=8 * tokens * tokens, transcendentals=tokens * tokens
            ),
            name="softmax",
        )(bias, parts[-2], *state)
        parts = pl.pallas_call(
            functools.partial(finish_kernel, owned, blocks, rows),
            out_shape=[part] * blocks + held + [jax.ShapeDtypeStruct((tokens, tokens), low)],
            in_specs=[vmem] * 13,
            out_specs=[vmem] * (blocks + 9),
            input_output_aliases={4 + n: blocks + n for n in range(9)},
            scratch_shapes=[
                pltpu.VMEM((tokens, tokens), low),
                pltpu.VMEM((width, tokens), low),
                pltpu.VMEM((width, tokens), low),
                pltpu.VMEM((8, tokens), full),
            ],
            compiler_params=pltpu.CompilerParams(vmem_limit_bytes=24 * MIB),
            name="finish",
        )(bias, stats, mixed, parts[-1], *state, weights_low)[:blocks]
    else:
        parts = pl.pallas_call(
            functools.partial(head_kernel, owned, partner, rows),
            out_shape=[part] * blocks,
            in_specs=[smem] * 3 + [pl.BlockSpec(memory_space=pl.ANY)] + [vmem] * (blocks - 1),
            out_specs=[vmem] * blocks,
            scratch_shapes=[
                pltpu.VMEM((4, rows, width), low),
                pltpu.VMEM((tokens, width), low),
                pltpu.VMEM((width, tokens), low),
                pltpu.VMEM((width, tokens), low),
                pltpu.VMEM((width, tokens), low),
                pltpu.VMEM((tokens, stretch), full),
                pltpu.VMEM((tokens, stretch), low),
                pltpu.VMEM((tokens, stretch), low),
                pltpu.VMEM((width, stretch), low),
                pltpu.VMEM((tokens, width), full),
                pltpu.VMEM((tokens, width), full),
                pltpu.VMEM((blocks, 2, width, rows), low),
                pltpu.SemaphoreType.DMA,
            ],
            compiler_params=pltpu.CompilerParams(vmem_limit_bytes=48 * MIB),
            name="head_attention",
        )(frame_ids, sink_frame, window, home, *parts)
    back = [[(owner, source) for source, owner in step] for step in pairs]
    parts = [parts[0]] + [lax.ppermute(parts[s], axes, back[s]) for s in range(1, blocks)]

    return pl.pallas_call(
        functools.partial(unpack_kernel, sent, width),
        out_shape=[local] * 4,
        in_specs=[vmem] * blocks,
        out_specs=[vmem] * 4,
        compiler_params=pltpu.CompilerParams(vmem_limit_bytes=24 * MIB),
        name="unpack",
    )(*parts)


def solution(mesh):
    spec = P("tm", "head")
    return jax.shard_map(
        per_device,
        mesh=mesh,
        in_specs=(spec, spec, spec, spec, P(), P(), P("head")),
        out_specs=(spec, spec, spec, spec),
        check_vma=False,
    )
```

```python
import functools
import math

import jax
import jax.numpy as jnp
import numpy as np
from jax import lax
from jax.experimental import pallas as pl
from jax.experimental.pallas import tpu as pltpu
from jax.sharding import PartitionSpec as P

hidden_score = -1e30
MIB = 1 << 20
shared_vmem = 431 << 17
split_limit = 1024


even_rounds = (
    {
        0: (6, 5, 7, 3, 1, 4, 2),
        2: (4, 3, 5, 7, 6, 0, 1),
        3: (0, 6, 4, 5, 2, 1, 7),
        4: (7, 2, 3, 1, 0, 6, 5),
        5: (2, 1, 0, 6, 7, 3, 4),
    },
    {
        2: (5, 6, 7, 1, 0, 4, 3),
        3: (0, 5, 4, 6, 7, 1, 2),
        4: (7, 1, 3, 2, 5, 6, 0),
        5: (3, 4, 2, 0, 1, 7, 6),
        7: (1, 2, 0, 4, 6, 3, 5),
    },
)


def plan(blocks, groups, heads):
    laid_out = []
    for group in range(groups):
        if blocks == 8 and heads == 5:
            laid_out.append(even_rounds[group % 2])
        else:
            owners = [(head * blocks // heads + group % 2) % blocks for head in range(heads)]
            laid_out.append({u: [(u - step) % blocks for step in range(1, blocks)] for u in owners})
    owned = np.full((groups, blocks), -1)
    sent = np.full((blocks, groups, blocks), -1)
    partner = np.full((blocks, groups, blocks), -1)
    pairs = [[] for _ in range(blocks)]
    for group, rounds in enumerate(laid_out):
        for head, (owner, sources) in enumerate(rounds.items()):
            owned[group, owner] = head
            for step, source in enumerate((owner, *sources)):
                sent[step, group, source] = head
                partner[step, group, owner] = source
                pairs[step].append((source * groups + group, owner * groups + group))
    return owned, sent, partner, [sorted(step) for step in pairs]


def looked_up(table, group, block):
    groups, blocks = table.shape
    period = next(p for p in range(1, groups + 1) if (table == table[np.arange(groups) % p]).all())
    bits = int(table.max() + 1).bit_length()
    per_word = 31 // bits
    word = jnp.int32(0)
    for row in range(period):
        for first in range(0, blocks, per_word):
            values = table[row, first : first + per_word] + 1
            packed = sum(int(value) << (bits * n) for n, value in enumerate(values))
            here = (lax.rem(group, period) == row) & (block >= first) & (block < first + per_word)
            word = jnp.where(here, packed, word)
    return ((word >> (bits * lax.rem(block, per_word))) & ((1 << bits) - 1)) - 1


def dot(a, b, contract):
    return lax.dot_general(a, b, (contract, ((), ())), preferred_element_type=jnp.float32)


NN = ((1,), (0,))
NT = ((1,), (1,))


def head_columns(head, width):
    return pl.ds(pl.multiple_of(head * width, width), width)


def pack_kernel(sent, width, query, key, value, grad_out, *refs):
    outs, (staged, sems) = refs[:-2], refs[-2:]
    group, block = lax.axis_index("head"), lax.axis_index("tm")
    arrays = (query, key, value, grad_out)
    loads = [pltpu.make_async_copy(a, staged.at[n], sems.at[n]) for n, a in enumerate(arrays)]
    for load in loads:
        load.start()
    heads = [looked_up(table, group, block) for table in sent]
    for load in loads:
        load.wait()
    for out, head in zip(outs, heads):

        @pl.when(head >= 0)
        def _():
            columns = head_columns(head, width)
            for n in range(3):
                out[n] = staged[n, :, columns]
            out[3] = staged[3, :, columns].T


def unpack_kernel(sent, width, *refs):
    parts, (attended, query_grad, key_grad, value_grad) = refs[:-4], refs[-4:]
    group, block = lax.axis_index("head"), lax.axis_index("tm")
    for step, part in enumerate(parts):
        head = looked_up(sent[step], group, block)

        @pl.when(head >= 0)
        def _():
            columns = head_columns(head, width)
            attended[:, columns] = part[0].T
            query_grad[:, columns] = part[1].T
            key_grad[:, columns] = part[2]
            value_grad[:, columns] = part[3]


def head_kernel(owned, partner, rows, frame_ids, sink_frame, window, local, *refs):
    blocks = len(partner)
    parts, outs, scratch = refs[: blocks - 1], refs[blocks - 1 : 2 * blocks - 1], refs[2 * blocks - 1 :]
    (here, q_all, kt_all, vt_all, gt_all, weights, weights_low, grads_low, grad_scaled, dk, dv, res, sem) = scratch
    parts = (here, *parts)
    group, block = lax.axis_index("head"), lax.axis_index("tm")
    head = looked_up(owned, group, block)
    width = q_all.shape[1]
    scaling = 1.0 / math.sqrt(width)
    rescale = scaling * math.log2(math.e)
    stretch = weights.shape[1]
    half = stretch // 2
    each = half // rows

    @pl.when(head >= 0)
    def _():
        fetch = pltpu.make_async_copy(local, here, sem)
        fetch.start()
        span = window[head]
        sink = sink_frame[0]
        frames = [frame_ids[looked_up(table, group, block)] for table in partner]

        def placed(j):
            at = pl.ds(j * rows, rows)
            q_all[at, :] = parts[j][0]
            kt_all[:, at] = parts[j][1].T
            vt_all[:, at] = parts[j][2].T
            gt_all[:, at] = parts[j][3]

        for j in range(1, blocks):
            placed(j)
        fetch.wait()
        placed(0)
        dk[...] = jnp.zeros_like(dk)
        dv[...] = jnp.zeros_like(dv)
        lane_block = lax.broadcasted_iota(jnp.int32, (1, half), 1) // rows

        def one_stretch(i, carry):
            at = [pl.ds(pl.multiple_of(i * stretch + h * half, half), half) for h in range(2)]
            lanes = [pl.ds(h * half, half) for h in range(2)]
            keys = [pl.ds(j * rows, rows) for j in range(blocks)]
            q_rows = [q_all[at[h], :] for h in range(2)]
            top = [jnp.full((1, half), hidden_score, jnp.float32)] * 2
            total = [jnp.zeros((1, half), jnp.float32)] * 2
            delta = [None] * 2
            own = [[], []]
            for h in range(2):
                for k in range(each):
                    n = i * 2 * each + h * each + k
                    own[h].append(sum(jnp.where(n == j, frames[j], 0) for j in range(blocks)))

            def score(h, j):
                bias = jnp.zeros((1, half), jnp.float32)
                for k in range(each):
                    seen = (frames[j] <= own[h][k]) & (frames[j] > own[h][k] - span)
                    seen = seen | ((frames[j] == sink) & (sink <= own[h][k]))
                    bias = jnp.where(lane_block == k, jnp.where(seen, 0.0, hidden_score), bias)
                scores = dot(parts[j][1], q_rows[h], NT) * rescale + bias
                weights[keys[j], lanes[h]] = scores
                top[h] = jnp.maximum(top[h], jnp.max(scores, axis=0, keepdims=True))

            def weigh(h, j):
                p = jnp.exp2(weights[keys[j], lanes[h]] - top[h])
                total[h] = total[h] + jnp.sum(p, axis=0, keepdims=True)
                weights[keys[j], lanes[h]] = p
                weights_low[keys[j], lanes[h]] = p.astype(jnp.bfloat16)

            def attend(h):
                inverse = 1.0 / total[h]
                mixed = (dot(vt_all[...], weights_low[:, lanes[h]], NN) * inverse).astype(jnp.bfloat16)
                grad_t = gt_all[:, at[h]].astype(jnp.float32)
                delta[h] = jnp.sum(grad_t * mixed.astype(jnp.float32), axis=0, keepdims=True) * inverse
                grad_scaled[:, lanes[h]] = (grad_t * inverse).astype(jnp.bfloat16)
                for k in range(each):
                    res[i * 2 * each + h * each + k, 0] = mixed[:, k * rows : (k + 1) * rows]

            def differ(h, j):
                g = dot(parts[j][2], grad_scaled[:, lanes[h]], NN) - delta[h]
                grads_low[keys[j], lanes[h]] = (weights[keys[j], lanes[h]] * g).astype(jnp.bfloat16)

            def query_part(h):
                grad = (dot(kt_all[...], grads_low[:, lanes[h]], NN) * scaling).astype(jnp.bfloat16)
                for k in range(each):
                    res[i * 2 * each + h * each + k, 1] = grad[:, k * rows : (k + 1) * rows]

            for j in range(blocks):
                score(0, j)
            for j in range(blocks):
                score(1, j)
                weigh(0, j)
            attend(0)
            for j in range(blocks):
                weigh(1, j)
                differ(0, j)
            attend(1)
            query_part(0)
            q_both = jnp.concatenate(q_rows, axis=0)
            for j in range(blocks):
                differ(1, j)
                dk[keys[j], :] += dot(grads_low[keys[j], :], q_both, NN)
                dv[keys[j], :] += dot(weights_low[keys[j], :], grad_scaled[...], NT)
            query_part(1)
            return carry

        lax.fori_loop(0, blocks * rows // stretch, one_stretch, 0)
        for j, out in enumerate(outs):
            at = pl.ds(j * rows, rows)
            out[0] = res[j, 0]
            out[1] = res[j, 1]
            out[2] = (dk[at, :] * scaling).astype(jnp.bfloat16)
            out[3] = dv[at, :].astype(jnp.bfloat16)


def seen_bias(frame, own, span, sink):
    seen = ((frame <= own) & (frame > own - span)) | ((frame == sink) & (sink <= own))
    return jnp.where(seen, 0.0, hidden_score)


def frames_by_lane(frames, rows):
    lane_block = lax.broadcasted_iota(jnp.int32, (1, len(frames) * rows), 1) // rows
    row = jnp.zeros_like(lane_block)
    for n, frame in enumerate(frames):
        row = jnp.where(lane_block == n, frame, row)
    return row


def place_block(part, j, rows, q_all, k_all, v_all, kt_all, vt_all, gt_all):
    at = pl.ds(j * rows, rows)
    q_all[at, :] = part[0]
    k_all[at, :] = part[1]
    v_all[at, :] = part[2]
    kt_all[:, at] = part[1].T
    vt_all[:, at] = part[2].T
    gt_all[:, at] = part[3]


def pair_products(j, held, rows, bias, scores, dots, q_all, k_all, v_all, gt_all):
    width = q_all.shape[1]
    rescale = math.log2(math.e) / math.sqrt(width)
    before = held * rows
    at = pl.ds(j * rows, rows)
    every = pl.ds(0, before + rows)
    scores[at, every] = dot(k_all[at, :], q_all[every, :], NT) * rescale + bias[pl.ds(j, 1), every]
    dots[at, every] = dot(v_all[at, :], gt_all[:, every], NN)
    column = dot(k_all[pl.ds(0, before), :], q_all[at, :], NT) * rescale
    for n in range(held):
        keys = pl.ds(n * rows, rows)
        scores[keys, at] = column[n * rows : (n + 1) * rows, :] + bias[pl.ds(n, 1), at]
    dots[pl.ds(0, before), at] = dot(v_all[pl.ds(0, before), :], gt_all[:, at], NN)


def lane_chunks(start, stop, size):
    return [pl.ds(first, min(size, stop - first)) for first in range(start, stop, size)]


def products_kernel(owned, partner, rows, frame_ids, sink_frame, window, *refs):
    blocks = len(partner)
    held = blocks - 2
    parts, (bias, scores, dots, *places) = refs[:held], refs[held:]
    group, block = lax.axis_index("head"), lax.axis_index("tm")
    head = looked_up(owned, group, block)

    @pl.when(head >= 0)
    def _():
        span = window[head]
        sink = sink_frame[0]
        frames = [frame_ids[looked_up(table, group, block)] for table in partner]
        every = frames_by_lane(frames, rows)
        for j in range(blocks):
            bias[pl.ds(j, 1), :] = seen_bias(frames[j], every, span, sink)
        for j in range(held):
            place_block(parts[j], j, rows, *places)
        q_all, k_all, v_all, _, _, gt_all = places
        lanes = pl.ds(0, held * rows)
        rescale = math.log2(math.e) / math.sqrt(q_all.shape[1])
        for j in range(held):
            keys = pl.ds(j * rows, rows)
            scores[keys, lanes] = dot(parts[j][1], q_all[lanes, :], NT) * rescale + bias[pl.ds(j, 1), lanes]
            dots[keys, lanes] = dot(parts[j][2], gt_all[:, lanes], NN)


def softmax_kernel(owned, blocks, rows, bias, *refs):
    part, refs = refs[0], refs[9:]
    scores, dots, q_all, k_all, v_all, kt_all, vt_all, gt_all, low, stats, mixed = refs
    head = looked_up(owned, lax.axis_index("head"), lax.axis_index("tm"))

    @pl.when(head >= 0)
    def _():
        newest = blocks - 2
        held = pl.ds(0, (newest + 1) * rows)
        place_block(part, newest, rows, q_all, k_all, v_all, kt_all, vt_all, gt_all)
        pair_products(newest, newest, rows, bias, scores, dots, q_all, k_all, v_all, gt_all)
        for lanes in lane_chunks(0, (newest + 1) * rows, 2 * rows):
            top = jnp.max(scores[held, lanes], axis=0, keepdims=True)
            total = jnp.zeros_like(top)
            for j in range(newest + 1):
                keys = pl.ds(j * rows, rows)
                p = jnp.exp2(scores[keys, lanes] - top)
                total = total + jnp.sum(p, axis=0, keepdims=True)
                scores[keys, lanes] = p
                low[keys, lanes] = p.astype(jnp.bfloat16)
            stats[pl.ds(0, 1), lanes] = top
            stats[pl.ds(1, 1), lanes] = total
            mixed[:, lanes] = dot(vt_all[:, held], low[held, lanes], NN)


def finish_kernel(owned, blocks, rows, bias, stats, mixed, *refs):
    part, refs = refs[0], refs[10:]
    outs, refs = refs[:blocks], refs[blocks:]
    scores, dots, q_all, k_all, v_all, kt_all, vt_all, gt_all, low, grads_low, old_scaled, new_scaled, factors = refs
    head = looked_up(owned, lax.axis_index("head"), lax.axis_index("tm"))
    width = q_all.shape[1]
    scaling = 1.0 / math.sqrt(width)

    @pl.when(head >= 0)
    def _():
        newest = blocks - 1
        at = pl.ds(newest * rows, rows)
        place_block(part, newest, rows, q_all, k_all, v_all, kt_all, vt_all, gt_all)
        pair_products(newest, newest, rows, bias, scores, dots, q_all, k_all, v_all, gt_all)

        def settle(lanes, total, old_factor, weighted):
            inverse = 1.0 / total
            attended = (weighted * inverse).astype(jnp.bfloat16)
            grad_t = gt_all[:, lanes].astype(jnp.float32)
            delta = jnp.sum(grad_t * attended.astype(jnp.float32), axis=0, keepdims=True)
            old = inverse * old_factor
            old_scaled[:, lanes] = (grad_t * old).astype(jnp.bfloat16)
            new_scaled[:, lanes] = (grad_t * inverse).astype(jnp.bfloat16)
            factors[pl.ds(0, 1), lanes] = old
            factors[pl.ds(1, 1), lanes] = delta * old
            factors[pl.ds(2, 1), lanes] = inverse
            factors[pl.ds(3, 1), lanes] = delta * inverse
            for k in range(lanes.size // rows):
                outs[lanes.start // rows + k][0] = attended[:, k * rows : (k + 1) * rows]

        for lanes in lane_chunks(0, newest * rows, 2 * rows):
            fresh = scores[at, lanes]
            before = stats[pl.ds(0, 1), lanes]
            top = jnp.maximum(before, jnp.max(fresh, axis=0, keepdims=True))
            correction = jnp.exp2(before - top)
            p = jnp.exp2(fresh - top)
            p_low = p.astype(jnp.bfloat16)
            scores[at, lanes] = p
            low[at, lanes] = p_low
            total = stats[pl.ds(1, 1), lanes] * correction + jnp.sum(p, axis=0, keepdims=True)
            weighted = mixed[:, lanes] * correction + dot(vt_all[:, at], p_low, NN)
            settle(lanes, total, correction, weighted)
        column = scores[:, at]
        p = jnp.exp2(column - jnp.max(column, axis=0, keepdims=True))
        p_low = p.astype(jnp.bfloat16)
        scores[:, at] = p
        low[:, at] = p_low
        settle(at, jnp.sum(p, axis=0, keepdims=True), 1.0, dot(vt_all[...], p_low, NN))

        for j, out in enumerate(outs):
            keys = pl.ds(j * rows, rows)
            row = 0 if j < newest else 2
            scaled = old_scaled if j < newest else new_scaled
            for lanes in lane_chunks(0, blocks * rows, 4 * rows):
                g = dots[keys, lanes] * factors[pl.ds(row, 1), lanes] - factors[pl.ds(row + 1, 1), lanes]
                grads_low[keys, lanes] = (scores[keys, lanes] * g).astype(jnp.bfloat16)
            out[2] = (dot(grads_low[keys, :], q_all[...], NN) * scaling).astype(jnp.bfloat16)
            out[3] = dot(low[keys, :], scaled[...], NT).astype(jnp.bfloat16)
        for lanes in lane_chunks(0, blocks * rows, 2 * rows):
            grad = (dot(kt_all[...], grads_low[:, lanes], NN) * scaling).astype(jnp.bfloat16)
            for k in range(lanes.size // rows):
                outs[lanes.start // rows + k][1] = grad[:, k * rows : (k + 1) * rows]


def per_device(query, key, value, grad_out, frame_ids, sink_frame, window):
    rows, row_width = query.shape
    heads = window.shape[0]
    width = row_width // heads
    blocks = lax.axis_size("tm")
    owned, sent, partner, pairs = plan(blocks, lax.axis_size("head"), heads)
    axes = ("tm", "head")
    smem = pl.BlockSpec(memory_space=pltpu.SMEM)
    vmem = pl.BlockSpec(memory_space=pltpu.VMEM)
    in_place = pl.BlockSpec(memory_space=pltpu.HBM)
    part = jax.ShapeDtypeStruct((4, rows, width), query.dtype)
    local = jax.ShapeDtypeStruct(query.shape, query.dtype)

    parts = pl.pallas_call(
        functools.partial(pack_kernel, sent, width),
        out_shape=[part] * blocks,
        in_specs=[in_place] * 4,
        out_specs=[vmem] * blocks,
        scratch_shapes=[pltpu.VMEM((4, rows, row_width), query.dtype), pltpu.SemaphoreType.DMA((4,))],
        compiler_params=pltpu.CompilerParams(vmem_limit_bytes=shared_vmem - blocks * 8 * rows * width),
        name="pack",
    )(query, key, value, grad_out)
    parts = [parts[0]] + [lax.ppermute(parts[s], axes, pairs[s]) for s in range(1, blocks)]

    tokens = blocks * rows
    stretch = (4 if blocks % 4 == 0 else 2) * rows
    low, full = query.dtype, jnp.float32
    if tokens <= split_limit:
        square = jax.ShapeDtypeStruct((tokens, tokens), full)
        tall = jax.ShapeDtypeStruct((tokens, width), low)
        wide = jax.ShapeDtypeStruct((width, tokens), low)
        table = jax.ShapeDtypeStruct((blocks, tokens), full)
        held = [square] * 2 + [tall] * 3 + [wide] * 3
        flops = 2 * rows * rows * width
        bias, *state = pl.pallas_call(
            functools.partial(products_kernel, owned, partner, rows),
            out_shape=[table, *held],
            in_specs=[smem] * 3 + [vmem] * (blocks - 2),
            out_specs=[vmem] * 9,
            compiler_params=pltpu.CompilerParams(vmem_limit_bytes=20 * MIB),
            cost_estimate=pl.CostEstimate(
                flops=2 * flops * (blocks - 2) ** 2, bytes_accessed=8 * tokens * tokens, transcendentals=0
            ),
            name="products",
        )(frame_ids, sink_frame, window, *parts[:-2])
        *state, weights_low, stats, mixed = pl.pallas_call(
            functools.partial(softmax_kernel, owned, blocks, rows),
            out_shape=[
                *held,
                jax.ShapeDtypeStruct((tokens, tokens), low),
                table,
                jax.ShapeDtypeStruct((width, tokens), full),
            ],
            in_specs=[vmem] * 10,
            out_specs=[vmem] * 11,
            input_output_aliases={2 + n: n for n in range(8)},
            compiler_params=pltpu.CompilerParams(vmem_limit_bytes=20 * MIB),
            cost_estimate=pl.CostEstimate(
                flops=3 * flops * blocks**2, bytes_accessed=8 * tokens * tokens, transcendentals=tokens * tokens
            ),
            name="softmax",
        )(bias, parts[-2], *state)
        parts = pl.pallas_call(
            functools.partial(finish_kernel, owned, blocks, rows),
            out_shape=[part] * blocks + held + [jax.ShapeDtypeStruct((tokens, tokens), low)],
            in_specs=[vmem] * 13,
            out_specs=[vmem] * (blocks + 9),
            input_output_aliases={4 + n: blocks + n for n in range(9)},
            scratch_shapes=[
                pltpu.VMEM((tokens, tokens), low),
                pltpu.VMEM((width, tokens), low),
                pltpu.VMEM((width, tokens), low),
                pltpu.VMEM((8, tokens), full),
            ],
            compiler_params=pltpu.CompilerParams(vmem_limit_bytes=24 * MIB),
            name="finish",
        )(bias, stats, mixed, parts[-1], *state, weights_low)[:blocks]
    else:
        parts = pl.pallas_call(
            functools.partial(head_kernel, owned, partner, rows),
            out_shape=[part] * blocks,
            in_specs=[smem] * 3 + [pl.BlockSpec(memory_space=pl.ANY)] + [vmem] * (blocks - 1),
            out_specs=[vmem] * blocks,
            scratch_shapes=[
                pltpu.VMEM((4, rows, width), low),
                pltpu.VMEM((tokens, width), low),
                pltpu.VMEM((width, tokens), low),
                pltpu.VMEM((width, tokens), low),
                pltpu.VMEM((width, tokens), low),
                pltpu.VMEM((tokens, stretch), full),
                pltpu.VMEM((tokens, stretch), low),
                pltpu.VMEM((tokens, stretch), low),
                pltpu.VMEM((width, stretch), low),
                pltpu.VMEM((tokens, width), full),
                pltpu.VMEM((tokens, width), full),
                pltpu.VMEM((blocks, 2, width, rows), low),
                pltpu.SemaphoreType.DMA,
            ],
            compiler_params=pltpu.CompilerParams(vmem_limit_bytes=48 * MIB),
            name="head_attention",
        )(frame_ids, sink_frame, window, *parts)
    back = [[(owner, source) for source, owner in step] for step in pairs]
    parts = [parts[0]] + [lax.ppermute(parts[s], axes, back[s]) for s in range(1, blocks)]

    return pl.pallas_call(
        functools.partial(unpack_kernel, sent, width),
        out_shape=[local] * 4,
        in_specs=[vmem] * blocks,
        out_specs=[vmem] * 4,
        compiler_params=pltpu.CompilerParams(vmem_limit_bytes=24 * MIB),
        name="unpack",
    )(*parts)


def solution(mesh):
    spec = P("tm", "head")
    return jax.shard_map(
        per_device,
        mesh=mesh,
        in_specs=(spec, spec, spec, spec, P(), P(), P("head")),
        out_specs=(spec, spec, spec, spec),
        check_vma=False,
    )
```

```python
import functools
import math

import jax
import jax.numpy as jnp
import numpy as np
from jax import lax
from jax.experimental import pallas as pl
from jax.experimental.pallas import tpu as pltpu
from jax.sharding import PartitionSpec as P

hidden_score = -1e30
MIB = 1 << 20
vmem_bytes = 64 * MIB
split_limit = 1024


even_rounds = (
    {
        1: (4, 6, 3, 2, 7, 0, 5),
        2: (3, 7, 5, 6, 1, 4, 0),
        3: (2, 0, 4, 5, 6, 7, 1),
        4: (7, 3, 2, 1, 0, 5, 6),
        5: (1, 2, 6, 0, 4, 3, 7),
    },
    {
        0: (5, 7, 6, 3, 1, 2, 4),
        1: (6, 4, 5, 7, 2, 3, 0),
        4: (0, 1, 7, 2, 5, 6, 3),
        6: (2, 5, 1, 4, 3, 0, 7),
        7: (3, 2, 0, 1, 4, 5, 6),
    },
)


def plan(blocks, groups, heads):
    laid_out = []
    for group in range(groups):
        if blocks == 8 and heads == 5:
            laid_out.append(even_rounds[group % 2])
        else:
            owners = [(head * blocks // heads + group % 2) % blocks for head in range(heads)]
            laid_out.append({u: [(u - step) % blocks for step in range(1, blocks)] for u in owners})
    owned = np.full((groups, blocks), -1)
    sent = np.full((blocks, groups, blocks), -1)
    partner = np.full((blocks, groups, blocks), -1)
    pairs = [[] for _ in range(blocks)]
    for group, rounds in enumerate(laid_out):
        for head, (owner, sources) in enumerate(rounds.items()):
            owned[group, owner] = head
            for step, source in enumerate((owner, *sources)):
                sent[step, group, source] = head
                partner[step, group, owner] = source
                pairs[step].append((source * groups + group, owner * groups + group))
    return owned, sent, partner, [sorted(step) for step in pairs]


def looked_up(table, group, block):
    groups, blocks = table.shape
    period = next(p for p in range(1, groups + 1) if (table == table[np.arange(groups) % p]).all())
    bits = int(table.max() + 1).bit_length()
    per_word = 31 // bits
    word = jnp.int32(0)
    for row in range(period):
        for first in range(0, blocks, per_word):
            values = table[row, first : first + per_word] + 1
            packed = sum(int(value) << (bits * n) for n, value in enumerate(values))
            here = (lax.rem(group, period) == row) & (block >= first) & (block < first + per_word)
            word = jnp.where(here, packed, word)
    return ((word >> (bits * lax.rem(block, per_word))) & ((1 << bits) - 1)) - 1


def dot(a, b, contract):
    return lax.dot_general(a, b, (contract, ((), ())), preferred_element_type=jnp.float32)


NN = ((1,), (0,))
NT = ((1,), (1,))


def head_columns(head, width):
    return pl.ds(pl.multiple_of(head * width, width), width)


def pack_kernel(owned, partner, sent, width, query, key, value, grad_out, frame_ids, sink_frame, window, *refs):
    blocks = len(sent)
    home, outs, refs = refs[0], refs[1:blocks], refs[blocks:]
    staged, tiles, packed, frames_here, sink_here, window_here, in_sems, out_sems = refs
    group, block = lax.axis_index("head"), lax.axis_index("tm")
    arrays = (query, key, value, grad_out)
    loads = [pltpu.make_async_copy(a, staged.at[n], in_sems.at[n]) for n, a in enumerate(arrays)]
    small = ((frame_ids, frames_here), (sink_frame, sink_here), (window, window_here))
    loads += [pltpu.make_async_copy(a, here, in_sems.at[4 + n]) for n, (a, here) in enumerate(small)]
    for load in loads:
        load.start()
    heads = [looked_up(table, group, block) for table in sent]
    stores = [pltpu.make_async_copy(packed.at[n], out, out_sems.at[1 + n]) for n, out in enumerate(outs)]
    keep = pltpu.make_async_copy(tiles, home.at[pl.ds(0, tiles.shape[0])], out_sems.at[0])
    for load in loads:
        load.wait()

    def fill(target, head):
        columns = head_columns(head, width)
        for n in range(3):
            target[n] = staged[n, :, columns]
        target[3] = staged[3, :, columns].T

    for step, head in enumerate(heads[1:]):

        @pl.when(head >= 0)
        def _():
            fill(packed.at[step], head)
            stores[step].start()

    @pl.when(heads[0] >= 0)
    def _():
        fill(tiles, heads[0])
        if tiles.shape[0] > 4:
            frames = [frames_here[looked_up(table, group, block)] for table in partner]
            row = lax.broadcasted_iota(jnp.int32, tiles.shape[1:], 0)
            theirs, own = jnp.zeros_like(row), jnp.zeros_like(row)
            for n, frame in enumerate(frames):
                theirs = jnp.where(row // blocks == n, frame, theirs)
                own = jnp.where(lax.rem(row, blocks) == n, frame, own)
            tiles[4] = seen_bias(theirs, own, window_here[heads[0]], sink_here[0]).astype(tiles.dtype)
        keep.start()

    for step, head in enumerate(heads[1:]):

        @pl.when(head >= 0)
        def _():
            stores[step].wait()

    @pl.when(heads[0] >= 0)
    def _():
        keep.wait()


def unpack_kernel(sent, width, *refs):
    parts, (attended, query_grad, key_grad, value_grad) = refs[:-4], refs[-4:]
    group, block = lax.axis_index("head"), lax.axis_index("tm")
    for step, part in enumerate(parts):
        head = looked_up(sent[step], group, block)

        @pl.when(head >= 0)
        def _():
            columns = head_columns(head, width)
            attended[:, columns] = part[0].T
            query_grad[:, columns] = part[1].T
            key_grad[:, columns] = part[2]
            value_grad[:, columns] = part[3]


def head_kernel(owned, partner, rows, frame_ids, sink_frame, window, local, *refs):
    blocks = len(partner)
    parts, outs, scratch = refs[: blocks - 1], refs[blocks - 1 : 2 * blocks - 1], refs[2 * blocks - 1 :]
    (here, q_all, kt_all, vt_all, gt_all, weights, weights_low, grads_low, grad_scaled, dk, dv, res, sem) = scratch
    parts = (here, *parts)
    group, block = lax.axis_index("head"), lax.axis_index("tm")
    head = looked_up(owned, group, block)
    width = q_all.shape[1]
    scaling = 1.0 / math.sqrt(width)
    rescale = scaling * math.log2(math.e)
    stretch = weights.shape[1]
    half = stretch // 2
    each = half // rows

    @pl.when(head >= 0)
    def _():
        fetch = pltpu.make_async_copy(local.at[pl.ds(0, 4)], here, sem)
        fetch.start()
        span = window[head]
        sink = sink_frame[0]
        frames = [frame_ids[looked_up(table, group, block)] for table in partner]

        def placed(j):
            at = pl.ds(j * rows, rows)
            q_all[at, :] = parts[j][0]
            kt_all[:, at] = parts[j][1].T
            vt_all[:, at] = parts[j][2].T
            gt_all[:, at] = parts[j][3]

        for j in range(1, blocks):
            placed(j)
        fetch.wait()
        placed(0)
        dk[...] = jnp.zeros_like(dk)
        dv[...] = jnp.zeros_like(dv)
        lane_block = lax.broadcasted_iota(jnp.int32, (1, half), 1) // rows

        def one_stretch(i, carry):
            at = [pl.ds(pl.multiple_of(i * stretch + h * half, half), half) for h in range(2)]
            lanes = [pl.ds(h * half, half) for h in range(2)]
            keys = [pl.ds(j * rows, rows) for j in range(blocks)]
            q_rows = [q_all[at[h], :] for h in range(2)]
            top = [jnp.full((1, half), hidden_score, jnp.float32)] * 2
            total = [jnp.zeros((1, half), jnp.float32)] * 2
            delta = [None] * 2
            own = [[], []]
            for h in range(2):
                for k in range(each):
                    n = i * 2 * each + h * each + k
                    own[h].append(sum(jnp.where(n == j, frames[j], 0) for j in range(blocks)))

            def score(h, j):
                bias = jnp.zeros((1, half), jnp.float32)
                for k in range(each):
                    seen = (frames[j] <= own[h][k]) & (frames[j] > own[h][k] - span)
                    seen = seen | ((frames[j] == sink) & (sink <= own[h][k]))
                    bias = jnp.where(lane_block == k, jnp.where(seen, 0.0, hidden_score), bias)
                scores = dot(parts[j][1], q_rows[h], NT) * rescale + bias
                weights[keys[j], lanes[h]] = scores
                top[h] = jnp.maximum(top[h], jnp.max(scores, axis=0, keepdims=True))

            def weigh(h, j):
                p = jnp.exp2(weights[keys[j], lanes[h]] - top[h])
                total[h] = total[h] + jnp.sum(p, axis=0, keepdims=True)
                weights[keys[j], lanes[h]] = p
                weights_low[keys[j], lanes[h]] = p.astype(jnp.bfloat16)

            def attend(h):
                inverse = 1.0 / total[h]
                mixed = (dot(vt_all[...], weights_low[:, lanes[h]], NN) * inverse).astype(jnp.bfloat16)
                grad_t = gt_all[:, at[h]].astype(jnp.float32)
                delta[h] = jnp.sum(grad_t * mixed.astype(jnp.float32), axis=0, keepdims=True) * inverse
                grad_scaled[:, lanes[h]] = (grad_t * inverse).astype(jnp.bfloat16)
                for k in range(each):
                    res[i * 2 * each + h * each + k, 0] = mixed[:, k * rows : (k + 1) * rows]

            def differ(h, j):
                g = dot(parts[j][2], grad_scaled[:, lanes[h]], NN) - delta[h]
                grads_low[keys[j], lanes[h]] = (weights[keys[j], lanes[h]] * g).astype(jnp.bfloat16)

            def query_part(h):
                grad = (dot(kt_all[...], grads_low[:, lanes[h]], NN) * scaling).astype(jnp.bfloat16)
                for k in range(each):
                    res[i * 2 * each + h * each + k, 1] = grad[:, k * rows : (k + 1) * rows]

            for j in range(blocks):
                score(0, j)
            for j in range(blocks):
                score(1, j)
                weigh(0, j)
            attend(0)
            for j in range(blocks):
                weigh(1, j)
                differ(0, j)
            attend(1)
            query_part(0)
            q_both = jnp.concatenate(q_rows, axis=0)
            for j in range(blocks):
                differ(1, j)
                dk[keys[j], :] += dot(grads_low[keys[j], :], q_both, NN)
                dv[keys[j], :] += dot(weights_low[keys[j], :], grad_scaled[...], NT)
            query_part(1)
            return carry

        lax.fori_loop(0, blocks * rows // stretch, one_stretch, 0)
        for j, out in enumerate(outs):
            at = pl.ds(j * rows, rows)
            out[0] = res[j, 0]
            out[1] = res[j, 1]
            out[2] = (dk[at, :] * scaling).astype(jnp.bfloat16)
            out[3] = dv[at, :].astype(jnp.bfloat16)


def seen_bias(frame, own, span, sink):
    seen = ((frame <= own) & (frame > own - span)) | ((frame == sink) & (sink <= own))
    return jnp.where(seen, 0.0, hidden_score)


def frames_by_lane(frames, rows):
    lane_block = lax.broadcasted_iota(jnp.int32, (1, len(frames) * rows), 1) // rows
    row = jnp.zeros_like(lane_block)
    for n, frame in enumerate(frames):
        row = jnp.where(lane_block == n, frame, row)
    return row


def place_block(part, j, rows, q_all, k_all, v_all, kt_all, vt_all, gt_all):
    at = pl.ds(j * rows, rows)
    q_all[at, :] = part[0]
    k_all[at, :] = part[1]
    v_all[at, :] = part[2]
    kt_all[:, at] = part[1].T
    vt_all[:, at] = part[2].T
    gt_all[:, at] = part[3]


def pair_products(j, held, rows, bias, scores, dots, q_all, k_all, v_all, gt_all):
    width = q_all.shape[1]
    rescale = math.log2(math.e) / math.sqrt(width)
    before = held * rows
    at = pl.ds(j * rows, rows)
    every = pl.ds(0, before + rows)
    scores[at, every] = dot(k_all[at, :], q_all[every, :], NT) * rescale + bias[pl.ds(j, 1), every]
    dots[at, every] = dot(v_all[at, :], gt_all[:, every], NN)
    column = dot(k_all[pl.ds(0, before), :], q_all[at, :], NT) * rescale
    for n in range(held):
        keys = pl.ds(n * rows, rows)
        scores[keys, at] = column[n * rows : (n + 1) * rows, :] + bias[pl.ds(n, 1), at]
    dots[pl.ds(0, before), at] = dot(v_all[pl.ds(0, before), :], gt_all[:, at], NN)


def lane_chunks(start, stop, size):
    return [pl.ds(first, min(size, stop - first)) for first in range(start, stop, size)]


def products_kernel(owned, blocks, rows, home, *refs):
    held = blocks - 2
    parts, refs = refs[: held - 1], refs[held - 1 :]
    bias, scores, dots, *places, tiles, sem = refs
    head = looked_up(owned, lax.axis_index("head"), lax.axis_index("tm"))

    @pl.when(head >= 0)
    def _():
        fetch = pltpu.make_async_copy(home.at[pl.ds(0, tiles.shape[0])], tiles, sem)
        fetch.start()
        for j, part in enumerate(parts):
            place_block(part, j + 1, rows, *places)
        fetch.wait()
        place_block(tiles, 0, rows, *places)
        mask = tiles[4].astype(jnp.float32)
        for j in range(blocks):
            for n in range(blocks):
                row = j * blocks + n
                bias[pl.ds(j, 1), pl.ds(n * rows, rows)] = mask[row : row + 1, :]
        q_all, k_all, v_all, _, _, gt_all = places
        lanes = pl.ds(0, held * rows)
        rescale = math.log2(math.e) / math.sqrt(q_all.shape[1])
        for j in range(held):
            keys = pl.ds(j * rows, rows)
            scores[keys, lanes] = dot(k_all[keys, :], q_all[lanes, :], NT) * rescale + bias[pl.ds(j, 1), lanes]
            dots[keys, lanes] = dot(v_all[keys, :], gt_all[:, lanes], NN)


def softmax_kernel(owned, blocks, rows, bias, *refs):
    part, refs = refs[0], refs[9:]
    scores, dots, q_all, k_all, v_all, kt_all, vt_all, gt_all, low, stats, mixed = refs
    head = looked_up(owned, lax.axis_index("head"), lax.axis_index("tm"))

    @pl.when(head >= 0)
    def _():
        newest = blocks - 2
        held = pl.ds(0, (newest + 1) * rows)
        place_block(part, newest, rows, q_all, k_all, v_all, kt_all, vt_all, gt_all)
        pair_products(newest, newest, rows, bias, scores, dots, q_all, k_all, v_all, gt_all)
        for lanes in lane_chunks(0, (newest + 1) * rows, 2 * rows):
            top = jnp.max(scores[held, lanes], axis=0, keepdims=True)
            total = jnp.zeros_like(top)
            for j in range(newest + 1):
                keys = pl.ds(j * rows, rows)
                p = jnp.exp2(scores[keys, lanes] - top)
                total = total + jnp.sum(p, axis=0, keepdims=True)
                scores[keys, lanes] = p
                low[keys, lanes] = p.astype(jnp.bfloat16)
            stats[pl.ds(0, 1), lanes] = top
            stats[pl.ds(1, 1), lanes] = total
            mixed[:, lanes] = dot(vt_all[:, held], low[held, lanes], NN)


def finish_kernel(owned, blocks, rows, bias, stats, mixed, *refs):
    part, refs = refs[0], refs[10:]
    outs, refs = refs[:blocks], refs[blocks:]
    scores, dots, q_all, k_all, v_all, kt_all, vt_all, gt_all, low, grads_low, old_scaled, new_scaled, factors = refs
    head = looked_up(owned, lax.axis_index("head"), lax.axis_index("tm"))
    width = q_all.shape[1]
    scaling = 1.0 / math.sqrt(width)

    @pl.when(head >= 0)
    def _():
        newest = blocks - 1
        at = pl.ds(newest * rows, rows)
        place_block(part, newest, rows, q_all, k_all, v_all, kt_all, vt_all, gt_all)
        pair_products(newest, newest, rows, bias, scores, dots, q_all, k_all, v_all, gt_all)

        def settle(lanes, total, old_factor, weighted):
            inverse = 1.0 / total
            attended = (weighted * inverse).astype(jnp.bfloat16)
            grad_t = gt_all[:, lanes].astype(jnp.float32)
            delta = jnp.sum(grad_t * attended.astype(jnp.float32), axis=0, keepdims=True)
            old = inverse * old_factor
            old_scaled[:, lanes] = (grad_t * old).astype(jnp.bfloat16)
            new_scaled[:, lanes] = (grad_t * inverse).astype(jnp.bfloat16)
            factors[pl.ds(0, 1), lanes] = old
            factors[pl.ds(1, 1), lanes] = delta * old
            factors[pl.ds(2, 1), lanes] = inverse
            factors[pl.ds(3, 1), lanes] = delta * inverse
            for k in range(lanes.size // rows):
                outs[lanes.start // rows + k][0] = attended[:, k * rows : (k + 1) * rows]

        for lanes in lane_chunks(0, newest * rows, 2 * rows):
            fresh = scores[at, lanes]
            before = stats[pl.ds(0, 1), lanes]
            top = jnp.maximum(before, jnp.max(fresh, axis=0, keepdims=True))
            correction = jnp.exp2(before - top)
            p = jnp.exp2(fresh - top)
            p_low = p.astype(jnp.bfloat16)
            scores[at, lanes] = p
            low[at, lanes] = p_low
            total = stats[pl.ds(1, 1), lanes] * correction + jnp.sum(p, axis=0, keepdims=True)
            weighted = mixed[:, lanes] * correction + dot(vt_all[:, at], p_low, NN)
            settle(lanes, total, correction, weighted)
        column = scores[:, at]
        p = jnp.exp2(column - jnp.max(column, axis=0, keepdims=True))
        p_low = p.astype(jnp.bfloat16)
        scores[:, at] = p
        low[:, at] = p_low
        settle(at, jnp.sum(p, axis=0, keepdims=True), 1.0, dot(vt_all[...], p_low, NN))

        for j, out in enumerate(outs):
            keys = pl.ds(j * rows, rows)
            row = 0 if j < newest else 2
            scaled = old_scaled if j < newest else new_scaled
            for lanes in lane_chunks(0, blocks * rows, 4 * rows):
                g = dots[keys, lanes] * factors[pl.ds(row, 1), lanes] - factors[pl.ds(row + 1, 1), lanes]
                grads_low[keys, lanes] = (scores[keys, lanes] * g).astype(jnp.bfloat16)
            out[2] = (dot(grads_low[keys, :], q_all[...], NN) * scaling).astype(jnp.bfloat16)
            out[3] = dot(low[keys, :], scaled[...], NT).astype(jnp.bfloat16)
        for lanes in lane_chunks(0, blocks * rows, 2 * rows):
            grad = (dot(kt_all[...], grads_low[:, lanes], NN) * scaling).astype(jnp.bfloat16)
            for k in range(lanes.size // rows):
                outs[lanes.start // rows + k][1] = grad[:, k * rows : (k + 1) * rows]


def per_device(query, key, value, grad_out, frame_ids, sink_frame, window):
    rows, row_width = query.shape
    heads = window.shape[0]
    width = row_width // heads
    blocks = lax.axis_size("tm")
    owned, sent, partner, pairs = plan(blocks, lax.axis_size("head"), heads)
    axes = ("tm", "head")
    smem = pl.BlockSpec(memory_space=pltpu.SMEM)
    vmem = pl.BlockSpec(memory_space=pltpu.VMEM)
    in_place = pl.BlockSpec(memory_space=pltpu.HBM)
    part = jax.ShapeDtypeStruct((4, rows, width), query.dtype)
    local = jax.ShapeDtypeStruct(query.shape, query.dtype)

    tokens = blocks * rows
    split = tokens <= split_limit
    tiles = 5 if split else 4
    home_tiles = vmem_bytes // (2 * rows * width)
    home, *parts = pl.pallas_call(
        functools.partial(pack_kernel, owned, partner, sent, width),
        out_shape=[jax.ShapeDtypeStruct((home_tiles, rows, width), query.dtype)] + [part] * (blocks - 1),
        in_specs=[in_place] * 7,
        out_specs=[in_place] * blocks,
        scratch_shapes=[
            pltpu.VMEM((4, rows, row_width), query.dtype),
            pltpu.VMEM((tiles, rows, width), query.dtype),
            pltpu.VMEM((blocks - 1, 4, rows, width), query.dtype),
            pltpu.SMEM(frame_ids.shape, jnp.int32),
            pltpu.SMEM(sink_frame.shape, jnp.int32),
            pltpu.SMEM(window.shape, jnp.int32),
            pltpu.SemaphoreType.DMA((7,)),
            pltpu.SemaphoreType.DMA((blocks,)),
        ],
        compiler_params=pltpu.CompilerParams(vmem_limit_bytes=62 * MIB),
        name="pack",
    )(query, key, value, grad_out, frame_ids, sink_frame, window)
    parts = [lax.ppermute(parts[s - 1], axes, pairs[s]) for s in range(1, blocks)]

    stretch = (4 if blocks % 4 == 0 else 2) * rows
    low, full = query.dtype, jnp.float32
    if split:
        square = jax.ShapeDtypeStruct((tokens, tokens), full)
        tall = jax.ShapeDtypeStruct((tokens, width), low)
        wide = jax.ShapeDtypeStruct((width, tokens), low)
        table = jax.ShapeDtypeStruct((blocks, tokens), full)
        held = [square] * 2 + [tall] * 3 + [wide] * 3
        flops = 2 * rows * rows * width
        bias, *state = pl.pallas_call(
            functools.partial(products_kernel, owned, blocks, rows),
            out_shape=[table, *held],
            in_specs=[in_place] + [vmem] * (blocks - 3),
            out_specs=[vmem] * 9,
            scratch_shapes=[pltpu.VMEM((tiles, rows, width), low), pltpu.SemaphoreType.DMA],
            compiler_params=pltpu.CompilerParams(vmem_limit_bytes=20 * MIB),
            cost_estimate=pl.CostEstimate(
                flops=2 * flops * (blocks - 2) ** 2, bytes_accessed=8 * tokens * tokens, transcendentals=0
            ),
            name="products",
        )(home, *parts[:-2])
        *state, weights_low, stats, mixed = pl.pallas_call(
            functools.partial(softmax_kernel, owned, blocks, rows),
            out_shape=[
                *held,
                jax.ShapeDtypeStruct((tokens, tokens), low),
                table,
                jax.ShapeDtypeStruct((width, tokens), full),
            ],
            in_specs=[vmem] * 10,
            out_specs=[vmem] * 11,
            input_output_aliases={2 + n: n for n in range(8)},
            compiler_params=pltpu.CompilerParams(vmem_limit_bytes=20 * MIB),
            cost_estimate=pl.CostEstimate(
                flops=3 * flops * blocks**2, bytes_accessed=8 * tokens * tokens, transcendentals=tokens * tokens
            ),
            name="softmax",
        )(bias, parts[-2], *state)
        parts = pl.pallas_call(
            functools.partial(finish_kernel, owned, blocks, rows),
            out_shape=[part] * blocks + held + [jax.ShapeDtypeStruct((tokens, tokens), low)],
            in_specs=[vmem] * 13,
            out_specs=[vmem] * (blocks + 9),
            input_output_aliases={4 + n: blocks + n for n in range(9)},
            scratch_shapes=[
                pltpu.VMEM((tokens, tokens), low),
                pltpu.VMEM((width, tokens), low),
                pltpu.VMEM((width, tokens), low),
                pltpu.VMEM((8, tokens), full),
            ],
            compiler_params=pltpu.CompilerParams(vmem_limit_bytes=24 * MIB),
            name="finish",
        )(bias, stats, mixed, parts[-1], *state, weights_low)[:blocks]
    else:
        parts = pl.pallas_call(
            functools.partial(head_kernel, owned, partner, rows),
            out_shape=[part] * blocks,
            in_specs=[smem] * 3 + [pl.BlockSpec(memory_space=pl.ANY)] + [vmem] * (blocks - 1),
            out_specs=[vmem] * blocks,
            scratch_shapes=[
                pltpu.VMEM((4, rows, width), low),
                pltpu.VMEM((tokens, width), low),
                pltpu.VMEM((width, tokens), low),
                pltpu.VMEM((width, tokens), low),
                pltpu.VMEM((width, tokens), low),
                pltpu.VMEM((tokens, stretch), full),
                pltpu.VMEM((tokens, stretch), low),
                pltpu.VMEM((tokens, stretch), low),
                pltpu.VMEM((width, stretch), low),
                pltpu.VMEM((tokens, width), full),
                pltpu.VMEM((tokens, width), full),
                pltpu.VMEM((blocks, 2, width, rows), low),
                pltpu.SemaphoreType.DMA,
            ],
            compiler_params=pltpu.CompilerParams(vmem_limit_bytes=48 * MIB),
            name="head_attention",
        )(frame_ids, sink_frame, window, home, *parts)
    back = [[(owner, source) for source, owner in step] for step in pairs]
    parts = [parts[0]] + [lax.ppermute(parts[s], axes, back[s]) for s in range(1, blocks)]

    return pl.pallas_call(
        functools.partial(unpack_kernel, sent, width),
        out_shape=[local] * 4,
        in_specs=[vmem] * blocks,
        out_specs=[vmem] * 4,
        compiler_params=pltpu.CompilerParams(vmem_limit_bytes=24 * MIB),
        name="unpack",
    )(*parts)


def solution(mesh):
    spec = P("tm", "head")
    return jax.shard_map(
        per_device,
        mesh=mesh,
        in_specs=(spec, spec, spec, spec, P(), P(), P("head")),
        out_specs=(spec, spec, spec, spec),
        check_vma=False,
    )
```

```python
import functools
import math

import jax
import jax.numpy as jnp
import numpy as np
from jax import lax
from jax.experimental import pallas as pl
from jax.experimental.pallas import tpu as pltpu
from jax.sharding import PartitionSpec as P

hidden_score = -1e30
MIB = 1 << 20
vmem_bytes = 64 * MIB
split_limit = 1024


even_rounds = (
    {
        1: (4, 6, 3, 2, 7, 0, 5),
        2: (3, 7, 5, 6, 1, 4, 0),
        3: (2, 0, 4, 5, 6, 7, 1),
        4: (7, 3, 2, 1, 0, 5, 6),
        5: (1, 2, 6, 0, 4, 3, 7),
    },
    {
        0: (5, 7, 6, 3, 1, 2, 4),
        1: (6, 4, 5, 7, 2, 3, 0),
        4: (0, 1, 7, 2, 5, 6, 3),
        6: (2, 5, 1, 4, 3, 0, 7),
        7: (3, 2, 0, 1, 4, 5, 6),
    },
)
even_rounds_back = (2, 4, 5, 6, 7, 1, 3)


def plan(blocks, groups, heads):
    laid_out = []
    for group in range(groups):
        if blocks == 8 and heads == 5:
            laid_out.append(even_rounds[group % 2])
        else:
            owners = [(head * blocks // heads + group % 2) % blocks for head in range(heads)]
            laid_out.append({u: [(u - step) % blocks for step in range(1, blocks)] for u in owners})
    owned = np.full((groups, blocks), -1)
    sent = np.full((blocks, groups, blocks), -1)
    partner = np.full((blocks, groups, blocks), -1)
    pairs = [[] for _ in range(blocks)]
    for group, rounds in enumerate(laid_out):
        for head, (owner, sources) in enumerate(rounds.items()):
            owned[group, owner] = head
            for step, source in enumerate((owner, *sources)):
                sent[step, group, source] = head
                partner[step, group, owner] = source
                pairs[step].append((source * groups + group, owner * groups + group))
    return owned, sent, partner, [sorted(step) for step in pairs]


def looked_up(table, group, block):
    groups, blocks = table.shape
    period = next(p for p in range(1, groups + 1) if (table == table[np.arange(groups) % p]).all())
    bits = int(table.max() + 1).bit_length()
    per_word = 31 // bits
    word = jnp.int32(0)
    for row in range(period):
        for first in range(0, blocks, per_word):
            values = table[row, first : first + per_word] + 1
            packed = sum(int(value) << (bits * n) for n, value in enumerate(values))
            here = (lax.rem(group, period) == row) & (block >= first) & (block < first + per_word)
            word = jnp.where(here, packed, word)
    return ((word >> (bits * lax.rem(block, per_word))) & ((1 << bits) - 1)) - 1


def dot(a, b, contract):
    return lax.dot_general(a, b, (contract, ((), ())), preferred_element_type=jnp.float32)


NN = ((1,), (0,))
NT = ((1,), (1,))


def head_columns(head, width):
    return pl.ds(pl.multiple_of(head * width, width), width)


def pack_kernel(owned, partner, sent, width, query, key, value, grad_out, frame_ids, sink_frame, window, *refs):
    blocks = len(sent)
    home, outs, refs = refs[0], refs[1:blocks], refs[blocks:]
    staged, tiles, packed, frames_here, sink_here, window_here, in_sems, out_sems = refs
    group, block = lax.axis_index("head"), lax.axis_index("tm")
    arrays = (query, key, value, grad_out)
    loads = [pltpu.make_async_copy(a, staged.at[n], in_sems.at[n]) for n, a in enumerate(arrays)]
    small = ((frame_ids, frames_here), (sink_frame, sink_here), (window, window_here))
    loads += [pltpu.make_async_copy(a, here, in_sems.at[4 + n]) for n, (a, here) in enumerate(small)]
    for load in loads:
        load.start()
    heads = [looked_up(table, group, block) for table in sent]
    stores = [pltpu.make_async_copy(packed.at[n], out, out_sems.at[1 + n]) for n, out in enumerate(outs)]
    keep = pltpu.make_async_copy(tiles, home.at[pl.ds(0, tiles.shape[0])], out_sems.at[0])
    for load in loads:
        load.wait()

    def fill(target, head):
        columns = head_columns(head, width)
        for n in range(3):
            target[n] = staged[n, :, columns]
        target[3] = staged[3, :, columns].T

    for step, head in enumerate(heads[1:]):

        @pl.when(head >= 0)
        def _():
            fill(packed.at[step], head)
            stores[step].start()

    @pl.when(heads[0] >= 0)
    def _():
        fill(tiles, heads[0])
        if tiles.shape[0] > 4:
            frames = [frames_here[looked_up(table, group, block)] for table in partner]
            row = lax.broadcasted_iota(jnp.int32, tiles.shape[1:], 0)
            theirs, own = jnp.zeros_like(row), jnp.zeros_like(row)
            for n, frame in enumerate(frames):
                theirs = jnp.where(row // blocks == n, frame, theirs)
                own = jnp.where(lax.rem(row, blocks) == n, frame, own)
            tiles[4] = seen_bias(theirs, own, window_here[heads[0]], sink_here[0]).astype(tiles.dtype)
        keep.start()

    for step, head in enumerate(heads[1:]):

        @pl.when(head >= 0)
        def _():
            stores[step].wait()

    @pl.when(heads[0] >= 0)
    def _():
        keep.wait()


def unpack_kernel(sent, width, *refs):
    parts, (attended, query_grad, key_grad, value_grad) = refs[:-4], refs[-4:]
    group, block = lax.axis_index("head"), lax.axis_index("tm")
    for step, part in enumerate(parts):
        head = looked_up(sent[step], group, block)

        @pl.when(head >= 0)
        def _():
            columns = head_columns(head, width)
            attended[:, columns] = part[0].T
            query_grad[:, columns] = part[1].T
            key_grad[:, columns] = part[2]
            value_grad[:, columns] = part[3]


def head_kernel(owned, partner, rows, frame_ids, sink_frame, window, local, *refs):
    blocks = len(partner)
    parts, outs, scratch = refs[: blocks - 1], refs[blocks - 1 : 2 * blocks - 1], refs[2 * blocks - 1 :]
    (here, q_all, kt_all, vt_all, gt_all, weights, weights_low, grads_low, grad_scaled, dk, dv, res, sem) = scratch
    parts = (here, *parts)
    group, block = lax.axis_index("head"), lax.axis_index("tm")
    head = looked_up(owned, group, block)
    width = q_all.shape[1]
    scaling = 1.0 / math.sqrt(width)
    rescale = scaling * math.log2(math.e)
    stretch = weights.shape[1]
    half = stretch // 2
    each = half // rows

    @pl.when(head >= 0)
    def _():
        fetch = pltpu.make_async_copy(local.at[pl.ds(0, 4)], here, sem)
        fetch.start()
        span = window[head]
        sink = sink_frame[0]
        frames = [frame_ids[looked_up(table, group, block)] for table in partner]

        def placed(j):
            at = pl.ds(j * rows, rows)
            q_all[at, :] = parts[j][0]
            kt_all[:, at] = parts[j][1].T
            vt_all[:, at] = parts[j][2].T
            gt_all[:, at] = parts[j][3]

        for j in range(1, blocks):
            placed(j)
        fetch.wait()
        placed(0)
        dk[...] = jnp.zeros_like(dk)
        dv[...] = jnp.zeros_like(dv)
        lane_block = lax.broadcasted_iota(jnp.int32, (1, half), 1) // rows

        def one_stretch(i, carry):
            at = [pl.ds(pl.multiple_of(i * stretch + h * half, half), half) for h in range(2)]
            lanes = [pl.ds(h * half, half) for h in range(2)]
            keys = [pl.ds(j * rows, rows) for j in range(blocks)]
            q_rows = [q_all[at[h], :] for h in range(2)]
            top = [jnp.full((1, half), hidden_score, jnp.float32)] * 2
            total = [jnp.zeros((1, half), jnp.float32)] * 2
            delta = [None] * 2
            own = [[], []]
            for h in range(2):
                for k in range(each):
                    n = i * 2 * each + h * each + k
                    own[h].append(sum(jnp.where(n == j, frames[j], 0) for j in range(blocks)))

            def score(h, j):
                bias = jnp.zeros((1, half), jnp.float32)
                for k in range(each):
                    seen = (frames[j] <= own[h][k]) & (frames[j] > own[h][k] - span)
                    seen = seen | ((frames[j] == sink) & (sink <= own[h][k]))
                    bias = jnp.where(lane_block == k, jnp.where(seen, 0.0, hidden_score), bias)
                scores = dot(parts[j][1], q_rows[h], NT) * rescale + bias
                weights[keys[j], lanes[h]] = scores
                top[h] = jnp.maximum(top[h], jnp.max(scores, axis=0, keepdims=True))

            def weigh(h, j):
                p = jnp.exp2(weights[keys[j], lanes[h]] - top[h])
                total[h] = total[h] + jnp.sum(p, axis=0, keepdims=True)
                weights[keys[j], lanes[h]] = p
                weights_low[keys[j], lanes[h]] = p.astype(jnp.bfloat16)

            def attend(h):
                inverse = 1.0 / total[h]
                mixed = (dot(vt_all[...], weights_low[:, lanes[h]], NN) * inverse).astype(jnp.bfloat16)
                grad_t = gt_all[:, at[h]].astype(jnp.float32)
                delta[h] = jnp.sum(grad_t * mixed.astype(jnp.float32), axis=0, keepdims=True) * inverse
                grad_scaled[:, lanes[h]] = (grad_t * inverse).astype(jnp.bfloat16)
                for k in range(each):
                    res[i * 2 * each + h * each + k, 0] = mixed[:, k * rows : (k + 1) * rows]

            def differ(h, j):
                g = dot(parts[j][2], grad_scaled[:, lanes[h]], NN) - delta[h]
                grads_low[keys[j], lanes[h]] = (weights[keys[j], lanes[h]] * g).astype(jnp.bfloat16)

            def query_part(h):
                grad = (dot(kt_all[...], grads_low[:, lanes[h]], NN) * scaling).astype(jnp.bfloat16)
                for k in range(each):
                    res[i * 2 * each + h * each + k, 1] = grad[:, k * rows : (k + 1) * rows]

            for j in range(blocks):
                score(0, j)
            for j in range(blocks):
                score(1, j)
                weigh(0, j)
            attend(0)
            for j in range(blocks):
                weigh(1, j)
                differ(0, j)
            attend(1)
            query_part(0)
            q_both = jnp.concatenate(q_rows, axis=0)
            for j in range(blocks):
                differ(1, j)
                dk[keys[j], :] += dot(grads_low[keys[j], :], q_both, NN)
                dv[keys[j], :] += dot(weights_low[keys[j], :], grad_scaled[...], NT)
            query_part(1)
            return carry

        lax.fori_loop(0, blocks * rows // stretch, one_stretch, 0)
        for j, out in enumerate(outs):
            at = pl.ds(j * rows, rows)
            out[0] = res[j, 0]
            out[1] = res[j, 1]
            out[2] = (dk[at, :] * scaling).astype(jnp.bfloat16)
            out[3] = dv[at, :].astype(jnp.bfloat16)


def seen_bias(frame, own, span, sink):
    seen = ((frame <= own) & (frame > own - span)) | ((frame == sink) & (sink <= own))
    return jnp.where(seen, 0.0, hidden_score)


def frames_by_lane(frames, rows):
    lane_block = lax.broadcasted_iota(jnp.int32, (1, len(frames) * rows), 1) // rows
    row = jnp.zeros_like(lane_block)
    for n, frame in enumerate(frames):
        row = jnp.where(lane_block == n, frame, row)
    return row


def place_block(part, j, rows, q_all, k_all, v_all, kt_all, vt_all, gt_all):
    at = pl.ds(j * rows, rows)
    q_all[at, :] = part[0]
    k_all[at, :] = part[1]
    v_all[at, :] = part[2]
    kt_all[:, at] = part[1].T
    vt_all[:, at] = part[2].T
    gt_all[:, at] = part[3]


def pair_products(j, held, rows, bias, scores, dots, q_all, k_all, v_all, gt_all):
    width = q_all.shape[1]
    rescale = math.log2(math.e) / math.sqrt(width)
    before = held * rows
    at = pl.ds(j * rows, rows)
    every = pl.ds(0, before + rows)
    scores[at, every] = dot(k_all[at, :], q_all[every, :], NT) * rescale + bias[pl.ds(j, 1), every]
    dots[at, every] = dot(v_all[at, :], gt_all[:, every], NN)
    column = dot(k_all[pl.ds(0, before), :], q_all[at, :], NT) * rescale
    for n in range(held):
        keys = pl.ds(n * rows, rows)
        scores[keys, at] = column[n * rows : (n + 1) * rows, :] + bias[pl.ds(n, 1), at]
    dots[pl.ds(0, before), at] = dot(v_all[pl.ds(0, before), :], gt_all[:, at], NN)


def lane_chunks(start, stop, size):
    return [pl.ds(first, min(size, stop - first)) for first in range(start, stop, size)]


def products_kernel(owned, blocks, rows, home, *refs):
    held = blocks - 2
    parts, refs = refs[: held - 1], refs[held - 1 :]
    bias, scores, dots, *places, tiles, sem = refs
    head = looked_up(owned, lax.axis_index("head"), lax.axis_index("tm"))

    @pl.when(head >= 0)
    def _():
        fetch = pltpu.make_async_copy(home.at[pl.ds(0, tiles.shape[0])], tiles, sem)
        fetch.start()
        for j, part in enumerate(parts):
            place_block(part, j + 1, rows, *places)
        fetch.wait()
        place_block(tiles, 0, rows, *places)
        mask = tiles[4].astype(jnp.float32)
        for j in range(blocks):
            for n in range(blocks):
                row = j * blocks + n
                bias[pl.ds(j, 1), pl.ds(n * rows, rows)] = mask[row : row + 1, :]
        q_all, k_all, v_all, _, _, gt_all = places
        lanes = pl.ds(0, held * rows)
        rescale = math.log2(math.e) / math.sqrt(q_all.shape[1])
        for j in range(held):
            keys = pl.ds(j * rows, rows)
            scores[keys, lanes] = dot(k_all[keys, :], q_all[lanes, :], NT) * rescale + bias[pl.ds(j, 1), lanes]
            dots[keys, lanes] = dot(v_all[keys, :], gt_all[:, lanes], NN)


def softmax_kernel(owned, blocks, rows, bias, *refs):
    part, refs = refs[0], refs[9:]
    scores, dots, q_all, k_all, v_all, kt_all, vt_all, gt_all, low, stats, mixed = refs
    head = looked_up(owned, lax.axis_index("head"), lax.axis_index("tm"))

    @pl.when(head >= 0)
    def _():
        newest = blocks - 2
        held = pl.ds(0, (newest + 1) * rows)
        place_block(part, newest, rows, q_all, k_all, v_all, kt_all, vt_all, gt_all)
        pair_products(newest, newest, rows, bias, scores, dots, q_all, k_all, v_all, gt_all)
        for lanes in lane_chunks(0, (newest + 1) * rows, 2 * rows):
            top = jnp.max(scores[held, lanes], axis=0, keepdims=True)
            total = jnp.zeros_like(top)
            for j in range(newest + 1):
                keys = pl.ds(j * rows, rows)
                p = jnp.exp2(scores[keys, lanes] - top)
                total = total + jnp.sum(p, axis=0, keepdims=True)
                scores[keys, lanes] = p
                low[keys, lanes] = p.astype(jnp.bfloat16)
            stats[pl.ds(0, 1), lanes] = top
            stats[pl.ds(1, 1), lanes] = total
            mixed[:, lanes] = dot(vt_all[:, held], low[held, lanes], NN)


def finish_kernel(owned, blocks, rows, bias, stats, mixed, *refs):
    part, refs = refs[0], refs[10:]
    outs, refs = refs[:blocks], refs[blocks:]
    scores, dots, q_all, k_all, v_all, kt_all, vt_all, gt_all, low, grads_low, old_scaled, new_scaled, factors = refs
    head = looked_up(owned, lax.axis_index("head"), lax.axis_index("tm"))
    width = q_all.shape[1]
    scaling = 1.0 / math.sqrt(width)

    @pl.when(head >= 0)
    def _():
        newest = blocks - 1
        at = pl.ds(newest * rows, rows)
        place_block(part, newest, rows, q_all, k_all, v_all, kt_all, vt_all, gt_all)
        pair_products(newest, newest, rows, bias, scores, dots, q_all, k_all, v_all, gt_all)

        def settle(lanes, total, old_factor, weighted):
            inverse = 1.0 / total
            attended = (weighted * inverse).astype(jnp.bfloat16)
            grad_t = gt_all[:, lanes].astype(jnp.float32)
            delta = jnp.sum(grad_t * attended.astype(jnp.float32), axis=0, keepdims=True)
            old = inverse * old_factor
            old_scaled[:, lanes] = (grad_t * old).astype(jnp.bfloat16)
            new_scaled[:, lanes] = (grad_t * inverse).astype(jnp.bfloat16)
            factors[pl.ds(0, 1), lanes] = old
            factors[pl.ds(1, 1), lanes] = delta * old
            factors[pl.ds(2, 1), lanes] = inverse
            factors[pl.ds(3, 1), lanes] = delta * inverse
            for k in range(lanes.size // rows):
                outs[lanes.start // rows + k][0] = attended[:, k * rows : (k + 1) * rows]

        for lanes in lane_chunks(0, newest * rows, 2 * rows):
            fresh = scores[at, lanes]
            before = stats[pl.ds(0, 1), lanes]
            top = jnp.maximum(before, jnp.max(fresh, axis=0, keepdims=True))
            correction = jnp.exp2(before - top)
            p = jnp.exp2(fresh - top)
            p_low = p.astype(jnp.bfloat16)
            scores[at, lanes] = p
            low[at, lanes] = p_low
            total = stats[pl.ds(1, 1), lanes] * correction + jnp.sum(p, axis=0, keepdims=True)
            weighted = mixed[:, lanes] * correction + dot(vt_all[:, at], p_low, NN)
            settle(lanes, total, correction, weighted)
        column = scores[:, at]
        p = jnp.exp2(column - jnp.max(column, axis=0, keepdims=True))
        p_low = p.astype(jnp.bfloat16)
        scores[:, at] = p
        low[:, at] = p_low
        settle(at, jnp.sum(p, axis=0, keepdims=True), 1.0, dot(vt_all[...], p_low, NN))

        for j, out in enumerate(outs):
            keys = pl.ds(j * rows, rows)
            row = 0 if j < newest else 2
            scaled = old_scaled if j < newest else new_scaled
            for lanes in lane_chunks(0, blocks * rows, 4 * rows):
                g = dots[keys, lanes] * factors[pl.ds(row, 1), lanes] - factors[pl.ds(row + 1, 1), lanes]
                grads_low[keys, lanes] = (scores[keys, lanes] * g).astype(jnp.bfloat16)
            out[2] = (dot(grads_low[keys, :], q_all[...], NN) * scaling).astype(jnp.bfloat16)
            out[3] = dot(low[keys, :], scaled[...], NT).astype(jnp.bfloat16)
        for lanes in lane_chunks(0, blocks * rows, 2 * rows):
            grad = (dot(kt_all[...], grads_low[:, lanes], NN) * scaling).astype(jnp.bfloat16)
            for k in range(lanes.size // rows):
                outs[lanes.start // rows + k][1] = grad[:, k * rows : (k + 1) * rows]


def per_device(query, key, value, grad_out, frame_ids, sink_frame, window):
    rows, row_width = query.shape
    heads = window.shape[0]
    width = row_width // heads
    blocks = lax.axis_size("tm")
    owned, sent, partner, pairs = plan(blocks, lax.axis_size("head"), heads)
    axes = ("tm", "head")
    smem = pl.BlockSpec(memory_space=pltpu.SMEM)
    vmem = pl.BlockSpec(memory_space=pltpu.VMEM)
    in_place = pl.BlockSpec(memory_space=pltpu.HBM)
    part = jax.ShapeDtypeStruct((4, rows, width), query.dtype)
    local = jax.ShapeDtypeStruct(query.shape, query.dtype)

    tokens = blocks * rows
    split = tokens <= split_limit
    tiles = 5 if split else 4
    home_tiles = vmem_bytes // (2 * rows * width)
    home, *parts = pl.pallas_call(
        functools.partial(pack_kernel, owned, partner, sent, width),
        out_shape=[jax.ShapeDtypeStruct((home_tiles, rows, width), query.dtype)] + [part] * (blocks - 1),
        in_specs=[in_place] * 7,
        out_specs=[in_place] * blocks,
        scratch_shapes=[
            pltpu.VMEM((4, rows, row_width), query.dtype),
            pltpu.VMEM((tiles, rows, width), query.dtype),
            pltpu.VMEM((blocks - 1, 4, rows, width), query.dtype),
            pltpu.SMEM(frame_ids.shape, jnp.int32),
            pltpu.SMEM(sink_frame.shape, jnp.int32),
            pltpu.SMEM(window.shape, jnp.int32),
            pltpu.SemaphoreType.DMA((7,)),
            pltpu.SemaphoreType.DMA((blocks,)),
        ],
        compiler_params=pltpu.CompilerParams(vmem_limit_bytes=62 * MIB),
        name="pack",
    )(query, key, value, grad_out, frame_ids, sink_frame, window)
    parts = [lax.ppermute(parts[s - 1], axes, pairs[s]) for s in range(1, blocks)]

    stretch = (4 if blocks % 4 == 0 else 2) * rows
    low, full = query.dtype, jnp.float32
    if split:
        square = jax.ShapeDtypeStruct((tokens, tokens), full)
        tall = jax.ShapeDtypeStruct((tokens, width), low)
        wide = jax.ShapeDtypeStruct((width, tokens), low)
        table = jax.ShapeDtypeStruct((blocks, tokens), full)
        held = [square] * 2 + [tall] * 3 + [wide] * 3
        flops = 2 * rows * rows * width
        bias, *state = pl.pallas_call(
            functools.partial(products_kernel, owned, blocks, rows),
            out_shape=[table, *held],
            in_specs=[in_place] + [vmem] * (blocks - 3),
            out_specs=[vmem] * 9,
            scratch_shapes=[pltpu.VMEM((tiles, rows, width), low), pltpu.SemaphoreType.DMA],
            compiler_params=pltpu.CompilerParams(vmem_limit_bytes=20 * MIB),
            cost_estimate=pl.CostEstimate(
                flops=2 * flops * (blocks - 2) ** 2, bytes_accessed=8 * tokens * tokens, transcendentals=0
            ),
            name="products",
        )(home, *parts[:-2])
        *state, weights_low, stats, mixed = pl.pallas_call(
            functools.partial(softmax_kernel, owned, blocks, rows),
            out_shape=[
                *held,
                jax.ShapeDtypeStruct((tokens, tokens), low),
                table,
                jax.ShapeDtypeStruct((width, tokens), full),
            ],
            in_specs=[vmem] * 10,
            out_specs=[vmem] * 11,
            input_output_aliases={2 + n: n for n in range(8)},
            compiler_params=pltpu.CompilerParams(vmem_limit_bytes=20 * MIB),
            cost_estimate=pl.CostEstimate(
                flops=3 * flops * blocks**2, bytes_accessed=8 * tokens * tokens, transcendentals=tokens * tokens
            ),
            name="softmax",
        )(bias, parts[-2], *state)
        parts = pl.pallas_call(
            functools.partial(finish_kernel, owned, blocks, rows),
            out_shape=[part] * blocks + held + [jax.ShapeDtypeStruct((tokens, tokens), low)],
            in_specs=[vmem] * 13,
            out_specs=[vmem] * (blocks + 9),
            input_output_aliases={4 + n: blocks + n for n in range(9)},
            scratch_shapes=[
                pltpu.VMEM((tokens, tokens), low),
                pltpu.VMEM((width, tokens), low),
                pltpu.VMEM((width, tokens), low),
                pltpu.VMEM((8, tokens), full),
            ],
            compiler_params=pltpu.CompilerParams(vmem_limit_bytes=24 * MIB),
            name="finish",
        )(bias, stats, mixed, parts[-1], *state, weights_low)[:blocks]
    else:
        parts = pl.pallas_call(
            functools.partial(head_kernel, owned, partner, rows),
            out_shape=[part] * blocks,
            in_specs=[smem] * 3 + [pl.BlockSpec(memory_space=pl.ANY)] + [vmem] * (blocks - 1),
            out_specs=[vmem] * blocks,
            scratch_shapes=[
                pltpu.VMEM((4, rows, width), low),
                pltpu.VMEM((tokens, width), low),
                pltpu.VMEM((width, tokens), low),
                pltpu.VMEM((width, tokens), low),
                pltpu.VMEM((width, tokens), low),
                pltpu.VMEM((tokens, stretch), full),
                pltpu.VMEM((tokens, stretch), low),
                pltpu.VMEM((tokens, stretch), low),
                pltpu.VMEM((width, stretch), low),
                pltpu.VMEM((tokens, width), full),
                pltpu.VMEM((tokens, width), full),
                pltpu.VMEM((blocks, 2, width, rows), low),
                pltpu.SemaphoreType.DMA,
            ],
            compiler_params=pltpu.CompilerParams(vmem_limit_bytes=48 * MIB),
            name="head_attention",
        )(frame_ids, sink_frame, window, home, *parts)
    back = [[(owner, source) for source, owner in step] for step in pairs]
    order = even_rounds_back if blocks == 8 and heads == 5 else range(1, blocks)
    parts = [parts[0]] + [lax.ppermute(parts[s], axes, back[s]) for s in order]

    return pl.pallas_call(
        functools.partial(unpack_kernel, sent[np.array([0, *order])], width),
        out_shape=[local] * 4,
        in_specs=[vmem] * blocks,
        out_specs=[vmem] * 4,
        compiler_params=pltpu.CompilerParams(vmem_limit_bytes=24 * MIB),
        name="unpack",
    )(*parts)


def solution(mesh):
    spec = P("tm", "head")
    return jax.shard_map(
        per_device,
        mesh=mesh,
        in_specs=(spec, spec, spec, spec, P(), P(), P("head")),
        out_specs=(spec, spec, spec, spec),
        check_vma=False,
    )
```

```python
import functools
import math

import jax
import jax.numpy as jnp
import numpy as np
from jax import lax
from jax.experimental import pallas as pl
from jax.experimental.pallas import tpu as pltpu
from jax.sharding import PartitionSpec as P

hidden_score = -1e30
MIB = 1 << 20
vmem_bytes = 64 * MIB
split_limit = 1024


even_rounds = (
    {
        1: (4, 6, 3, 2, 7, 0, 5),
        2: (3, 7, 5, 6, 1, 4, 0),
        3: (2, 0, 4, 5, 6, 7, 1),
        4: (7, 3, 2, 1, 0, 5, 6),
        5: (1, 2, 6, 0, 4, 3, 7),
    },
    {
        0: (5, 7, 6, 3, 1, 2, 4),
        1: (6, 4, 5, 7, 2, 3, 0),
        4: (0, 1, 7, 2, 5, 6, 3),
        6: (2, 5, 1, 4, 3, 0, 7),
        7: (3, 2, 0, 1, 4, 5, 6),
    },
)
even_rounds_back = (2, 4, 5, 6, 7, 1, 3)


def plan(blocks, groups, heads):
    laid_out = []
    for group in range(groups):
        if blocks == 8 and heads == 5:
            laid_out.append(even_rounds[group % 2])
        else:
            owners = [(head * blocks // heads + group % 2) % blocks for head in range(heads)]
            laid_out.append({u: [(u - step) % blocks for step in range(1, blocks)] for u in owners})
    owned = np.full((groups, blocks), -1)
    sent = np.full((blocks, groups, blocks), -1)
    partner = np.full((blocks, groups, blocks), -1)
    pairs = [[] for _ in range(blocks)]
    for group, rounds in enumerate(laid_out):
        for head, (owner, sources) in enumerate(rounds.items()):
            owned[group, owner] = head
            for step, source in enumerate((owner, *sources)):
                sent[step, group, source] = head
                partner[step, group, owner] = source
                pairs[step].append((source * groups + group, owner * groups + group))
    return owned, sent, partner, [sorted(step) for step in pairs]


def looked_up(table, group, block):
    groups, blocks = table.shape
    period = next(p for p in range(1, groups + 1) if (table == table[np.arange(groups) % p]).all())
    bits = int(table.max() + 1).bit_length()
    per_word = 31 // bits
    word = jnp.int32(0)
    for row in range(period):
        for first in range(0, blocks, per_word):
            values = table[row, first : first + per_word] + 1
            packed = sum(int(value) << (bits * n) for n, value in enumerate(values))
            here = (lax.rem(group, period) == row) & (block >= first) & (block < first + per_word)
            word = jnp.where(here, packed, word)
    return ((word >> (bits * lax.rem(block, per_word))) & ((1 << bits) - 1)) - 1


def dot(a, b, contract):
    return lax.dot_general(a, b, (contract, ((), ())), preferred_element_type=jnp.float32)


NN = ((1,), (0,))
NT = ((1,), (1,))


def head_columns(head, width):
    return pl.ds(pl.multiple_of(head * width, width), width)


def pack_kernel(owned, partner, sent, width, query, key, value, grad_out, frame_ids, sink_frame, window, *refs):
    blocks = len(sent)
    home, outs, refs = refs[0], refs[1:blocks], refs[blocks:]
    staged, tiles, packed, frames_here, sink_here, window_here, in_sems, out_sems = refs
    group, block = lax.axis_index("head"), lax.axis_index("tm")
    arrays = (query, key, value, grad_out)
    loads = [pltpu.make_async_copy(a, staged.at[n], in_sems.at[n]) for n, a in enumerate(arrays)]
    small = ((frame_ids, frames_here), (sink_frame, sink_here), (window, window_here))
    loads += [pltpu.make_async_copy(a, here, in_sems.at[4 + n]) for n, (a, here) in enumerate(small)]
    for load in loads:
        load.start()
    heads = [looked_up(table, group, block) for table in sent]
    stores = [pltpu.make_async_copy(packed.at[n], out, out_sems.at[1 + n]) for n, out in enumerate(outs)]
    keep = pltpu.make_async_copy(tiles, home.at[pl.ds(0, tiles.shape[0])], out_sems.at[0])
    for load in loads:
        load.wait()

    def fill(target, head):
        columns = head_columns(head, width)
        for n in range(3):
            target[n] = staged[n, :, columns]
        target[3] = staged[3, :, columns].T

    for step, head in enumerate(heads[1:]):

        @pl.when(head >= 0)
        def _():
            fill(packed.at[step], head)
            stores[step].start()

    @pl.when(heads[0] >= 0)
    def _():
        fill(tiles, heads[0])
        if tiles.shape[0] > 4:
            frames = [frames_here[looked_up(table, group, block)] for table in partner]
            row = lax.broadcasted_iota(jnp.int32, tiles.shape[1:], 0)
            theirs, own = jnp.zeros_like(row), jnp.zeros_like(row)
            for n, frame in enumerate(frames):
                theirs = jnp.where(row // blocks == n, frame, theirs)
                own = jnp.where(lax.rem(row, blocks) == n, frame, own)
            tiles[4] = seen_bias(theirs, own, window_here[heads[0]], sink_here[0]).astype(tiles.dtype)
        keep.start()

    for step, head in enumerate(heads[1:]):

        @pl.when(head >= 0)
        def _():
            stores[step].wait()

    @pl.when(heads[0] >= 0)
    def _():
        keep.wait()


def unpack_kernel(sent, width, *refs):
    parts, (attended, query_grad, key_grad, value_grad) = refs[:-4], refs[-4:]
    group, block = lax.axis_index("head"), lax.axis_index("tm")
    for step, part in enumerate(parts):
        head = looked_up(sent[step], group, block)

        @pl.when(head >= 0)
        def _():
            columns = head_columns(head, width)
            attended[:, columns] = part[0].T
            query_grad[:, columns] = part[1].T
            key_grad[:, columns] = part[2]
            value_grad[:, columns] = part[3]


def head_kernel(owned, partner, rows, frame_ids, sink_frame, window, local, *refs):
    blocks = len(partner)
    parts, outs, scratch = refs[: blocks - 1], refs[blocks - 1 : 2 * blocks - 1], refs[2 * blocks - 1 :]
    (here, q_all, kt_all, vt_all, gt_all, weights, weights_low, grads_low, grad_scaled, dk, dv, res, sem) = scratch
    parts = (here, *parts)
    group, block = lax.axis_index("head"), lax.axis_index("tm")
    head = looked_up(owned, group, block)
    width = q_all.shape[1]
    scaling = 1.0 / math.sqrt(width)
    rescale = scaling * math.log2(math.e)
    stretch = weights.shape[1]
    half = stretch // 2
    each = half // rows

    @pl.when(head >= 0)
    def _():
        fetch = pltpu.make_async_copy(local.at[pl.ds(0, 4)], here, sem)
        fetch.start()
        span = window[head]
        sink = sink_frame[0]
        frames = [frame_ids[looked_up(table, group, block)] for table in partner]

        def placed(j):
            at = pl.ds(j * rows, rows)
            q_all[at, :] = parts[j][0]
            kt_all[:, at] = parts[j][1].T
            vt_all[:, at] = parts[j][2].T
            gt_all[:, at] = parts[j][3]

        for j in range(1, blocks):
            placed(j)
        fetch.wait()
        placed(0)
        dk[...] = jnp.zeros_like(dk)
        dv[...] = jnp.zeros_like(dv)
        lane_block = lax.broadcasted_iota(jnp.int32, (1, half), 1) // rows

        def one_stretch(i, carry):
            at = [pl.ds(pl.multiple_of(i * stretch + h * half, half), half) for h in range(2)]
            lanes = [pl.ds(h * half, half) for h in range(2)]
            keys = [pl.ds(j * rows, rows) for j in range(blocks)]
            q_rows = [q_all[at[h], :] for h in range(2)]
            top = [jnp.full((1, half), hidden_score, jnp.float32)] * 2
            total = [jnp.zeros((1, half), jnp.float32)] * 2
            delta = [None] * 2
            own = [[], []]
            for h in range(2):
                for k in range(each):
                    n = i * 2 * each + h * each + k
                    own[h].append(sum(jnp.where(n == j, frames[j], 0) for j in range(blocks)))

            def score(h, j):
                bias = jnp.zeros((1, half), jnp.float32)
                for k in range(each):
                    seen = (frames[j] <= own[h][k]) & (frames[j] > own[h][k] - span)
                    seen = seen | ((frames[j] == sink) & (sink <= own[h][k]))
                    bias = jnp.where(lane_block == k, jnp.where(seen, 0.0, hidden_score), bias)
                scores = dot(parts[j][1], q_rows[h], NT) * rescale + bias
                weights[keys[j], lanes[h]] = scores
                top[h] = jnp.maximum(top[h], jnp.max(scores, axis=0, keepdims=True))

            def weigh(h, j):
                p = jnp.exp2(weights[keys[j], lanes[h]] - top[h])
                total[h] = total[h] + jnp.sum(p, axis=0, keepdims=True)
                weights[keys[j], lanes[h]] = p
                weights_low[keys[j], lanes[h]] = p.astype(jnp.bfloat16)

            def attend(h):
                inverse = 1.0 / total[h]
                mixed = (dot(vt_all[...], weights_low[:, lanes[h]], NN) * inverse).astype(jnp.bfloat16)
                grad_t = gt_all[:, at[h]].astype(jnp.float32)
                delta[h] = jnp.sum(grad_t * mixed.astype(jnp.float32), axis=0, keepdims=True) * inverse
                grad_scaled[:, lanes[h]] = (grad_t * inverse).astype(jnp.bfloat16)
                for k in range(each):
                    res[i * 2 * each + h * each + k, 0] = mixed[:, k * rows : (k + 1) * rows]

            def differ(h, j):
                g = dot(parts[j][2], grad_scaled[:, lanes[h]], NN) - delta[h]
                grads_low[keys[j], lanes[h]] = (weights[keys[j], lanes[h]] * g).astype(jnp.bfloat16)

            def query_part(h):
                grad = (dot(kt_all[...], grads_low[:, lanes[h]], NN) * scaling).astype(jnp.bfloat16)
                for k in range(each):
                    res[i * 2 * each + h * each + k, 1] = grad[:, k * rows : (k + 1) * rows]

            for j in range(blocks):
                score(0, j)
            for j in range(blocks):
                score(1, j)
                weigh(0, j)
            attend(0)
            for j in range(blocks):
                weigh(1, j)
                differ(0, j)
            attend(1)
            query_part(0)
            q_both = jnp.concatenate(q_rows, axis=0)
            for j in range(blocks):
                differ(1, j)
                dk[keys[j], :] += dot(grads_low[keys[j], :], q_both, NN)
                dv[keys[j], :] += dot(weights_low[keys[j], :], grad_scaled[...], NT)
            query_part(1)
            return carry

        lax.fori_loop(0, blocks * rows // stretch, one_stretch, 0)
        for j, out in enumerate(outs):
            at = pl.ds(j * rows, rows)
            out[0] = res[j, 0]
            out[1] = res[j, 1]
            out[2] = (dk[at, :] * scaling).astype(jnp.bfloat16)
            out[3] = dv[at, :].astype(jnp.bfloat16)


def seen_bias(frame, own, span, sink):
    seen = ((frame <= own) & (frame > own - span)) | ((frame == sink) & (sink <= own))
    return jnp.where(seen, 0.0, hidden_score)


def frames_by_lane(frames, rows):
    lane_block = lax.broadcasted_iota(jnp.int32, (1, len(frames) * rows), 1) // rows
    row = jnp.zeros_like(lane_block)
    for n, frame in enumerate(frames):
        row = jnp.where(lane_block == n, frame, row)
    return row


def place_block(part, j, rows, q_all, k_all, v_all, kt_all, vt_all, gt_all):
    at = pl.ds(j * rows, rows)
    q_all[at, :] = part[0]
    k_all[at, :] = part[1]
    v_all[at, :] = part[2]
    kt_all[:, at] = part[1].T
    vt_all[:, at] = part[2].T
    gt_all[:, at] = part[3]


def pair_products(j, held, rows, bias, scores, dots, q_all, k_all, v_all, gt_all):
    width = q_all.shape[1]
    rescale = math.log2(math.e) / math.sqrt(width)
    before = held * rows
    at = pl.ds(j * rows, rows)
    every = pl.ds(0, before + rows)
    scores[at, every] = dot(k_all[at, :], q_all[every, :], NT) * rescale + bias[pl.ds(j, 1), every]
    dots[at, every] = dot(v_all[at, :], gt_all[:, every], NN)
    column = dot(k_all[pl.ds(0, before), :], q_all[at, :], NT) * rescale
    for n in range(held):
        keys = pl.ds(n * rows, rows)
        scores[keys, at] = column[n * rows : (n + 1) * rows, :] + bias[pl.ds(n, 1), at]
    dots[pl.ds(0, before), at] = dot(v_all[pl.ds(0, before), :], gt_all[:, at], NN)


def lane_chunks(start, stop, size):
    return [pl.ds(first, min(size, stop - first)) for first in range(start, stop, size)]


def products_kernel(owned, blocks, rows, home, *refs):
    held = blocks - 3
    parts, refs = refs[: held - 1], refs[held - 1 :]
    bias, scores, dots, *places, tiles, sem = refs
    head = looked_up(owned, lax.axis_index("head"), lax.axis_index("tm"))

    @pl.when(head >= 0)
    def _():
        fetch = pltpu.make_async_copy(home.at[pl.ds(0, tiles.shape[0])], tiles, sem)
        fetch.start()
        for j, part in enumerate(parts):
            place_block(part, j + 1, rows, *places)
        fetch.wait()
        place_block(tiles, 0, rows, *places)
        mask = tiles[4].astype(jnp.float32)
        for j in range(blocks):
            for n in range(blocks):
                row = j * blocks + n
                bias[pl.ds(j, 1), pl.ds(n * rows, rows)] = mask[row : row + 1, :]
        q_all, k_all, v_all, _, _, gt_all = places
        lanes = pl.ds(0, held * rows)
        rescale = math.log2(math.e) / math.sqrt(q_all.shape[1])
        for j in range(held):
            keys = pl.ds(j * rows, rows)
            scores[keys, lanes] = dot(k_all[keys, :], q_all[lanes, :], NT) * rescale + bias[pl.ds(j, 1), lanes]
            dots[keys, lanes] = dot(v_all[keys, :], gt_all[:, lanes], NN)


def join_kernel(owned, index, rows, bias, *refs):
    part, (scores, dots, q_all, k_all, v_all, kt_all, vt_all, gt_all) = refs[0], refs[9:]
    head = looked_up(owned, lax.axis_index("head"), lax.axis_index("tm"))

    @pl.when(head >= 0)
    def _():
        place_block(part, index, rows, q_all, k_all, v_all, kt_all, vt_all, gt_all)
        pair_products(index, index, rows, bias, scores, dots, q_all, k_all, v_all, gt_all)


def softmax_kernel(owned, blocks, rows, bias, *refs):
    part, refs = refs[0], refs[9:]
    scores, dots, q_all, k_all, v_all, kt_all, vt_all, gt_all, low, stats, mixed = refs
    head = looked_up(owned, lax.axis_index("head"), lax.axis_index("tm"))

    @pl.when(head >= 0)
    def _():
        newest = blocks - 2
        held = pl.ds(0, (newest + 1) * rows)
        place_block(part, newest, rows, q_all, k_all, v_all, kt_all, vt_all, gt_all)
        pair_products(newest, newest, rows, bias, scores, dots, q_all, k_all, v_all, gt_all)
        for lanes in lane_chunks(0, (newest + 1) * rows, 2 * rows):
            top = jnp.max(scores[held, lanes], axis=0, keepdims=True)
            total = jnp.zeros_like(top)
            for j in range(newest + 1):
                keys = pl.ds(j * rows, rows)
                p = jnp.exp2(scores[keys, lanes] - top)
                total = total + jnp.sum(p, axis=0, keepdims=True)
                scores[keys, lanes] = p
                low[keys, lanes] = p.astype(jnp.bfloat16)
            stats[pl.ds(0, 1), lanes] = top
            stats[pl.ds(1, 1), lanes] = total
            mixed[:, lanes] = dot(vt_all[:, held], low[held, lanes], NN)


def finish_kernel(owned, blocks, rows, bias, stats, mixed, *refs):
    part, refs = refs[0], refs[10:]
    outs, refs = refs[:blocks], refs[blocks:]
    scores, dots, q_all, k_all, v_all, kt_all, vt_all, gt_all, low, grads_low, old_scaled, new_scaled, factors = refs
    head = looked_up(owned, lax.axis_index("head"), lax.axis_index("tm"))
    width = q_all.shape[1]
    scaling = 1.0 / math.sqrt(width)

    @pl.when(head >= 0)
    def _():
        newest = blocks - 1
        at = pl.ds(newest * rows, rows)
        place_block(part, newest, rows, q_all, k_all, v_all, kt_all, vt_all, gt_all)
        pair_products(newest, newest, rows, bias, scores, dots, q_all, k_all, v_all, gt_all)

        def settle(lanes, total, old_factor, weighted):
            inverse = 1.0 / total
            attended = (weighted * inverse).astype(jnp.bfloat16)
            grad_t = gt_all[:, lanes].astype(jnp.float32)
            delta = jnp.sum(grad_t * attended.astype(jnp.float32), axis=0, keepdims=True)
            old = inverse * old_factor
            old_scaled[:, lanes] = (grad_t * old).astype(jnp.bfloat16)
            new_scaled[:, lanes] = (grad_t * inverse).astype(jnp.bfloat16)
            factors[pl.ds(0, 1), lanes] = old
            factors[pl.ds(1, 1), lanes] = delta * old
            factors[pl.ds(2, 1), lanes] = inverse
            factors[pl.ds(3, 1), lanes] = delta * inverse
            for k in range(lanes.size // rows):
                outs[lanes.start // rows + k][0] = attended[:, k * rows : (k + 1) * rows]

        for lanes in lane_chunks(0, newest * rows, 2 * rows):
            fresh = scores[at, lanes]
            before = stats[pl.ds(0, 1), lanes]
            top = jnp.maximum(before, jnp.max(fresh, axis=0, keepdims=True))
            correction = jnp.exp2(before - top)
            p = jnp.exp2(fresh - top)
            p_low = p.astype(jnp.bfloat16)
            scores[at, lanes] = p
            low[at, lanes] = p_low
            total = stats[pl.ds(1, 1), lanes] * correction + jnp.sum(p, axis=0, keepdims=True)
            weighted = mixed[:, lanes] * correction + dot(vt_all[:, at], p_low, NN)
            settle(lanes, total, correction, weighted)
        column = scores[:, at]
        p = jnp.exp2(column - jnp.max(column, axis=0, keepdims=True))
        p_low = p.astype(jnp.bfloat16)
        scores[:, at] = p
        low[:, at] = p_low
        settle(at, jnp.sum(p, axis=0, keepdims=True), 1.0, dot(vt_all[...], p_low, NN))

        for j, out in enumerate(outs):
            keys = pl.ds(j * rows, rows)
            row = 0 if j < newest else 2
            scaled = old_scaled if j < newest else new_scaled
            for lanes in lane_chunks(0, blocks * rows, 4 * rows):
                g = dots[keys, lanes] * factors[pl.ds(row, 1), lanes] - factors[pl.ds(row + 1, 1), lanes]
                grads_low[keys, lanes] = (scores[keys, lanes] * g).astype(jnp.bfloat16)
            out[2] = (dot(grads_low[keys, :], q_all[...], NN) * scaling).astype(jnp.bfloat16)
            out[3] = dot(low[keys, :], scaled[...], NT).astype(jnp.bfloat16)
        for lanes in lane_chunks(0, blocks * rows, 2 * rows):
            grad = (dot(kt_all[...], grads_low[:, lanes], NN) * scaling).astype(jnp.bfloat16)
            for k in range(lanes.size // rows):
                outs[lanes.start // rows + k][1] = grad[:, k * rows : (k + 1) * rows]


def per_device(query, key, value, grad_out, frame_ids, sink_frame, window):
    rows, row_width = query.shape
    heads = window.shape[0]
    width = row_width // heads
    blocks = lax.axis_size("tm")
    owned, sent, partner, pairs = plan(blocks, lax.axis_size("head"), heads)
    axes = ("tm", "head")
    smem = pl.BlockSpec(memory_space=pltpu.SMEM)
    vmem = pl.BlockSpec(memory_space=pltpu.VMEM)
    in_place = pl.BlockSpec(memory_space=pltpu.HBM)
    part = jax.ShapeDtypeStruct((4, rows, width), query.dtype)
    local = jax.ShapeDtypeStruct(query.shape, query.dtype)

    tokens = blocks * rows
    split = tokens <= split_limit
    tiles = 5 if split else 4
    home_tiles = vmem_bytes // (2 * rows * width)
    home, *parts = pl.pallas_call(
        functools.partial(pack_kernel, owned, partner, sent, width),
        out_shape=[jax.ShapeDtypeStruct((home_tiles, rows, width), query.dtype)] + [part] * (blocks - 1),
        in_specs=[in_place] * 7,
        out_specs=[in_place] * blocks,
        scratch_shapes=[
            pltpu.VMEM((4, rows, row_width), query.dtype),
            pltpu.VMEM((tiles, rows, width), query.dtype),
            pltpu.VMEM((blocks - 1, 4, rows, width), query.dtype),
            pltpu.SMEM(frame_ids.shape, jnp.int32),
            pltpu.SMEM(sink_frame.shape, jnp.int32),
            pltpu.SMEM(window.shape, jnp.int32),
            pltpu.SemaphoreType.DMA((7,)),
            pltpu.SemaphoreType.DMA((blocks,)),
        ],
        compiler_params=pltpu.CompilerParams(vmem_limit_bytes=62 * MIB),
        name="pack",
    )(query, key, value, grad_out, frame_ids, sink_frame, window)
    parts = [lax.ppermute(parts[s - 1], axes, pairs[s]) for s in range(1, blocks)]

    stretch = (4 if blocks % 4 == 0 else 2) * rows
    low, full = query.dtype, jnp.float32
    if split:
        square = jax.ShapeDtypeStruct((tokens, tokens), full)
        tall = jax.ShapeDtypeStruct((tokens, width), low)
        wide = jax.ShapeDtypeStruct((width, tokens), low)
        table = jax.ShapeDtypeStruct((blocks, tokens), full)
        held = [square] * 2 + [tall] * 3 + [wide] * 3
        flops = 2 * rows * rows * width
        bias, *state = pl.pallas_call(
            functools.partial(products_kernel, owned, blocks, rows),
            out_shape=[table, *held],
            in_specs=[in_place] + [vmem] * (blocks - 4),
            out_specs=[vmem] * 9,
            scratch_shapes=[pltpu.VMEM((tiles, rows, width), low), pltpu.SemaphoreType.DMA],
            compiler_params=pltpu.CompilerParams(vmem_limit_bytes=20 * MIB),
            cost_estimate=pl.CostEstimate(
                flops=2 * flops * (blocks - 3) ** 2, bytes_accessed=8 * tokens * tokens, transcendentals=0
            ),
            name="products",
        )(home, *parts[:-3])
        state = pl.pallas_call(
            functools.partial(join_kernel, owned, blocks - 3, rows),
            out_shape=held,
            in_specs=[vmem] * 10,
            out_specs=[vmem] * 8,
            input_output_aliases={2 + n: n for n in range(8)},
            compiler_params=pltpu.CompilerParams(vmem_limit_bytes=20 * MIB),
            cost_estimate=pl.CostEstimate(
                flops=4 * flops * blocks, bytes_accessed=16 * tokens * rows, transcendentals=0
            ),
            name="join",
        )(bias, parts[-3], *state)
        *state, weights_low, stats, mixed = pl.pallas_call(
            functools.partial(softmax_kernel, owned, blocks, rows),
            out_shape=[
                *held,
                jax.ShapeDtypeStruct((tokens, tokens), low),
                table,
                jax.ShapeDtypeStruct((width, tokens), full),
            ],
            in_specs=[vmem] * 10,
            out_specs=[vmem] * 11,
            input_output_aliases={2 + n: n for n in range(8)},
            compiler_params=pltpu.CompilerParams(vmem_limit_bytes=20 * MIB),
            cost_estimate=pl.CostEstimate(
                flops=3 * flops * blocks**2, bytes_accessed=8 * tokens * tokens, transcendentals=tokens * tokens
            ),
            name="softmax",
        )(bias, parts[-2], *state)
        parts = pl.pallas_call(
            functools.partial(finish_kernel, owned, blocks, rows),
            out_shape=[part] * blocks + held + [jax.ShapeDtypeStruct((tokens, tokens), low)],
            in_specs=[vmem] * 13,
            out_specs=[vmem] * (blocks + 9),
            input_output_aliases={4 + n: blocks + n for n in range(9)},
            scratch_shapes=[
                pltpu.VMEM((tokens, tokens), low),
                pltpu.VMEM((width, tokens), low),
                pltpu.VMEM((width, tokens), low),
                pltpu.VMEM((8, tokens), full),
            ],
            compiler_params=pltpu.CompilerParams(vmem_limit_bytes=24 * MIB),
            name="finish",
        )(bias, stats, mixed, parts[-1], *state, weights_low)[:blocks]
    else:
        parts = pl.pallas_call(
            functools.partial(head_kernel, owned, partner, rows),
            out_shape=[part] * blocks,
            in_specs=[smem] * 3 + [pl.BlockSpec(memory_space=pl.ANY)] + [vmem] * (blocks - 1),
            out_specs=[vmem] * blocks,
            scratch_shapes=[
                pltpu.VMEM((4, rows, width), low),
                pltpu.VMEM((tokens, width), low),
                pltpu.VMEM((width, tokens), low),
                pltpu.VMEM((width, tokens), low),
                pltpu.VMEM((width, tokens), low),
                pltpu.VMEM((tokens, stretch), full),
                pltpu.VMEM((tokens, stretch), low),
                pltpu.VMEM((tokens, stretch), low),
                pltpu.VMEM((width, stretch), low),
                pltpu.VMEM((tokens, width), full),
                pltpu.VMEM((tokens, width), full),
                pltpu.VMEM((blocks, 2, width, rows), low),
                pltpu.SemaphoreType.DMA,
            ],
            compiler_params=pltpu.CompilerParams(vmem_limit_bytes=48 * MIB),
            name="head_attention",
        )(frame_ids, sink_frame, window, home, *parts)
    back = [[(owner, source) for source, owner in step] for step in pairs]
    order = even_rounds_back if blocks == 8 and heads == 5 else range(1, blocks)
    parts = [parts[0]] + [lax.ppermute(parts[s], axes, back[s]) for s in order]

    return pl.pallas_call(
        functools.partial(unpack_kernel, sent[np.array([0, *order])], width),
        out_shape=[local] * 4,
        in_specs=[vmem] * blocks,
        out_specs=[vmem] * 4,
        compiler_params=pltpu.CompilerParams(vmem_limit_bytes=24 * MIB),
        name="unpack",
    )(*parts)


def solution(mesh):
    spec = P("tm", "head")
    return jax.shard_map(
        per_device,
        mesh=mesh,
        in_specs=(spec, spec, spec, spec, P(), P(), P("head")),
        out_specs=(spec, spec, spec, spec),
        check_vma=False,
    )
```

```python
import functools
import math

import jax
import jax.numpy as jnp
import numpy as np
from jax import lax
from jax.experimental import pallas as pl
from jax.experimental.pallas import tpu as pltpu
from jax.sharding import PartitionSpec as P

hidden_score = -1e30
MIB = 1 << 20
shared_vmem = 431 << 17
split_limit = 1024


even_rounds = (
    {
        1: (4, 6, 3, 2, 7, 0, 5),
        2: (3, 7, 5, 6, 1, 4, 0),
        3: (2, 0, 4, 5, 6, 7, 1),
        4: (7, 3, 2, 1, 0, 5, 6),
        5: (1, 2, 6, 0, 4, 3, 7),
    },
    {
        0: (5, 7, 6, 3, 1, 2, 4),
        1: (6, 4, 5, 7, 2, 3, 0),
        4: (0, 1, 7, 2, 5, 6, 3),
        6: (2, 5, 1, 4, 3, 0, 7),
        7: (3, 2, 0, 1, 4, 5, 6),
    },
)
even_rounds_back = (2, 4, 5, 6, 7, 1, 3)


def plan(blocks, groups, heads):
    laid_out = []
    for group in range(groups):
        if blocks == 8 and heads == 5:
            laid_out.append(even_rounds[group % 2])
        else:
            owners = [(head * blocks // heads + group % 2) % blocks for head in range(heads)]
            laid_out.append({u: [(u - step) % blocks for step in range(1, blocks)] for u in owners})
    owned = np.full((groups, blocks), -1)
    sent = np.full((blocks, groups, blocks), -1)
    partner = np.full((blocks, groups, blocks), -1)
    pairs = [[] for _ in range(blocks)]
    for group, rounds in enumerate(laid_out):
        for head, (owner, sources) in enumerate(rounds.items()):
            owned[group, owner] = head
            for step, source in enumerate((owner, *sources)):
                sent[step, group, source] = head
                partner[step, group, owner] = source
                pairs[step].append((source * groups + group, owner * groups + group))
    return owned, sent, partner, [sorted(step) for step in pairs]


def looked_up(table, group, block):
    groups, blocks = table.shape
    period = next(p for p in range(1, groups + 1) if (table == table[np.arange(groups) % p]).all())
    bits = int(table.max() + 1).bit_length()
    per_word = 31 // bits
    word = jnp.int32(0)
    for row in range(period):
        for first in range(0, blocks, per_word):
            values = table[row, first : first + per_word] + 1
            packed = sum(int(value) << (bits * n) for n, value in enumerate(values))
            here = (lax.rem(group, period) == row) & (block >= first) & (block < first + per_word)
            word = jnp.where(here, packed, word)
    return ((word >> (bits * lax.rem(block, per_word))) & ((1 << bits) - 1)) - 1


def dot(a, b, contract):
    return lax.dot_general(a, b, (contract, ((), ())), preferred_element_type=jnp.float32)


NN = ((1,), (0,))
NT = ((1,), (1,))


def head_columns(head, width):
    return pl.ds(pl.multiple_of(head * width, width), width)


def pack_kernel(sent, width, query, key, value, grad_out, *refs):
    outs, (staged, sems) = refs[:-2], refs[-2:]
    group, block = lax.axis_index("head"), lax.axis_index("tm")
    arrays = (query, key, value, grad_out)
    loads = [pltpu.make_async_copy(a, staged.at[n], sems.at[n]) for n, a in enumerate(arrays)]
    for load in loads:
        load.start()
    heads = [looked_up(table, group, block) for table in sent]
    for load in loads:
        load.wait()
    for out, head in zip(outs, heads):

        @pl.when(head >= 0)
        def _():
            columns = head_columns(head, width)
            for n in range(3):
                out[n] = staged[n, :, columns]
            out[3] = staged[3, :, columns].T


def unpack_kernel(sent, width, *refs):
    parts, (attended, query_grad, key_grad, value_grad) = refs[:-4], refs[-4:]
    group, block = lax.axis_index("head"), lax.axis_index("tm")
    for step, part in enumerate(parts):
        head = looked_up(sent[step], group, block)

        @pl.when(head >= 0)
        def _():
            columns = head_columns(head, width)
            attended[:, columns] = part[0].T
            query_grad[:, columns] = part[1].T
            key_grad[:, columns] = part[2]
            value_grad[:, columns] = part[3]


def head_kernel(owned, partner, rows, frame_ids, sink_frame, window, local, *refs):
    blocks = len(partner)
    parts, outs, scratch = refs[: blocks - 1], refs[blocks - 1 : 2 * blocks - 1], refs[2 * blocks - 1 :]
    (here, q_all, kt_all, vt_all, gt_all, weights, weights_low, grads_low, grad_scaled, dk, dv, res, sem) = scratch
    parts = (here, *parts)
    group, block = lax.axis_index("head"), lax.axis_index("tm")
    head = looked_up(owned, group, block)
    width = q_all.shape[1]
    scaling = 1.0 / math.sqrt(width)
    rescale = scaling * math.log2(math.e)
    stretch = weights.shape[1]
    half = stretch // 2
    each = half // rows

    @pl.when(head >= 0)
    def _():
        fetch = pltpu.make_async_copy(local, here, sem)
        fetch.start()
        span = window[head]
        sink = sink_frame[0]
        frames = [frame_ids[looked_up(table, group, block)] for table in partner]

        def placed(j):
            at = pl.ds(j * rows, rows)
            q_all[at, :] = parts[j][0]
            kt_all[:, at] = parts[j][1].T
            vt_all[:, at] = parts[j][2].T
            gt_all[:, at] = parts[j][3]

        for j in range(1, blocks):
            placed(j)
        fetch.wait()
        placed(0)
        dk[...] = jnp.zeros_like(dk)
        dv[...] = jnp.zeros_like(dv)
        lane_block = lax.broadcasted_iota(jnp.int32, (1, half), 1) // rows

        def one_stretch(i, carry):
            at = [pl.ds(pl.multiple_of(i * stretch + h * half, half), half) for h in range(2)]
            lanes = [pl.ds(h * half, half) for h in range(2)]
            keys = [pl.ds(j * rows, rows) for j in range(blocks)]
            q_rows = [q_all[at[h], :] for h in range(2)]
            top = [jnp.full((1, half), hidden_score, jnp.float32)] * 2
            total = [jnp.zeros((1, half), jnp.float32)] * 2
            delta = [None] * 2
            own = [[], []]
            for h in range(2):
                for k in range(each):
                    n = i * 2 * each + h * each + k
                    own[h].append(sum(jnp.where(n == j, frames[j], 0) for j in range(blocks)))

            def score(h, j):
                bias = jnp.zeros((1, half), jnp.float32)
                for k in range(each):
                    seen = (frames[j] <= own[h][k]) & (frames[j] > own[h][k] - span)
                    seen = seen | ((frames[j] == sink) & (sink <= own[h][k]))
                    bias = jnp.where(lane_block == k, jnp.where(seen, 0.0, hidden_score), bias)
                scores = dot(parts[j][1], q_rows[h], NT) * rescale + bias
                weights[keys[j], lanes[h]] = scores
                top[h] = jnp.maximum(top[h], jnp.max(scores, axis=0, keepdims=True))

            def weigh(h, j):
                p = jnp.exp2(weights[keys[j], lanes[h]] - top[h])
                total[h] = total[h] + jnp.sum(p, axis=0, keepdims=True)
                weights[keys[j], lanes[h]] = p
                weights_low[keys[j], lanes[h]] = p.astype(jnp.bfloat16)

            def attend(h):
                inverse = 1.0 / total[h]
                mixed = (dot(vt_all[...], weights_low[:, lanes[h]], NN) * inverse).astype(jnp.bfloat16)
                grad_t = gt_all[:, at[h]].astype(jnp.float32)
                delta[h] = jnp.sum(grad_t * mixed.astype(jnp.float32), axis=0, keepdims=True) * inverse
                grad_scaled[:, lanes[h]] = (grad_t * inverse).astype(jnp.bfloat16)
                for k in range(each):
                    res[i * 2 * each + h * each + k, 0] = mixed[:, k * rows : (k + 1) * rows]

            def differ(h, j):
                g = dot(parts[j][2], grad_scaled[:, lanes[h]], NN) - delta[h]
                grads_low[keys[j], lanes[h]] = (weights[keys[j], lanes[h]] * g).astype(jnp.bfloat16)

            def query_part(h):
                grad = (dot(kt_all[...], grads_low[:, lanes[h]], NN) * scaling).astype(jnp.bfloat16)
                for k in range(each):
                    res[i * 2 * each + h * each + k, 1] = grad[:, k * rows : (k + 1) * rows]

            for j in range(blocks):
                score(0, j)
            for j in range(blocks):
                score(1, j)
                weigh(0, j)
            attend(0)
            for j in range(blocks):
                weigh(1, j)
                differ(0, j)
            attend(1)
            query_part(0)
            q_both = jnp.concatenate(q_rows, axis=0)
            for j in range(blocks):
                differ(1, j)
                dk[keys[j], :] += dot(grads_low[keys[j], :], q_both, NN)
                dv[keys[j], :] += dot(weights_low[keys[j], :], grad_scaled[...], NT)
            query_part(1)
            return carry

        lax.fori_loop(0, blocks * rows // stretch, one_stretch, 0)
        for j, out in enumerate(outs):
            at = pl.ds(j * rows, rows)
            out[0] = res[j, 0]
            out[1] = res[j, 1]
            out[2] = (dk[at, :] * scaling).astype(jnp.bfloat16)
            out[3] = dv[at, :].astype(jnp.bfloat16)


def seen_bias(frame, own, span, sink):
    seen = ((frame <= own) & (frame > own - span)) | ((frame == sink) & (sink <= own))
    return jnp.where(seen, 0.0, hidden_score)


def frames_by_lane(frames, rows):
    lane_block = lax.broadcasted_iota(jnp.int32, (1, len(frames) * rows), 1) // rows
    row = jnp.zeros_like(lane_block)
    for n, frame in enumerate(frames):
        row = jnp.where(lane_block == n, frame, row)
    return row


def place_block(part, j, rows, q_all, k_all, v_all, kt_all, vt_all, gt_all):
    at = pl.ds(j * rows, rows)
    q_all[at, :] = part[0]
    k_all[at, :] = part[1]
    v_all[at, :] = part[2]
    kt_all[:, at] = part[1].T
    vt_all[:, at] = part[2].T
    gt_all[:, at] = part[3]


def pair_products(j, held, rows, bias, scores, dots, q_all, k_all, v_all, gt_all):
    width = q_all.shape[1]
    rescale = math.log2(math.e) / math.sqrt(width)
    before = held * rows
    at = pl.ds(j * rows, rows)
    every = pl.ds(0, before + rows)
    scores[at, every] = dot(k_all[at, :], q_all[every, :], NT) * rescale + bias[pl.ds(j, 1), every]
    dots[at, every] = dot(v_all[at, :], gt_all[:, every], NN)
    column = dot(k_all[pl.ds(0, before), :], q_all[at, :], NT) * rescale
    for n in range(held):
        keys = pl.ds(n * rows, rows)
        scores[keys, at] = column[n * rows : (n + 1) * rows, :] + bias[pl.ds(n, 1), at]
    dots[pl.ds(0, before), at] = dot(v_all[pl.ds(0, before), :], gt_all[:, at], NN)


def lane_chunks(start, stop, size):
    return [pl.ds(first, min(size, stop - first)) for first in range(start, stop, size)]


def products_kernel(owned, partner, rows, frame_ids, sink_frame, window, *refs):
    blocks = len(partner)
    held = blocks - 3
    parts, (bias, scores, dots, *places) = refs[:held], refs[held:]
    group, block = lax.axis_index("head"), lax.axis_index("tm")
    head = looked_up(owned, group, block)

    @pl.when(head >= 0)
    def _():
        span = window[head]
        sink = sink_frame[0]
        frames = [frame_ids[looked_up(table, group, block)] for table in partner]
        every = frames_by_lane(frames, rows)
        for j in range(blocks):
            bias[pl.ds(j, 1), :] = seen_bias(frames[j], every, span, sink)
        for j in range(held):
            place_block(parts[j], j, rows, *places)
        q_all, k_all, v_all, _, _, gt_all = places
        lanes = pl.ds(0, held * rows)
        rescale = math.log2(math.e) / math.sqrt(q_all.shape[1])
        for j in range(held):
            keys = pl.ds(j * rows, rows)
            scores[keys, lanes] = dot(parts[j][1], q_all[lanes, :], NT) * rescale + bias[pl.ds(j, 1), lanes]
            dots[keys, lanes] = dot(parts[j][2], gt_all[:, lanes], NN)


def join_kernel(owned, index, rows, bias, *refs):
    part, (scores, dots, q_all, k_all, v_all, kt_all, vt_all, gt_all) = refs[0], refs[9:]
    head = looked_up(owned, lax.axis_index("head"), lax.axis_index("tm"))

    @pl.when(head >= 0)
    def _():
        place_block(part, index, rows, q_all, k_all, v_all, kt_all, vt_all, gt_all)
        pair_products(index, index, rows, bias, scores, dots, q_all, k_all, v_all, gt_all)


def softmax_kernel(owned, blocks, rows, bias, *refs):
    part, refs = refs[0], refs[9:]
    scores, dots, q_all, k_all, v_all, kt_all, vt_all, gt_all, low, stats, mixed = refs
    head = looked_up(owned, lax.axis_index("head"), lax.axis_index("tm"))

    @pl.when(head >= 0)
    def _():
        newest = blocks - 2
        held = pl.ds(0, (newest + 1) * rows)
        place_block(part, newest, rows, q_all, k_all, v_all, kt_all, vt_all, gt_all)
        pair_products(newest, newest, rows, bias, scores, dots, q_all, k_all, v_all, gt_all)
        for lanes in lane_chunks(0, (newest + 1) * rows, 2 * rows):
            top = jnp.max(scores[held, lanes], axis=0, keepdims=True)
            total = jnp.zeros_like(top)
            for j in range(newest + 1):
                keys = pl.ds(j * rows, rows)
                p = jnp.exp2(scores[keys, lanes] - top)
                total = total + jnp.sum(p, axis=0, keepdims=True)
                scores[keys, lanes] = p
                low[keys, lanes] = p.astype(jnp.bfloat16)
            stats[pl.ds(0, 1), lanes] = top
            stats[pl.ds(1, 1), lanes] = total
            mixed[:, lanes] = dot(vt_all[:, held], low[held, lanes], NN)


def finish_kernel(owned, blocks, rows, bias, stats, mixed, *refs):
    part, refs = refs[0], refs[10:]
    outs, refs = refs[:blocks], refs[blocks:]
    scores, dots, q_all, k_all, v_all, kt_all, vt_all, gt_all, low, grads_low, old_scaled, new_scaled, factors = refs
    head = looked_up(owned, lax.axis_index("head"), lax.axis_index("tm"))
    width = q_all.shape[1]
    scaling = 1.0 / math.sqrt(width)

    @pl.when(head >= 0)
    def _():
        newest = blocks - 1
        at = pl.ds(newest * rows, rows)
        place_block(part, newest, rows, q_all, k_all, v_all, kt_all, vt_all, gt_all)
        pair_products(newest, newest, rows, bias, scores, dots, q_all, k_all, v_all, gt_all)

        def settle(lanes, total, old_factor, weighted):
            inverse = 1.0 / total
            attended = (weighted * inverse).astype(jnp.bfloat16)
            grad_t = gt_all[:, lanes].astype(jnp.float32)
            delta = jnp.sum(grad_t * attended.astype(jnp.float32), axis=0, keepdims=True)
            old = inverse * old_factor
            old_scaled[:, lanes] = (grad_t * old).astype(jnp.bfloat16)
            new_scaled[:, lanes] = (grad_t * inverse).astype(jnp.bfloat16)
            factors[pl.ds(0, 1), lanes] = old
            factors[pl.ds(1, 1), lanes] = delta * old
            factors[pl.ds(2, 1), lanes] = inverse
            factors[pl.ds(3, 1), lanes] = delta * inverse
            for k in range(lanes.size // rows):
                outs[lanes.start // rows + k][0] = attended[:, k * rows : (k + 1) * rows]

        for lanes in lane_chunks(0, newest * rows, 2 * rows):
            fresh = scores[at, lanes]
            before = stats[pl.ds(0, 1), lanes]
            top = jnp.maximum(before, jnp.max(fresh, axis=0, keepdims=True))
            correction = jnp.exp2(before - top)
            p = jnp.exp2(fresh - top)
            p_low = p.astype(jnp.bfloat16)
            scores[at, lanes] = p
            low[at, lanes] = p_low
            total = stats[pl.ds(1, 1), lanes] * correction + jnp.sum(p, axis=0, keepdims=True)
            weighted = mixed[:, lanes] * correction + dot(vt_all[:, at], p_low, NN)
            settle(lanes, total, correction, weighted)
        column = scores[:, at]
        p = jnp.exp2(column - jnp.max(column, axis=0, keepdims=True))
        p_low = p.astype(jnp.bfloat16)
        scores[:, at] = p
        low[:, at] = p_low
        settle(at, jnp.sum(p, axis=0, keepdims=True), 1.0, dot(vt_all[...], p_low, NN))

        for j, out in enumerate(outs):
            keys = pl.ds(j * rows, rows)
            row = 0 if j < newest else 2
            scaled = old_scaled if j < newest else new_scaled
            for lanes in lane_chunks(0, blocks * rows, 4 * rows):
                g = dots[keys, lanes] * factors[pl.ds(row, 1), lanes] - factors[pl.ds(row + 1, 1), lanes]
                grads_low[keys, lanes] = (scores[keys, lanes] * g).astype(jnp.bfloat16)
            out[2] = (dot(grads_low[keys, :], q_all[...], NN) * scaling).astype(jnp.bfloat16)
            out[3] = dot(low[keys, :], scaled[...], NT).astype(jnp.bfloat16)
        for lanes in lane_chunks(0, blocks * rows, 2 * rows):
            grad = (dot(kt_all[...], grads_low[:, lanes], NN) * scaling).astype(jnp.bfloat16)
            for k in range(lanes.size // rows):
                outs[lanes.start // rows + k][1] = grad[:, k * rows : (k + 1) * rows]


def per_device(query, key, value, grad_out, frame_ids, sink_frame, window):
    rows, row_width = query.shape
    heads = window.shape[0]
    width = row_width // heads
    blocks = lax.axis_size("tm")
    owned, sent, partner, pairs = plan(blocks, lax.axis_size("head"), heads)
    axes = ("tm", "head")
    smem = pl.BlockSpec(memory_space=pltpu.SMEM)
    vmem = pl.BlockSpec(memory_space=pltpu.VMEM)
    in_place = pl.BlockSpec(memory_space=pltpu.HBM)
    part = jax.ShapeDtypeStruct((4, rows, width), query.dtype)
    local = jax.ShapeDtypeStruct(query.shape, query.dtype)

    parts = pl.pallas_call(
        functools.partial(pack_kernel, sent, width),
        out_shape=[part] * blocks,
        in_specs=[in_place] * 4,
        out_specs=[vmem] * blocks,
        scratch_shapes=[pltpu.VMEM((4, rows, row_width), query.dtype), pltpu.SemaphoreType.DMA((4,))],
        compiler_params=pltpu.CompilerParams(vmem_limit_bytes=shared_vmem - blocks * 8 * rows * width),
        name="pack",
    )(query, key, value, grad_out)
    parts = [parts[0]] + [lax.ppermute(parts[s], axes, pairs[s]) for s in range(1, blocks)]

    tokens = blocks * rows
    stretch = (4 if blocks % 4 == 0 else 2) * rows
    low, full = query.dtype, jnp.float32
    if tokens <= split_limit:
        square = jax.ShapeDtypeStruct((tokens, tokens), full)
        tall = jax.ShapeDtypeStruct((tokens, width), low)
        wide = jax.ShapeDtypeStruct((width, tokens), low)
        table = jax.ShapeDtypeStruct((blocks, tokens), full)
        held = [square] * 2 + [tall] * 3 + [wide] * 3
        flops = 2 * rows * rows * width
        bias, *state = pl.pallas_call(
            functools.partial(products_kernel, owned, partner, rows),
            out_shape=[table, *held],
            in_specs=[smem] * 3 + [vmem] * (blocks - 3),
            out_specs=[vmem] * 9,
            compiler_params=pltpu.CompilerParams(vmem_limit_bytes=20 * MIB),
            cost_estimate=pl.CostEstimate(
                flops=2 * flops * (blocks - 3) ** 2, bytes_accessed=8 * tokens * tokens, transcendentals=0
            ),
            name="products",
        )(frame_ids, sink_frame, window, *parts[:-3])
        state = pl.pallas_call(
            functools.partial(join_kernel, owned, blocks - 3, rows),
            out_shape=held,
            in_specs=[vmem] * 10,
            out_specs=[vmem] * 8,
            input_output_aliases={2 + n: n for n in range(8)},
            compiler_params=pltpu.CompilerParams(vmem_limit_bytes=20 * MIB),
            cost_estimate=pl.CostEstimate(
                flops=4 * flops * blocks, bytes_accessed=16 * tokens * rows, transcendentals=0
            ),
            name="join",
        )(bias, parts[-3], *state)
        *state, weights_low, stats, mixed = pl.pallas_call(
            functools.partial(softmax_kernel, owned, blocks, rows),
            out_shape=[
                *held,
                jax.ShapeDtypeStruct((tokens, tokens), low),
                table,
                jax.ShapeDtypeStruct((width, tokens), full),
            ],
            in_specs=[vmem] * 10,
            out_specs=[vmem] * 11,
            input_output_aliases={2 + n: n for n in range(8)},
            compiler_params=pltpu.CompilerParams(vmem_limit_bytes=20 * MIB),
            cost_estimate=pl.CostEstimate(
                flops=3 * flops * blocks**2, bytes_accessed=8 * tokens * tokens, transcendentals=tokens * tokens
            ),
            name="softmax",
        )(bias, parts[-2], *state)
        parts = pl.pallas_call(
            functools.partial(finish_kernel, owned, blocks, rows),
            out_shape=[part] * blocks + held + [jax.ShapeDtypeStruct((tokens, tokens), low)],
            in_specs=[vmem] * 13,
            out_specs=[vmem] * (blocks + 9),
            input_output_aliases={4 + n: blocks + n for n in range(9)},
            scratch_shapes=[
                pltpu.VMEM((tokens, tokens), low),
                pltpu.VMEM((width, tokens), low),
                pltpu.VMEM((width, tokens), low),
                pltpu.VMEM((8, tokens), full),
            ],
            compiler_params=pltpu.CompilerParams(vmem_limit_bytes=24 * MIB),
            name="finish",
        )(bias, stats, mixed, parts[-1], *state, weights_low)[:blocks]
    else:
        parts = pl.pallas_call(
            functools.partial(head_kernel, owned, partner, rows),
            out_shape=[part] * blocks,
            in_specs=[smem] * 3 + [pl.BlockSpec(memory_space=pl.ANY)] + [vmem] * (blocks - 1),
            out_specs=[vmem] * blocks,
            scratch_shapes=[
                pltpu.VMEM((4, rows, width), low),
                pltpu.VMEM((tokens, width), low),
                pltpu.VMEM((width, tokens), low),
                pltpu.VMEM((width, tokens), low),
                pltpu.VMEM((width, tokens), low),
                pltpu.VMEM((tokens, stretch), full),
                pltpu.VMEM((tokens, stretch), low),
                pltpu.VMEM((tokens, stretch), low),
                pltpu.VMEM((width, stretch), low),
                pltpu.VMEM((tokens, width), full),
                pltpu.VMEM((tokens, width), full),
                pltpu.VMEM((blocks, 2, width, rows), low),
                pltpu.SemaphoreType.DMA,
            ],
            compiler_params=pltpu.CompilerParams(vmem_limit_bytes=48 * MIB),
            name="head_attention",
        )(frame_ids, sink_frame, window, *parts)
    back = [[(owner, source) for source, owner in step] for step in pairs]
    order = even_rounds_back if blocks == 8 and heads == 5 else range(1, blocks)
    parts = [parts[0]] + [lax.ppermute(parts[s], axes, back[s]) for s in order]

    return pl.pallas_call(
        functools.partial(unpack_kernel, sent[np.array([0, *order])], width),
        out_shape=[local] * 4,
        in_specs=[vmem] * blocks,
        out_specs=[vmem] * 4,
        compiler_params=pltpu.CompilerParams(vmem_limit_bytes=24 * MIB),
        name="unpack",
    )(*parts)


def solution(mesh):
    spec = P("tm", "head")
    return jax.shard_map(
        per_device,
        mesh=mesh,
        in_specs=(spec, spec, spec, spec, P(), P(), P("head")),
        out_specs=(spec, spec, spec, spec),
        check_vma=False,
    )
```

```python
import functools
import math

import jax
import jax.numpy as jnp
import numpy as np
from jax import lax
from jax.experimental import pallas as pl
from jax.experimental.pallas import tpu as pltpu
from jax.sharding import PartitionSpec as P

hidden_score = -1e30
MIB = 1 << 20
vmem_bytes = 64 * MIB
split_limit = 1024


even_rounds = (
    {
        1: (4, 6, 3, 2, 7, 0, 5),
        2: (3, 7, 5, 6, 1, 4, 0),
        3: (2, 0, 4, 5, 6, 7, 1),
        4: (7, 3, 2, 1, 0, 5, 6),
        5: (1, 2, 6, 0, 4, 3, 7),
    },
    {
        0: (5, 7, 6, 3, 1, 2, 4),
        1: (6, 4, 5, 7, 2, 3, 0),
        4: (0, 1, 7, 2, 5, 6, 3),
        6: (2, 5, 1, 4, 3, 0, 7),
        7: (3, 2, 0, 1, 4, 5, 6),
    },
)
even_rounds_back = (2, 4, 5, 1, 3, 6, 7)


def plan(blocks, groups, heads):
    laid_out = []
    for group in range(groups):
        if blocks == 8 and heads == 5:
            laid_out.append(even_rounds[group % 2])
        else:
            owners = [(head * blocks // heads + group % 2) % blocks for head in range(heads)]
            laid_out.append({u: [(u - step) % blocks for step in range(1, blocks)] for u in owners})
    owned = np.full((groups, blocks), -1)
    sent = np.full((blocks, groups, blocks), -1)
    partner = np.full((blocks, groups, blocks), -1)
    pairs = [[] for _ in range(blocks)]
    for group, rounds in enumerate(laid_out):
        for head, (owner, sources) in enumerate(rounds.items()):
            owned[group, owner] = head
            for step, source in enumerate((owner, *sources)):
                sent[step, group, source] = head
                partner[step, group, owner] = source
                pairs[step].append((source * groups + group, owner * groups + group))
    return owned, sent, partner, [sorted(step) for step in pairs]


def looked_up(table, group, block):
    groups, blocks = table.shape
    period = next(p for p in range(1, groups + 1) if (table == table[np.arange(groups) % p]).all())
    bits = int(table.max() + 1).bit_length()
    per_word = 31 // bits
    word = jnp.int32(0)
    for row in range(period):
        for first in range(0, blocks, per_word):
            values = table[row, first : first + per_word] + 1
            packed = sum(int(value) << (bits * n) for n, value in enumerate(values))
            here = (lax.rem(group, period) == row) & (block >= first) & (block < first + per_word)
            word = jnp.where(here, packed, word)
    return ((word >> (bits * lax.rem(block, per_word))) & ((1 << bits) - 1)) - 1


def dot(a, b, contract):
    return lax.dot_general(a, b, (contract, ((), ())), preferred_element_type=jnp.float32)


NN = ((1,), (0,))
NT = ((1,), (1,))


def head_columns(head, width):
    return pl.ds(pl.multiple_of(head * width, width), width)


def pack_kernel(owned, partner, sent, width, query, key, value, grad_out, frame_ids, sink_frame, window, *refs):
    blocks = len(sent)
    home, outs, refs = refs[0], refs[1:blocks], refs[blocks:]
    staged, tiles, packed, frames_here, sink_here, window_here, in_sems, out_sems = refs
    group, block = lax.axis_index("head"), lax.axis_index("tm")
    arrays = (query, key, value, grad_out)
    loads = [pltpu.make_async_copy(a, staged.at[n], in_sems.at[n]) for n, a in enumerate(arrays)]
    small = ((frame_ids, frames_here), (sink_frame, sink_here), (window, window_here))
    loads += [pltpu.make_async_copy(a, here, in_sems.at[4 + n]) for n, (a, here) in enumerate(small)]
    for load in loads:
        load.start()
    heads = [looked_up(table, group, block) for table in sent]
    stores = [pltpu.make_async_copy(packed.at[n], out, out_sems.at[1 + n]) for n, out in enumerate(outs)]
    keep = pltpu.make_async_copy(tiles, home.at[pl.ds(0, tiles.shape[0])], out_sems.at[0])
    for load in loads:
        load.wait()

    def fill(target, head):
        columns = head_columns(head, width)
        for n in range(3):
            target[n] = staged[n, :, columns]
        target[3] = staged[3, :, columns].T

    for step, head in enumerate(heads[1:]):

        @pl.when(head >= 0)
        def _():
            fill(packed.at[step], head)
            stores[step].start()

    @pl.when(heads[0] >= 0)
    def _():
        fill(tiles, heads[0])
        if tiles.shape[0] > 4:
            frames = [frames_here[looked_up(table, group, block)] for table in partner]
            row = lax.broadcasted_iota(jnp.int32, tiles.shape[1:], 0)
            theirs, own = jnp.zeros_like(row), jnp.zeros_like(row)
            for n, frame in enumerate(frames):
                theirs = jnp.where(row // blocks == n, frame, theirs)
                own = jnp.where(lax.rem(row, blocks) == n, frame, own)
            tiles[4] = seen_bias(theirs, own, window_here[heads[0]], sink_here[0]).astype(tiles.dtype)
        keep.start()

    for step, head in enumerate(heads[1:]):

        @pl.when(head >= 0)
        def _():
            stores[step].wait()

    @pl.when(heads[0] >= 0)
    def _():
        keep.wait()


def unpack_kernel(sent, width, *refs):
    parts, (attended, query_grad, key_grad, value_grad) = refs[:-4], refs[-4:]
    group, block = lax.axis_index("head"), lax.axis_index("tm")
    for step, part in enumerate(parts):
        head = looked_up(sent[step], group, block)

        @pl.when(head >= 0)
        def _():
            columns = head_columns(head, width)
            attended[:, columns] = part[0].T
            query_grad[:, columns] = part[1].T
            key_grad[:, columns] = part[2]
            value_grad[:, columns] = part[3]


def head_kernel(owned, partner, rows, frame_ids, sink_frame, window, local, *refs):
    blocks = len(partner)
    parts, outs, scratch = refs[: blocks - 1], refs[blocks - 1 : 2 * blocks - 1], refs[2 * blocks - 1 :]
    (here, q_all, kt_all, vt_all, gt_all, weights, weights_low, grads_low, grad_scaled, dk, dv, res, sem) = scratch
    parts = (here, *parts)
    group, block = lax.axis_index("head"), lax.axis_index("tm")
    head = looked_up(owned, group, block)
    width = q_all.shape[1]
    scaling = 1.0 / math.sqrt(width)
    rescale = scaling * math.log2(math.e)
    stretch = weights.shape[1]
    half = stretch // 2
    each = half // rows

    @pl.when(head >= 0)
    def _():
        fetch = pltpu.make_async_copy(local.at[pl.ds(0, 4)], here, sem)
        fetch.start()
        span = window[head]
        sink = sink_frame[0]
        frames = [frame_ids[looked_up(table, group, block)] for table in partner]

        def placed(j):
            at = pl.ds(j * rows, rows)
            q_all[at, :] = parts[j][0]
            kt_all[:, at] = parts[j][1].T
            vt_all[:, at] = parts[j][2].T
            gt_all[:, at] = parts[j][3]

        for j in range(1, blocks):
            placed(j)
        fetch.wait()
        placed(0)
        dk[...] = jnp.zeros_like(dk)
        dv[...] = jnp.zeros_like(dv)
        lane_block = lax.broadcasted_iota(jnp.int32, (1, half), 1) // rows

        def one_stretch(i, carry):
            at = [pl.ds(pl.multiple_of(i * stretch + h * half, half), half) for h in range(2)]
            lanes = [pl.ds(h * half, half) for h in range(2)]
            keys = [pl.ds(j * rows, rows) for j in range(blocks)]
            q_rows = [q_all[at[h], :] for h in range(2)]
            top = [jnp.full((1, half), hidden_score, jnp.float32)] * 2
            total = [jnp.zeros((1, half), jnp.float32)] * 2
            delta = [None] * 2
            own = [[], []]
            for h in range(2):
                for k in range(each):
                    n = i * 2 * each + h * each + k
                    own[h].append(sum(jnp.where(n == j, frames[j], 0) for j in range(blocks)))

            def score(h, j):
                bias = jnp.zeros((1, half), jnp.float32)
                for k in range(each):
                    seen = (frames[j] <= own[h][k]) & (frames[j] > own[h][k] - span)
                    seen = seen | ((frames[j] == sink) & (sink <= own[h][k]))
                    bias = jnp.where(lane_block == k, jnp.where(seen, 0.0, hidden_score), bias)
                scores = dot(parts[j][1], q_rows[h], NT) * rescale + bias
                weights[keys[j], lanes[h]] = scores
                top[h] = jnp.maximum(top[h], jnp.max(scores, axis=0, keepdims=True))

            def weigh(h, j):
                p = jnp.exp2(weights[keys[j], lanes[h]] - top[h])
                total[h] = total[h] + jnp.sum(p, axis=0, keepdims=True)
                weights[keys[j], lanes[h]] = p
                weights_low[keys[j], lanes[h]] = p.astype(jnp.bfloat16)

            def attend(h):
                inverse = 1.0 / total[h]
                mixed = (dot(vt_all[...], weights_low[:, lanes[h]], NN) * inverse).astype(jnp.bfloat16)
                grad_t = gt_all[:, at[h]].astype(jnp.float32)
                delta[h] = jnp.sum(grad_t * mixed.astype(jnp.float32), axis=0, keepdims=True) * inverse
                grad_scaled[:, lanes[h]] = (grad_t * inverse).astype(jnp.bfloat16)
                for k in range(each):
                    res[i * 2 * each + h * each + k, 0] = mixed[:, k * rows : (k + 1) * rows]

            def differ(h, j):
                g = dot(parts[j][2], grad_scaled[:, lanes[h]], NN) - delta[h]
                grads_low[keys[j], lanes[h]] = (weights[keys[j], lanes[h]] * g).astype(jnp.bfloat16)

            def query_part(h):
                grad = (dot(kt_all[...], grads_low[:, lanes[h]], NN) * scaling).astype(jnp.bfloat16)
                for k in range(each):
                    res[i * 2 * each + h * each + k, 1] = grad[:, k * rows : (k + 1) * rows]

            for j in range(blocks):
                score(0, j)
            for j in range(blocks):
                score(1, j)
                weigh(0, j)
            attend(0)
            for j in range(blocks):
                weigh(1, j)
                differ(0, j)
            attend(1)
            query_part(0)
            q_both = jnp.concatenate(q_rows, axis=0)
            for j in range(blocks):
                differ(1, j)
                dk[keys[j], :] += dot(grads_low[keys[j], :], q_both, NN)
                dv[keys[j], :] += dot(weights_low[keys[j], :], grad_scaled[...], NT)
            query_part(1)
            return carry

        lax.fori_loop(0, blocks * rows // stretch, one_stretch, 0)
        for j, out in enumerate(outs):
            at = pl.ds(j * rows, rows)
            out[0] = res[j, 0]
            out[1] = res[j, 1]
            out[2] = (dk[at, :] * scaling).astype(jnp.bfloat16)
            out[3] = dv[at, :].astype(jnp.bfloat16)


def seen_bias(frame, own, span, sink):
    seen = ((frame <= own) & (frame > own - span)) | ((frame == sink) & (sink <= own))
    return jnp.where(seen, 0.0, hidden_score)


def frames_by_lane(frames, rows):
    lane_block = lax.broadcasted_iota(jnp.int32, (1, len(frames) * rows), 1) // rows
    row = jnp.zeros_like(lane_block)
    for n, frame in enumerate(frames):
        row = jnp.where(lane_block == n, frame, row)
    return row


def place_block(part, j, rows, q_all, k_all, v_all, kt_all, vt_all, gt_all):
    at = pl.ds(j * rows, rows)
    q_all[at, :] = part[0]
    k_all[at, :] = part[1]
    v_all[at, :] = part[2]
    kt_all[:, at] = part[1].T
    vt_all[:, at] = part[2].T
    gt_all[:, at] = part[3]


def pair_products(j, held, rows, bias, scores, dots, q_all, k_all, v_all, gt_all):
    width = q_all.shape[1]
    rescale = math.log2(math.e) / math.sqrt(width)
    before = held * rows
    at = pl.ds(j * rows, rows)
    every = pl.ds(0, before + rows)
    scores[at, every] = dot(k_all[at, :], q_all[every, :], NT) * rescale + bias[pl.ds(j, 1), every]
    dots[at, every] = dot(v_all[at, :], gt_all[:, every], NN)
    column = dot(k_all[pl.ds(0, before), :], q_all[at, :], NT) * rescale
    for n in range(held):
        keys = pl.ds(n * rows, rows)
        scores[keys, at] = column[n * rows : (n + 1) * rows, :] + bias[pl.ds(n, 1), at]
    dots[pl.ds(0, before), at] = dot(v_all[pl.ds(0, before), :], gt_all[:, at], NN)


def lane_chunks(start, stop, size):
    return [pl.ds(first, min(size, stop - first)) for first in range(start, stop, size)]


def products_kernel(owned, blocks, rows, home, *refs):
    held = blocks - 3
    parts, refs = refs[: held - 1], refs[held - 1 :]
    bias, scores, dots, *places, tiles, sem = refs
    head = looked_up(owned, lax.axis_index("head"), lax.axis_index("tm"))

    @pl.when(head >= 0)
    def _():
        fetch = pltpu.make_async_copy(home.at[pl.ds(0, tiles.shape[0])], tiles, sem)
        fetch.start()
        for j, part in enumerate(parts):
            place_block(part, j + 1, rows, *places)
        fetch.wait()
        place_block(tiles, 0, rows, *places)
        mask = tiles[4].astype(jnp.float32)
        for j in range(blocks):
            for n in range(blocks):
                row = j * blocks + n
                bias[pl.ds(j, 1), pl.ds(n * rows, rows)] = mask[row : row + 1, :]
        q_all, k_all, v_all, _, _, gt_all = places
        lanes = pl.ds(0, held * rows)
        rescale = math.log2(math.e) / math.sqrt(q_all.shape[1])
        for j in range(held):
            keys = pl.ds(j * rows, rows)
            scores[keys, lanes] = dot(k_all[keys, :], q_all[lanes, :], NT) * rescale + bias[pl.ds(j, 1), lanes]
            dots[keys, lanes] = dot(v_all[keys, :], gt_all[:, lanes], NN)


def join_kernel(owned, index, rows, bias, *refs):
    part, (scores, dots, q_all, k_all, v_all, kt_all, vt_all, gt_all) = refs[0], refs[9:]
    head = looked_up(owned, lax.axis_index("head"), lax.axis_index("tm"))

    @pl.when(head >= 0)
    def _():
        place_block(part, index, rows, q_all, k_all, v_all, kt_all, vt_all, gt_all)
        pair_products(index, index, rows, bias, scores, dots, q_all, k_all, v_all, gt_all)


def softmax_kernel(owned, blocks, rows, bias, *refs):
    part, refs = refs[0], refs[9:]
    scores, dots, q_all, k_all, v_all, kt_all, vt_all, gt_all, low, stats, mixed = refs
    head = looked_up(owned, lax.axis_index("head"), lax.axis_index("tm"))

    @pl.when(head >= 0)
    def _():
        newest = blocks - 2
        held = pl.ds(0, (newest + 1) * rows)
        place_block(part, newest, rows, q_all, k_all, v_all, kt_all, vt_all, gt_all)
        pair_products(newest, newest, rows, bias, scores, dots, q_all, k_all, v_all, gt_all)
        for lanes in lane_chunks(0, (newest + 1) * rows, 2 * rows):
            top = jnp.max(scores[held, lanes], axis=0, keepdims=True)
            total = jnp.zeros_like(top)
            for j in range(newest + 1):
                keys = pl.ds(j * rows, rows)
                p = jnp.exp2(scores[keys, lanes] - top)
                total = total + jnp.sum(p, axis=0, keepdims=True)
                scores[keys, lanes] = p
                low[keys, lanes] = p.astype(jnp.bfloat16)
            stats[pl.ds(0, 1), lanes] = top
            stats[pl.ds(1, 1), lanes] = total
            mixed[:, lanes] = dot(vt_all[:, held], low[held, lanes], NN)


def finish_kernel(owned, blocks, rows, bias, stats, mixed, *refs):
    part, refs = refs[0], refs[10:]
    outs, refs = refs[:blocks], refs[blocks:]
    scores, dots, q_all, k_all, v_all, kt_all, vt_all, gt_all, low, grads_low, old_scaled, new_scaled, factors = refs
    head = looked_up(owned, lax.axis_index("head"), lax.axis_index("tm"))
    width = q_all.shape[1]
    scaling = 1.0 / math.sqrt(width)

    @pl.when(head >= 0)
    def _():
        newest = blocks - 1
        at = pl.ds(newest * rows, rows)
        place_block(part, newest, rows, q_all, k_all, v_all, kt_all, vt_all, gt_all)
        pair_products(newest, newest, rows, bias, scores, dots, q_all, k_all, v_all, gt_all)

        def settle(lanes, total, old_factor, weighted):
            inverse = 1.0 / total
            attended = (weighted * inverse).astype(jnp.bfloat16)
            grad_t = gt_all[:, lanes].astype(jnp.float32)
            delta = jnp.sum(grad_t * attended.astype(jnp.float32), axis=0, keepdims=True)
            old = inverse * old_factor
            old_scaled[:, lanes] = (grad_t * old).astype(jnp.bfloat16)
            new_scaled[:, lanes] = (grad_t * inverse).astype(jnp.bfloat16)
            factors[pl.ds(0, 1), lanes] = old
            factors[pl.ds(1, 1), lanes] = delta * old
            factors[pl.ds(2, 1), lanes] = inverse
            factors[pl.ds(3, 1), lanes] = delta * inverse
            for k in range(lanes.size // rows):
                outs[lanes.start // rows + k][0] = attended[:, k * rows : (k + 1) * rows]

        for lanes in lane_chunks(0, newest * rows, 2 * rows):
            fresh = scores[at, lanes]
            before = stats[pl.ds(0, 1), lanes]
            top = jnp.maximum(before, jnp.max(fresh, axis=0, keepdims=True))
            correction = jnp.exp2(before - top)
            p = jnp.exp2(fresh - top)
            p_low = p.astype(jnp.bfloat16)
            scores[at, lanes] = p
            low[at, lanes] = p_low
            total = stats[pl.ds(1, 1), lanes] * correction + jnp.sum(p, axis=0, keepdims=True)
            weighted = mixed[:, lanes] * correction + dot(vt_all[:, at], p_low, NN)
            settle(lanes, total, correction, weighted)
        column = scores[:, at]
        p = jnp.exp2(column - jnp.max(column, axis=0, keepdims=True))
        p_low = p.astype(jnp.bfloat16)
        scores[:, at] = p
        low[:, at] = p_low
        settle(at, jnp.sum(p, axis=0, keepdims=True), 1.0, dot(vt_all[...], p_low, NN))

        for j, out in enumerate(outs):
            keys = pl.ds(j * rows, rows)
            row = 0 if j < newest else 2
            scaled = old_scaled if j < newest else new_scaled
            for lanes in lane_chunks(0, blocks * rows, 4 * rows):
                g = dots[keys, lanes] * factors[pl.ds(row, 1), lanes] - factors[pl.ds(row + 1, 1), lanes]
                grads_low[keys, lanes] = (scores[keys, lanes] * g).astype(jnp.bfloat16)
            out[2] = (dot(grads_low[keys, :], q_all[...], NN) * scaling).astype(jnp.bfloat16)
            out[3] = dot(low[keys, :], scaled[...], NT).astype(jnp.bfloat16)
        for lanes in lane_chunks(0, blocks * rows, 2 * rows):
            grad = (dot(kt_all[...], grads_low[:, lanes], NN) * scaling).astype(jnp.bfloat16)
            for k in range(lanes.size // rows):
                outs[lanes.start // rows + k][1] = grad[:, k * rows : (k + 1) * rows]


def per_device(query, key, value, grad_out, frame_ids, sink_frame, window):
    rows, row_width = query.shape
    heads = window.shape[0]
    width = row_width // heads
    blocks = lax.axis_size("tm")
    owned, sent, partner, pairs = plan(blocks, lax.axis_size("head"), heads)
    axes = ("tm", "head")
    smem = pl.BlockSpec(memory_space=pltpu.SMEM)
    vmem = pl.BlockSpec(memory_space=pltpu.VMEM)
    in_place = pl.BlockSpec(memory_space=pltpu.HBM)
    part = jax.ShapeDtypeStruct((4, rows, width), query.dtype)
    local = jax.ShapeDtypeStruct(query.shape, query.dtype)

    tokens = blocks * rows
    split = tokens <= split_limit
    tiles = 5 if split else 4
    home_tiles = vmem_bytes // (2 * rows * width)
    home, *parts = pl.pallas_call(
        functools.partial(pack_kernel, owned, partner, sent, width),
        out_shape=[jax.ShapeDtypeStruct((home_tiles, rows, width), query.dtype)] + [part] * (blocks - 1),
        in_specs=[in_place] * 7,
        out_specs=[in_place] * blocks,
        scratch_shapes=[
            pltpu.VMEM((4, rows, row_width), query.dtype),
            pltpu.VMEM((tiles, rows, width), query.dtype),
            pltpu.VMEM((blocks - 1, 4, rows, width), query.dtype),
            pltpu.SMEM(frame_ids.shape, jnp.int32),
            pltpu.SMEM(sink_frame.shape, jnp.int32),
            pltpu.SMEM(window.shape, jnp.int32),
            pltpu.SemaphoreType.DMA((7,)),
            pltpu.SemaphoreType.DMA((blocks,)),
        ],
        compiler_params=pltpu.CompilerParams(vmem_limit_bytes=62 * MIB),
        name="pack",
    )(query, key, value, grad_out, frame_ids, sink_frame, window)
    parts = [lax.ppermute(parts[s - 1], axes, pairs[s]) for s in range(1, blocks)]

    stretch = (4 if blocks % 4 == 0 else 2) * rows
    low, full = query.dtype, jnp.float32
    if split:
        square = jax.ShapeDtypeStruct((tokens, tokens), full)
        tall = jax.ShapeDtypeStruct((tokens, width), low)
        wide = jax.ShapeDtypeStruct((width, tokens), low)
        table = jax.ShapeDtypeStruct((blocks, tokens), full)
        held = [square] * 2 + [tall] * 3 + [wide] * 3
        flops = 2 * rows * rows * width
        bias, *state = pl.pallas_call(
            functools.partial(products_kernel, owned, blocks, rows),
            out_shape=[table, *held],
            in_specs=[in_place] + [vmem] * (blocks - 4),
            out_specs=[vmem] * 9,
            scratch_shapes=[pltpu.VMEM((tiles, rows, width), low), pltpu.SemaphoreType.DMA],
            compiler_params=pltpu.CompilerParams(vmem_limit_bytes=20 * MIB),
            cost_estimate=pl.CostEstimate(
                flops=2 * flops * (blocks - 3) ** 2, bytes_accessed=8 * tokens * tokens, transcendentals=0
            ),
            name="products",
        )(home, *parts[:-3])
        state = pl.pallas_call(
            functools.partial(join_kernel, owned, blocks - 3, rows),
            out_shape=held,
            in_specs=[vmem] * 10,
            out_specs=[vmem] * 8,
            input_output_aliases={2 + n: n for n in range(8)},
            compiler_params=pltpu.CompilerParams(vmem_limit_bytes=20 * MIB),
            cost_estimate=pl.CostEstimate(
                flops=4 * flops * blocks, bytes_accessed=16 * tokens * rows, transcendentals=0
            ),
            name="join",
        )(bias, parts[-3], *state)
        *state, weights_low, stats, mixed = pl.pallas_call(
            functools.partial(softmax_kernel, owned, blocks, rows),
            out_shape=[
                *held,
                jax.ShapeDtypeStruct((tokens, tokens), low),
                table,
                jax.ShapeDtypeStruct((width, tokens), full),
            ],
            in_specs=[vmem] * 10,
            out_specs=[vmem] * 11,
            input_output_aliases={2 + n: n for n in range(8)},
            compiler_params=pltpu.CompilerParams(vmem_limit_bytes=20 * MIB),
            cost_estimate=pl.CostEstimate(
                flops=3 * flops * blocks**2, bytes_accessed=8 * tokens * tokens, transcendentals=tokens * tokens
            ),
            name="softmax",
        )(bias, parts[-2], *state)
        parts = pl.pallas_call(
            functools.partial(finish_kernel, owned, blocks, rows),
            out_shape=[part] * blocks + held + [jax.ShapeDtypeStruct((tokens, tokens), low)],
            in_specs=[vmem] * 13,
            out_specs=[vmem] * (blocks + 9),
            input_output_aliases={4 + n: blocks + n for n in range(9)},
            scratch_shapes=[
                pltpu.VMEM((tokens, tokens), low),
                pltpu.VMEM((width, tokens), low),
                pltpu.VMEM((width, tokens), low),
                pltpu.VMEM((8, tokens), full),
            ],
            compiler_params=pltpu.CompilerParams(vmem_limit_bytes=24 * MIB),
            name="finish",
        )(bias, stats, mixed, parts[-1], *state, weights_low)[:blocks]
    else:
        parts = pl.pallas_call(
            functools.partial(head_kernel, owned, partner, rows),
            out_shape=[part] * blocks,
            in_specs=[smem] * 3 + [pl.BlockSpec(memory_space=pl.ANY)] + [vmem] * (blocks - 1),
            out_specs=[vmem] * blocks,
            scratch_shapes=[
                pltpu.VMEM((4, rows, width), low),
                pltpu.VMEM((tokens, width), low),
                pltpu.VMEM((width, tokens), low),
                pltpu.VMEM((width, tokens), low),
                pltpu.VMEM((width, tokens), low),
                pltpu.VMEM((tokens, stretch), full),
                pltpu.VMEM((tokens, stretch), low),
                pltpu.VMEM((tokens, stretch), low),
                pltpu.VMEM((width, stretch), low),
                pltpu.VMEM((tokens, width), full),
                pltpu.VMEM((tokens, width), full),
                pltpu.VMEM((blocks, 2, width, rows), low),
                pltpu.SemaphoreType.DMA,
            ],
            compiler_params=pltpu.CompilerParams(vmem_limit_bytes=48 * MIB),
            name="head_attention",
        )(frame_ids, sink_frame, window, home, *parts)
    back = [[(owner, source) for source, owner in step] for step in pairs]
    order = even_rounds_back if blocks == 8 and heads == 5 else range(1, blocks)
    parts = [parts[0]] + [lax.ppermute(parts[s], axes, back[s]) for s in order]

    return pl.pallas_call(
        functools.partial(unpack_kernel, sent[np.array([0, *order])], width),
        out_shape=[local] * 4,
        in_specs=[vmem] * blocks,
        out_specs=[vmem] * 4,
        compiler_params=pltpu.CompilerParams(vmem_limit_bytes=24 * MIB),
        name="unpack",
    )(*parts)


def solution(mesh):
    spec = P("tm", "head")
    return jax.shard_map(
        per_device,
        mesh=mesh,
        in_specs=(spec, spec, spec, spec, P(), P(), P("head")),
        out_specs=(spec, spec, spec, spec),
        check_vma=False,
    )
```

```python
import functools
import math

import jax
import jax.numpy as jnp
import numpy as np
from jax import lax
from jax.experimental import pallas as pl
from jax.experimental.pallas import tpu as pltpu
from jax.sharding import PartitionSpec as P

hidden_score = -1e30
MIB = 1 << 20
vmem_bytes = 64 * MIB
split_limit = 1024


even_rounds = (
    {
        1: (4, 6, 3, 2, 7, 0, 5),
        2: (3, 7, 5, 6, 1, 4, 0),
        3: (2, 0, 4, 5, 6, 7, 1),
        4: (7, 3, 2, 1, 0, 5, 6),
        5: (1, 2, 6, 0, 4, 3, 7),
    },
    {
        0: (5, 7, 6, 3, 1, 2, 4),
        1: (6, 4, 5, 7, 2, 3, 0),
        4: (0, 1, 7, 2, 5, 6, 3),
        6: (2, 5, 1, 4, 3, 0, 7),
        7: (3, 2, 0, 1, 4, 5, 6),
    },
)
even_rounds_back = (2, 4, 1, 3, 5, 6, 7)


def plan(blocks, groups, heads):
    laid_out = []
    for group in range(groups):
        if blocks == 8 and heads == 5:
            laid_out.append(even_rounds[group % 2])
        else:
            owners = [(head * blocks // heads + group % 2) % blocks for head in range(heads)]
            laid_out.append({u: [(u - step) % blocks for step in range(1, blocks)] for u in owners})
    owned = np.full((groups, blocks), -1)
    sent = np.full((blocks, groups, blocks), -1)
    partner = np.full((blocks, groups, blocks), -1)
    pairs = [[] for _ in range(blocks)]
    for group, rounds in enumerate(laid_out):
        for head, (owner, sources) in enumerate(rounds.items()):
            owned[group, owner] = head
            for step, source in enumerate((owner, *sources)):
                sent[step, group, source] = head
                partner[step, group, owner] = source
                pairs[step].append((source * groups + group, owner * groups + group))
    return owned, sent, partner, [sorted(step) for step in pairs]


def looked_up(table, group, block):
    groups, blocks = table.shape
    period = next(p for p in range(1, groups + 1) if (table == table[np.arange(groups) % p]).all())
    bits = int(table.max() + 1).bit_length()
    per_word = 31 // bits
    word = jnp.int32(0)
    for row in range(period):
        for first in range(0, blocks, per_word):
            values = table[row, first : first + per_word] + 1
            packed = sum(int(value) << (bits * n) for n, value in enumerate(values))
            here = (lax.rem(group, period) == row) & (block >= first) & (block < first + per_word)
            word = jnp.where(here, packed, word)
    return ((word >> (bits * lax.rem(block, per_word))) & ((1 << bits) - 1)) - 1


def dot(a, b, contract):
    return lax.dot_general(a, b, (contract, ((), ())), preferred_element_type=jnp.float32)


NN = ((1,), (0,))
NT = ((1,), (1,))


def head_columns(head, width):
    return pl.ds(pl.multiple_of(head * width, width), width)


def pack_kernel(owned, partner, sent, width, query, key, value, grad_out, frame_ids, sink_frame, window, *refs):
    blocks = len(sent)
    home, outs, refs = refs[0], refs[1:blocks], refs[blocks:]
    staged, tiles, packed, frames_here, sink_here, window_here, in_sems, out_sems = refs
    group, block = lax.axis_index("head"), lax.axis_index("tm")
    arrays = (query, key, value, grad_out)
    loads = [pltpu.make_async_copy(a, staged.at[n], in_sems.at[n]) for n, a in enumerate(arrays)]
    small = ((frame_ids, frames_here), (sink_frame, sink_here), (window, window_here))
    loads += [pltpu.make_async_copy(a, here, in_sems.at[4 + n]) for n, (a, here) in enumerate(small)]
    for load in loads:
        load.start()
    heads = [looked_up(table, group, block) for table in sent]
    stores = [pltpu.make_async_copy(packed.at[n], out, out_sems.at[1 + n]) for n, out in enumerate(outs)]
    keep = pltpu.make_async_copy(tiles, home.at[pl.ds(0, tiles.shape[0])], out_sems.at[0])
    for load in loads:
        load.wait()

    def fill(target, head):
        columns = head_columns(head, width)
        for n in range(3):
            target[n] = staged[n, :, columns]
        target[3] = staged[3, :, columns].T

    for step, head in enumerate(heads[1:]):

        @pl.when(head >= 0)
        def _():
            fill(packed.at[step], head)
            stores[step].start()

    @pl.when(heads[0] >= 0)
    def _():
        fill(tiles, heads[0])
        if tiles.shape[0] > 4:
            frames = [frames_here[looked_up(table, group, block)] for table in partner]
            row = lax.broadcasted_iota(jnp.int32, tiles.shape[1:], 0)
            theirs, own = jnp.zeros_like(row), jnp.zeros_like(row)
            for n, frame in enumerate(frames):
                theirs = jnp.where(row // blocks == n, frame, theirs)
                own = jnp.where(lax.rem(row, blocks) == n, frame, own)
            tiles[4] = seen_bias(theirs, own, window_here[heads[0]], sink_here[0]).astype(tiles.dtype)
        keep.start()

    for step, head in enumerate(heads[1:]):

        @pl.when(head >= 0)
        def _():
            stores[step].wait()

    @pl.when(heads[0] >= 0)
    def _():
        keep.wait()


def unpack_kernel(sent, width, *refs):
    parts, (attended, query_grad, key_grad, value_grad) = refs[:-4], refs[-4:]
    group, block = lax.axis_index("head"), lax.axis_index("tm")
    for step, part in enumerate(parts):
        head = looked_up(sent[step], group, block)

        @pl.when(head >= 0)
        def _():
            columns = head_columns(head, width)
            attended[:, columns] = part[0].T
            query_grad[:, columns] = part[1].T
            key_grad[:, columns] = part[2]
            value_grad[:, columns] = part[3]


def head_kernel(owned, partner, rows, frame_ids, sink_frame, window, local, *refs):
    blocks = len(partner)
    parts, outs, scratch = refs[: blocks - 1], refs[blocks - 1 : 2 * blocks - 1], refs[2 * blocks - 1 :]
    (here, q_all, kt_all, vt_all, gt_all, weights, weights_low, grads_low, grad_scaled, dk, dv, res, sem) = scratch
    parts = (here, *parts)
    group, block = lax.axis_index("head"), lax.axis_index("tm")
    head = looked_up(owned, group, block)
    width = q_all.shape[1]
    scaling = 1.0 / math.sqrt(width)
    rescale = scaling * math.log2(math.e)
    stretch = weights.shape[1]
    half = stretch // 2
    each = half // rows

    @pl.when(head >= 0)
    def _():
        fetch = pltpu.make_async_copy(local.at[pl.ds(0, 4)], here, sem)
        fetch.start()
        span = window[head]
        sink = sink_frame[0]
        frames = [frame_ids[looked_up(table, group, block)] for table in partner]

        def placed(j):
            at = pl.ds(j * rows, rows)
            q_all[at, :] = parts[j][0]
            kt_all[:, at] = parts[j][1].T
            vt_all[:, at] = parts[j][2].T
            gt_all[:, at] = parts[j][3]

        for j in range(1, blocks):
            placed(j)
        fetch.wait()
        placed(0)
        dk[...] = jnp.zeros_like(dk)
        dv[...] = jnp.zeros_like(dv)
        lane_block = lax.broadcasted_iota(jnp.int32, (1, half), 1) // rows

        def one_stretch(i, carry):
            at = [pl.ds(pl.multiple_of(i * stretch + h * half, half), half) for h in range(2)]
            lanes = [pl.ds(h * half, half) for h in range(2)]
            keys = [pl.ds(j * rows, rows) for j in range(blocks)]
            q_rows = [q_all[at[h], :] for h in range(2)]
            top = [jnp.full((1, half), hidden_score, jnp.float32)] * 2
            total = [jnp.zeros((1, half), jnp.float32)] * 2
            delta = [None] * 2
            own = [[], []]
            for h in range(2):
                for k in range(each):
                    n = i * 2 * each + h * each + k
                    own[h].append(sum(jnp.where(n == j, frames[j], 0) for j in range(blocks)))

            def score(h, j):
                bias = jnp.zeros((1, half), jnp.float32)
                for k in range(each):
                    seen = (frames[j] <= own[h][k]) & (frames[j] > own[h][k] - span)
                    seen = seen | ((frames[j] == sink) & (sink <= own[h][k]))
                    bias = jnp.where(lane_block == k, jnp.where(seen, 0.0, hidden_score), bias)
                scores = dot(parts[j][1], q_rows[h], NT) * rescale + bias
                weights[keys[j], lanes[h]] = scores
                top[h] = jnp.maximum(top[h], jnp.max(scores, axis=0, keepdims=True))

            def weigh(h, j):
                p = jnp.exp2(weights[keys[j], lanes[h]] - top[h])
                total[h] = total[h] + jnp.sum(p, axis=0, keepdims=True)
                weights[keys[j], lanes[h]] = p
                weights_low[keys[j], lanes[h]] = p.astype(jnp.bfloat16)

            def attend(h):
                inverse = 1.0 / total[h]
                mixed = (dot(vt_all[...], weights_low[:, lanes[h]], NN) * inverse).astype(jnp.bfloat16)
                grad_t = gt_all[:, at[h]].astype(jnp.float32)
                delta[h] = jnp.sum(grad_t * mixed.astype(jnp.float32), axis=0, keepdims=True) * inverse
                grad_scaled[:, lanes[h]] = (grad_t * inverse).astype(jnp.bfloat16)
                for k in range(each):
                    res[i * 2 * each + h * each + k, 0] = mixed[:, k * rows : (k + 1) * rows]

            def differ(h, j):
                g = dot(parts[j][2], grad_scaled[:, lanes[h]], NN) - delta[h]
                grads_low[keys[j], lanes[h]] = (weights[keys[j], lanes[h]] * g).astype(jnp.bfloat16)

            def query_part(h):
                grad = (dot(kt_all[...], grads_low[:, lanes[h]], NN) * scaling).astype(jnp.bfloat16)
                for k in range(each):
                    res[i * 2 * each + h * each + k, 1] = grad[:, k * rows : (k + 1) * rows]

            for j in range(blocks):
                score(0, j)
            for j in range(blocks):
                score(1, j)
                weigh(0, j)
            attend(0)
            for j in range(blocks):
                weigh(1, j)
                differ(0, j)
            attend(1)
            query_part(0)
            q_both = jnp.concatenate(q_rows, axis=0)
            for j in range(blocks):
                differ(1, j)
                dk[keys[j], :] += dot(grads_low[keys[j], :], q_both, NN)
                dv[keys[j], :] += dot(weights_low[keys[j], :], grad_scaled[...], NT)
            query_part(1)
            return carry

        lax.fori_loop(0, blocks * rows // stretch, one_stretch, 0)
        for j, out in enumerate(outs):
            at = pl.ds(j * rows, rows)
            out[0] = res[j, 0]
            out[1] = res[j, 1]
            out[2] = (dk[at, :] * scaling).astype(jnp.bfloat16)
            out[3] = dv[at, :].astype(jnp.bfloat16)


def seen_bias(frame, own, span, sink):
    seen = ((frame <= own) & (frame > own - span)) | ((frame == sink) & (sink <= own))
    return jnp.where(seen, 0.0, hidden_score)


def frames_by_lane(frames, rows):
    lane_block = lax.broadcasted_iota(jnp.int32, (1, len(frames) * rows), 1) // rows
    row = jnp.zeros_like(lane_block)
    for n, frame in enumerate(frames):
        row = jnp.where(lane_block == n, frame, row)
    return row


def place_block(part, j, rows, q_all, k_all, v_all, kt_all, vt_all, gt_all):
    at = pl.ds(j * rows, rows)
    q_all[at, :] = part[0]
    k_all[at, :] = part[1]
    v_all[at, :] = part[2]
    kt_all[:, at] = part[1].T
    vt_all[:, at] = part[2].T
    gt_all[:, at] = part[3]


def pair_products(j, held, rows, bias, scores, dots, q_all, k_all, v_all, gt_all):
    width = q_all.shape[1]
    rescale = math.log2(math.e) / math.sqrt(width)
    before = held * rows
    at = pl.ds(j * rows, rows)
    every = pl.ds(0, before + rows)
    scores[at, every] = dot(k_all[at, :], q_all[every, :], NT) * rescale + bias[pl.ds(j, 1), every]
    dots[at, every] = dot(v_all[at, :], gt_all[:, every], NN)
    column = dot(k_all[pl.ds(0, before), :], q_all[at, :], NT) * rescale
    for n in range(held):
        keys = pl.ds(n * rows, rows)
        scores[keys, at] = column[n * rows : (n + 1) * rows, :] + bias[pl.ds(n, 1), at]
    dots[pl.ds(0, before), at] = dot(v_all[pl.ds(0, before), :], gt_all[:, at], NN)


def lane_chunks(start, stop, size):
    return [pl.ds(first, min(size, stop - first)) for first in range(start, stop, size)]


def products_kernel(owned, blocks, rows, home, *refs):
    held = blocks - 3
    parts, refs = refs[: held - 1], refs[held - 1 :]
    bias, scores, dots, *places, tiles, sem = refs
    head = looked_up(owned, lax.axis_index("head"), lax.axis_index("tm"))

    @pl.when(head >= 0)
    def _():
        fetch = pltpu.make_async_copy(home.at[pl.ds(0, tiles.shape[0])], tiles, sem)
        fetch.start()
        for j, part in enumerate(parts):
            place_block(part, j + 1, rows, *places)
        fetch.wait()
        place_block(tiles, 0, rows, *places)
        mask = tiles[4].astype(jnp.float32)
        for j in range(blocks):
            for n in range(blocks):
                row = j * blocks + n
                bias[pl.ds(j, 1), pl.ds(n * rows, rows)] = mask[row : row + 1, :]
        q_all, k_all, v_all, _, _, gt_all = places
        lanes = pl.ds(0, held * rows)
        rescale = math.log2(math.e) / math.sqrt(q_all.shape[1])
        for j in range(held):
            keys = pl.ds(j * rows, rows)
            scores[keys, lanes] = dot(k_all[keys, :], q_all[lanes, :], NT) * rescale + bias[pl.ds(j, 1), lanes]
            dots[keys, lanes] = dot(v_all[keys, :], gt_all[:, lanes], NN)


def join_kernel(owned, index, rows, bias, *refs):
    part, (scores, dots, q_all, k_all, v_all, kt_all, vt_all, gt_all) = refs[0], refs[9:]
    head = looked_up(owned, lax.axis_index("head"), lax.axis_index("tm"))

    @pl.when(head >= 0)
    def _():
        place_block(part, index, rows, q_all, k_all, v_all, kt_all, vt_all, gt_all)
        pair_products(index, index, rows, bias, scores, dots, q_all, k_all, v_all, gt_all)


def softmax_kernel(owned, blocks, rows, bias, *refs):
    part, refs = refs[0], refs[9:]
    scores, dots, q_all, k_all, v_all, kt_all, vt_all, gt_all, low, stats, mixed = refs
    head = looked_up(owned, lax.axis_index("head"), lax.axis_index("tm"))

    @pl.when(head >= 0)
    def _():
        newest = blocks - 2
        held = pl.ds(0, (newest + 1) * rows)
        place_block(part, newest, rows, q_all, k_all, v_all, kt_all, vt_all, gt_all)
        pair_products(newest, newest, rows, bias, scores, dots, q_all, k_all, v_all, gt_all)
        for lanes in lane_chunks(0, (newest + 1) * rows, 2 * rows):
            top = jnp.max(scores[held, lanes], axis=0, keepdims=True)
            total = jnp.zeros_like(top)
            for j in range(newest + 1):
                keys = pl.ds(j * rows, rows)
                p = jnp.exp2(scores[keys, lanes] - top)
                total = total + jnp.sum(p, axis=0, keepdims=True)
                scores[keys, lanes] = p
                low[keys, lanes] = p.astype(jnp.bfloat16)
            stats[pl.ds(0, 1), lanes] = top
            stats[pl.ds(1, 1), lanes] = total
            mixed[:, lanes] = dot(vt_all[:, held], low[held, lanes], NN)


def finish_kernel(owned, blocks, rows, bias, stats, mixed, *refs):
    part, refs = refs[0], refs[10:]
    outs, refs = refs[:blocks], refs[blocks:]
    scores, dots, q_all, k_all, v_all, kt_all, vt_all, gt_all, low, grads_low, old_scaled, new_scaled, factors = refs
    head = looked_up(owned, lax.axis_index("head"), lax.axis_index("tm"))
    width = q_all.shape[1]
    scaling = 1.0 / math.sqrt(width)

    @pl.when(head >= 0)
    def _():
        newest = blocks - 1
        at = pl.ds(newest * rows, rows)
        place_block(part, newest, rows, q_all, k_all, v_all, kt_all, vt_all, gt_all)
        pair_products(newest, newest, rows, bias, scores, dots, q_all, k_all, v_all, gt_all)

        def settle(lanes, total, old_factor, weighted):
            inverse = 1.0 / total
            attended = (weighted * inverse).astype(jnp.bfloat16)
            grad_t = gt_all[:, lanes].astype(jnp.float32)
            delta = jnp.sum(grad_t * attended.astype(jnp.float32), axis=0, keepdims=True)
            old = inverse * old_factor
            old_scaled[:, lanes] = (grad_t * old).astype(jnp.bfloat16)
            new_scaled[:, lanes] = (grad_t * inverse).astype(jnp.bfloat16)
            factors[pl.ds(0, 1), lanes] = old
            factors[pl.ds(1, 1), lanes] = delta * old
            factors[pl.ds(2, 1), lanes] = inverse
            factors[pl.ds(3, 1), lanes] = delta * inverse
            for k in range(lanes.size // rows):
                outs[lanes.start // rows + k][0] = attended[:, k * rows : (k + 1) * rows]

        for lanes in lane_chunks(0, newest * rows, 2 * rows):
            fresh = scores[at, lanes]
            before = stats[pl.ds(0, 1), lanes]
            top = jnp.maximum(before, jnp.max(fresh, axis=0, keepdims=True))
            correction = jnp.exp2(before - top)
            p = jnp.exp2(fresh - top)
            p_low = p.astype(jnp.bfloat16)
            scores[at, lanes] = p
            low[at, lanes] = p_low
            total = stats[pl.ds(1, 1), lanes] * correction + jnp.sum(p, axis=0, keepdims=True)
            weighted = mixed[:, lanes] * correction + dot(vt_all[:, at], p_low, NN)
            settle(lanes, total, correction, weighted)
        column = scores[:, at]
        p = jnp.exp2(column - jnp.max(column, axis=0, keepdims=True))
        p_low = p.astype(jnp.bfloat16)
        scores[:, at] = p
        low[:, at] = p_low
        settle(at, jnp.sum(p, axis=0, keepdims=True), 1.0, dot(vt_all[...], p_low, NN))

        for j, out in enumerate(outs):
            keys = pl.ds(j * rows, rows)
            row = 0 if j < newest else 2
            scaled = old_scaled if j < newest else new_scaled
            for lanes in lane_chunks(0, blocks * rows, 4 * rows):
                g = dots[keys, lanes] * factors[pl.ds(row, 1), lanes] - factors[pl.ds(row + 1, 1), lanes]
                grads_low[keys, lanes] = (scores[keys, lanes] * g).astype(jnp.bfloat16)
            out[2] = (dot(grads_low[keys, :], q_all[...], NN) * scaling).astype(jnp.bfloat16)
            out[3] = dot(low[keys, :], scaled[...], NT).astype(jnp.bfloat16)
        for lanes in lane_chunks(0, blocks * rows, 2 * rows):
            grad = (dot(kt_all[...], grads_low[:, lanes], NN) * scaling).astype(jnp.bfloat16)
            for k in range(lanes.size // rows):
                outs[lanes.start // rows + k][1] = grad[:, k * rows : (k + 1) * rows]


def per_device(query, key, value, grad_out, frame_ids, sink_frame, window):
    rows, row_width = query.shape
    heads = window.shape[0]
    width = row_width // heads
    blocks = lax.axis_size("tm")
    owned, sent, partner, pairs = plan(blocks, lax.axis_size("head"), heads)
    axes = ("tm", "head")
    smem = pl.BlockSpec(memory_space=pltpu.SMEM)
    vmem = pl.BlockSpec(memory_space=pltpu.VMEM)
    in_place = pl.BlockSpec(memory_space=pltpu.HBM)
    part = jax.ShapeDtypeStruct((4, rows, width), query.dtype)
    local = jax.ShapeDtypeStruct(query.shape, query.dtype)

    tokens = blocks * rows
    split = tokens <= split_limit
    tiles = 5 if split else 4
    home_tiles = vmem_bytes // (2 * rows * width)
    home, *parts = pl.pallas_call(
        functools.partial(pack_kernel, owned, partner, sent, width),
        out_shape=[jax.ShapeDtypeStruct((home_tiles, rows, width), query.dtype)] + [part] * (blocks - 1),
        in_specs=[in_place] * 7,
        out_specs=[in_place] * blocks,
        scratch_shapes=[
            pltpu.VMEM((4, rows, row_width), query.dtype),
            pltpu.VMEM((tiles, rows, width), query.dtype),
            pltpu.VMEM((blocks - 1, 4, rows, width), query.dtype),
            pltpu.SMEM(frame_ids.shape, jnp.int32),
            pltpu.SMEM(sink_frame.shape, jnp.int32),
            pltpu.SMEM(window.shape, jnp.int32),
            pltpu.SemaphoreType.DMA((7,)),
            pltpu.SemaphoreType.DMA((blocks,)),
        ],
        compiler_params=pltpu.CompilerParams(vmem_limit_bytes=62 * MIB),
        name="pack",
    )(query, key, value, grad_out, frame_ids, sink_frame, window)
    parts = [lax.ppermute(parts[s - 1], axes, pairs[s]) for s in range(1, blocks)]

    stretch = (4 if blocks % 4 == 0 else 2) * rows
    low, full = query.dtype, jnp.float32
    if split:
        square = jax.ShapeDtypeStruct((tokens, tokens), full)
        tall = jax.ShapeDtypeStruct((tokens, width), low)
        wide = jax.ShapeDtypeStruct((width, tokens), low)
        table = jax.ShapeDtypeStruct((blocks, tokens), full)
        held = [square] * 2 + [tall] * 3 + [wide] * 3
        flops = 2 * rows * rows * width
        bias, *state = pl.pallas_call(
            functools.partial(products_kernel, owned, blocks, rows),
            out_shape=[table, *held],
            in_specs=[in_place] + [vmem] * (blocks - 4),
            out_specs=[vmem] * 9,
            scratch_shapes=[pltpu.VMEM((tiles, rows, width), low), pltpu.SemaphoreType.DMA],
            compiler_params=pltpu.CompilerParams(vmem_limit_bytes=20 * MIB),
            cost_estimate=pl.CostEstimate(
                flops=2 * flops * (blocks - 3) ** 2, bytes_accessed=8 * tokens * tokens, transcendentals=0
            ),
            name="products",
        )(home, *parts[:-3])
        state = pl.pallas_call(
            functools.partial(join_kernel, owned, blocks - 3, rows),
            out_shape=held,
            in_specs=[vmem] * 10,
            out_specs=[vmem] * 8,
            input_output_aliases={2 + n: n for n in range(8)},
            compiler_params=pltpu.CompilerParams(vmem_limit_bytes=20 * MIB),
            cost_estimate=pl.CostEstimate(
                flops=4 * flops * blocks, bytes_accessed=16 * tokens * rows, transcendentals=0
            ),
            name="join",
        )(bias, parts[-3], *state)
        *state, weights_low, stats, mixed = pl.pallas_call(
            functools.partial(softmax_kernel, owned, blocks, rows),
            out_shape=[
                *held,
                jax.ShapeDtypeStruct((tokens, tokens), low),
                table,
                jax.ShapeDtypeStruct((width, tokens), full),
            ],
            in_specs=[vmem] * 10,
            out_specs=[vmem] * 11,
            input_output_aliases={2 + n: n for n in range(8)},
            compiler_params=pltpu.CompilerParams(vmem_limit_bytes=20 * MIB),
            cost_estimate=pl.CostEstimate(
                flops=3 * flops * blocks**2, bytes_accessed=8 * tokens * tokens, transcendentals=tokens * tokens
            ),
            name="softmax",
        )(bias, parts[-2], *state)
        parts = pl.pallas_call(
            functools.partial(finish_kernel, owned, blocks, rows),
            out_shape=[part] * blocks + held + [jax.ShapeDtypeStruct((tokens, tokens), low)],
            in_specs=[vmem] * 13,
            out_specs=[vmem] * (blocks + 9),
            input_output_aliases={4 + n: blocks + n for n in range(9)},
            scratch_shapes=[
                pltpu.VMEM((tokens, tokens), low),
                pltpu.VMEM((width, tokens), low),
                pltpu.VMEM((width, tokens), low),
                pltpu.VMEM((8, tokens), full),
            ],
            compiler_params=pltpu.CompilerParams(vmem_limit_bytes=24 * MIB),
            name="finish",
        )(bias, stats, mixed, parts[-1], *state, weights_low)[:blocks]
    else:
        parts = pl.pallas_call(
            functools.partial(head_kernel, owned, partner, rows),
            out_shape=[part] * blocks,
            in_specs=[smem] * 3 + [pl.BlockSpec(memory_space=pl.ANY)] + [vmem] * (blocks - 1),
            out_specs=[vmem] * blocks,
            scratch_shapes=[
                pltpu.VMEM((4, rows, width), low),
                pltpu.VMEM((tokens, width), low),
                pltpu.VMEM((width, tokens), low),
                pltpu.VMEM((width, tokens), low),
                pltpu.VMEM((width, tokens), low),
                pltpu.VMEM((tokens, stretch), full),
                pltpu.VMEM((tokens, stretch), low),
                pltpu.VMEM((tokens, stretch), low),
                pltpu.VMEM((width, stretch), low),
                pltpu.VMEM((tokens, width), full),
                pltpu.VMEM((tokens, width), full),
                pltpu.VMEM((blocks, 2, width, rows), low),
                pltpu.SemaphoreType.DMA,
            ],
            compiler_params=pltpu.CompilerParams(vmem_limit_bytes=48 * MIB),
            name="head_attention",
        )(frame_ids, sink_frame, window, home, *parts)
    back = [[(owner, source) for source, owner in step] for step in pairs]
    order = even_rounds_back if blocks == 8 and heads == 5 else range(1, blocks)
    parts = [parts[0]] + [lax.ppermute(parts[s], axes, back[s]) for s in order]

    return pl.pallas_call(
        functools.partial(unpack_kernel, sent[np.array([0, *order])], width),
        out_shape=[local] * 4,
        in_specs=[vmem] * blocks,
        out_specs=[vmem] * 4,
        compiler_params=pltpu.CompilerParams(vmem_limit_bytes=24 * MIB),
        name="unpack",
    )(*parts)


def solution(mesh):
    spec = P("tm", "head")
    return jax.shard_map(
        per_device,
        mesh=mesh,
        in_specs=(spec, spec, spec, spec, P(), P(), P("head")),
        out_specs=(spec, spec, spec, spec),
        check_vma=False,
    )
```
